128 devices in a mesh: owner: 16 (over x_lo, z, core), col: 8 (over x_hi, y).
Axes of the slice: x: 4 (x_hi: 2, x_lo: 2; x = x_hi * 2 + x_lo), y: 4, z: 4, core: 2. Of those that a mesh axis runs over, the one named last changes fastest.
Arguments:
- token_ids: int32 [12288, 16], P('owner'), may hold values from 0 to 30719, as said below
- doc_lengths: int32 [12288], P(('owner', 'col')), may hold values from 1 to 16
- clusters: int32 [12288, 1], P(('owner', 'col')), may hold values from 0 to 63; in each aligned block of 96 rows (0 to 95, 96 to 191, ...) at most 3 rows name the same one
- embed_table: bfloat16 [30720, 1024], P('col'), may hold values from -6 to 6
- positions: bfloat16 [16, 1024], replicated, may hold values from -3 to 3
- w_in: bfloat16 [4096, 1024], P(('owner', 'col')), may hold values from -0.1875 to 0.1875
- w_out: bfloat16 [4096, 1024], P(('owner', 'col')), may hold values from -0.09375 to 0.09375
Outputs:
- best_match: float32 [12288], P(('owner', 'col'))
The draws below stay inside these ranges and needn't reach their ends.
Inputs may be any that keep to these rules, and one draw needn't show every extreme that they name: `token_ids`: the table is cut into 8 shards of 30720 / 8 consecutive rows; within the tokens of one device (aligned blocks of 96 documents) at most 384 ids lie in one shard, and exactly 384 in some shard of every block. `clusters`: within the rows of one device (aligned blocks of 96 rows) no cluster is named by more than 3 rows, a bound that some block reaches.
All inputs are finite; a program needn't handle non-finite values.
Results may differ from the reference program's by a relative error of at most 0.00035.
Values may be sent and summed in bfloat16 or wider, within the bound.
No kernel may reach another device: no remote copies, remote signals or barrier semaphores. Data moves between devices by JAX's collectives and lax.ppermute only.
A program may use at most 128 MiB of HBM per device.

```python
import math
import jax
import jax.numpy as jnp
import numpy as np
from jax import lax

D = 1024
FF = 4096
VOCAB = 30720
SEQ = 16
DOC_DEV = 96
CLUSTERS = 64
CAP = 3
DOCS = 12288
N_COL = 8


def draw_token_ids(key, part):
    key = jax.random.fold_in(key, 11)
    first_key, second_key, third_key, fourth_key = jax.random.split(key, 4)
    blocks = DOCS // DOC_DEV
    tok_block = DOC_DEV * SEQ
    share = tok_block // N_COL
    shard_rows = VOCAB // N_COL
    base = jnp.arange(tok_block, dtype=jnp.int32) // share
    base = jnp.where(base == 1, 0, base).astype(jnp.int32)
    rotate = jax.random.randint(first_key, (blocks, 1), 0, N_COL, dtype=jnp.int32)
    shard = (base[None, :] + rotate) % N_COL
    block_keys = jax.random.split(second_key, blocks)
    shard = jax.vmap(lambda one_key, row: jax.random.permutation(one_key, row))(block_keys, shard)
    first_pick = jax.random.randint(third_key, (blocks, tok_block), 0, shard_rows, dtype=jnp.int32)
    second_pick = jax.random.randint(fourth_key, (blocks, tok_block), 0, shard_rows, dtype=jnp.int32)
    within = jnp.minimum(first_pick, second_pick)
    return (shard * shard_rows + within).astype(jnp.int32).reshape(DOCS, SEQ)


def place_ends(entries, rng, smallest, top_value):
    dims = entries.shape
    place = [jax.random.randint(jax.random.fold_in(rng, axis), (), 0, dims[axis]) for axis in range(len(dims))]
    entries = entries.at[tuple(place)].set(smallest)
    longest = dims.index(max(dims))
    place[longest] = (place[longest] + 1) % dims[longest]
    return entries.at[tuple(place)].set(top_value)


def shard_levels(key, shape, shards, smallest, top_value):
    def one(dim, parts):
        heights = jax.random.uniform(jax.random.fold_in(jax.random.fold_in(key, 6), dim), (parts,), jnp.float32, smallest / len(shards), top_value / len(shards))
        return jnp.repeat(jnp.exp(heights), shape[dim] // parts).reshape((-1,) + (1,) * (len(shape) - dim - 1))

    level = one(*shards[0])
    for cut in shards[1:]:
        level = level * one(*cut)
    return level


def routed_block(own_key, own, number, rows, count, top, bound, slope):
    ranking = jax.random.permutation(own_key, count)
    packed, usual = shares(count, rows * top, bound, slope, True), shares(count, rows * top, bound, slope, False)
    places = jnp.arange(count)

    def named(tallies, offset_by):
        used = int((tallies > 0).sum())
        fixed = max(1, used // 4)
        shifted = fixed + (places - fixed + offset_by * (used - fixed)) % max(1, count - fixed)
        return jnp.zeros((count,), jnp.int32).at[ranking[jnp.where(places < fixed, places, shifted)]].set(jnp.asarray(tallies, jnp.int32))

    tallies = jnp.where(number % 4 == 0, named(packed, number // 4), named(usual, number - number // 4 - 1))
    mixed = jax.random.permutation(jax.random.fold_in(own, 3), count)
    source_of, taker = mixed[0:count // 2 * 2:2], mixed[1:count // 2 * 2:2]
    margin = jnp.minimum(tallies[source_of] - 1, bound - tallies[taker]) // 2
    margin = jnp.where((source_of == ranking[0]) | (taker == ranking[0]) | (tallies[taker] == 0), 0, jnp.maximum(margin, 0))
    shifted = jax.random.randint(jax.random.fold_in(own, 4), (count // 2,), 0, 1 << 20) % (margin + 1)
    tallies = tallies.at[source_of].add(-shifted).at[taker].add(shifted)
    items = jnp.searchsorted(jnp.cumsum(tallies), jnp.arange(rows * top), side="right").astype(jnp.int32)
    table = items.reshape(top, rows).T
    table = table[jax.random.permutation(jax.random.fold_in(own, 1), rows)]
    offset_by = jax.random.randint(jax.random.fold_in(own, 2), (rows, 1), 0, top)
    return jnp.take_along_axis(table, (jnp.arange(top)[None, :] + offset_by) % top, axis=1)


def shares(count, total, most, slope, full):
    weights = [(1 << 20) // math.isqrt(rank ** slope) + 1 for rank in range(1, count + 1)]
    largest = most if full else min(most, max(-(-total // count), total * weights[0] // sum(weights)))
    least = 1 if total - largest >= count - 1 else 0
    holding, rest = [largest] + [least] * (count - 1), total - largest - least * (count - 1)
    while rest > 0:
        free = [i for i in range(1, count) if holding[i] < largest] or [i for i in range(1, count) if holding[i] < most]
        pool, left = sum([weights[i] for i in free]), rest
        for i in free:
            extra = min(most - holding[i], max(1, left * weights[i] // pool), rest)
            holding[i] = holding[i] + extra
            rest = rest - extra
    return np.array(holding)


def noise(stream_key, extent, deviation, most, pieces=(), kind=jnp.bfloat16):
    values = jax.random.normal(stream_key, extent, jnp.float32) * deviation
    if len(pieces) > 0:
        values = shard_levels(stream_key, extent, pieces, -0.22, 0.18) * values
    return jnp.clip(values, min=-most, max=most).astype(kind)


def setup_inputs(seed: int = 0) -> dict:
    key_of = jax.random.split(jax.random.key(seed), 8)
    token_ids = draw_token_ids(jax.random.fold_in(key_of[7], 71), 0)
    doc_lengths = place_ends(jax.random.randint(key_of[1], (DOCS,), 1, SEQ + 1), jax.random.fold_in(key_of[1], 1), 1, SEQ).astype(jnp.int32)
    clusters_keys = jax.random.split(jax.random.fold_in(key_of[2], 1), DOCS // DOC_DEV)
    clusters_turns = jax.random.permutation(jax.random.fold_in(key_of[2], 3), DOCS // DOC_DEV)
    clusters = jax.vmap(lambda own, number: routed_block(jax.random.fold_in(key_of[2], 2), own, number, DOC_DEV, CLUSTERS, 1, CAP, 2))(clusters_keys, clusters_turns).reshape((DOCS, 1))
    embed_table = noise(key_of[3], (VOCAB, D), 1.0, 6.0, ((0, 8),))
    positions = noise(key_of[4], (SEQ, D), 0.5, 3.0)
    w_in = noise(key_of[5], (FF, D), D ** -0.5, 0.1875, ((0, 128),))
    w_out = noise(key_of[6], (FF, D), FF ** -0.5, 0.09375, ((0, 128),))
    return dict(token_ids=token_ids, doc_lengths=doc_lengths, clusters=clusters, embed_table=embed_table, positions=positions, w_in=w_in, w_out=w_out)


def layer_norm(values):
    mean = lax.optimization_barrier(jnp.mean(values, axis=-1, keepdims=True))
    centred = values - mean
    var = lax.optimization_barrier(jnp.mean(centred * centred, axis=-1, keepdims=True))
    return centred * lax.rsqrt(var + 1e-05)

def reference(token_ids, doc_lengths, clusters, embed_table, positions, w_in, w_out):
    blocks = DOCS // DOC_DEV
    id_blocks = token_ids.reshape(blocks, DOC_DEV, SEQ)
    len_blocks = doc_lengths.reshape(blocks, DOC_DEV)

    def encode(pair):
        ids, lengths = pair
        embedded = jnp.take(embed_table, ids, axis=0).astype(jnp.float32) + positions.astype(jnp.float32)[None]
        normed = layer_norm(embedded).reshape(DOC_DEV * SEQ, D)
        pre = jnp.dot(normed.astype(jnp.bfloat16), w_in.T, preferred_element_type=jnp.float32)
        hidden = jax.nn.gelu(pre, approximate=False).astype(jnp.bfloat16)
        states = normed + jnp.dot(hidden, w_out, preferred_element_type=jnp.float32)
        states = states.reshape(DOC_DEV, SEQ, D)
        valid = (jnp.arange(SEQ, dtype=jnp.int32)[None, :] < lengths[:, None]).astype(jnp.float32)
        pooled = lax.optimization_barrier(jnp.sum(states * valid[:, :, None], axis=1)) / lengths.astype(jnp.float32)[:, None]
        scale = lax.rsqrt(lax.optimization_barrier(jnp.sum(pooled * pooled, axis=-1, keepdims=True)) + 1e-06)
        return (pooled * scale).astype(jnp.bfloat16)
    embedding = lax.map(encode, (id_blocks, len_blocks)).reshape(DOCS, D)
    labels = clusters[:, 0]
    every = jnp.arange(DOCS, dtype=jnp.int32)

    def row_best(pair):
        rows, start = pair
        row_labels = lax.dynamic_slice_in_dim(labels, start, DOC_DEV)
        row_index = start + jnp.arange(DOC_DEV, dtype=jnp.int32)
        scores = jnp.dot(rows, embedding.T, preferred_element_type=jnp.float32)
        keep = (row_labels[:, None] == labels[None, :]) & (row_index[:, None] != every[None, :])
        return lax.optimization_barrier(jnp.max(jnp.where(keep, scores, -1.0), axis=1))
    starts = (jnp.arange(blocks, dtype=jnp.int32) * DOC_DEV).astype(jnp.int32)
    result = lax.map(row_best, (embedding.reshape(blocks, DOC_DEV, D), starts))
    return result.reshape(DOCS)
```

```python
import jax
import jax.numpy as jnp
from jax import lax
from jax.experimental import pallas as pl
from jax.experimental.pallas import tpu as pltpu
from jax.sharding import Mesh
from jax.sharding import PartitionSpec as P

OWN = ("x_lo", "z", "core")
COL = ("x_hi", "y")
X = ("x_lo", "x_hi")
CHIPS = ("x_lo", "z", "x_hi", "y")
SHARD_CAP = 384
TILE_BITS = 8
TILE = 1 << TILE_BITS
LANES = 128
SUB = 64
NONE = 1 << 30
LIMIT = 5.4 * 5.4
ERF_Q = (
    0.7978853416207131,
    0.03633264203955081,
    -3.271896418592583e-05,
    -5.512179284196367e-05,
    3.917683168513537e-06,
    -1.2794852180568973e-07,
    1.6281616374933989e-09,
)


def step(value, axis, by):
    count = 2 if axis == "core" else 4
    place = (lambda x: (x % 2) * 2 + x // 2) if axis == X else (lambda x: x)
    return lax.ppermute(value, axis, [(place(i), place((i + by) % count)) for i in range(count)])


def ring(value, axis):
    return [value] + [step(value, axis, by) for by in (1, -1, 2)]


def half_gelu(half):
    square = jnp.minimum(half * half, LIMIT / 4)
    total = jnp.full_like(square, ERF_Q[-1] * 4.0 ** (len(ERF_Q) - 1) * 2)
    for power in range(len(ERF_Q) - 2, -1, -1):
        total = total * square + ERF_Q[power] * 4.0**power * 2
    return half * jnp.tanh(half * total) + half


def members_of(docs, tile):
    lane = lax.broadcasted_iota(jnp.int32, docs.shape, 1)
    return (docs == lane + tile * LANES).astype(jnp.bfloat16)


def pool(docs, values, starts, first, tiles, total):
    high = values.astype(jnp.bfloat16)
    low = (values - high.astype(jnp.float32)).astype(jnp.bfloat16)
    for tile in range(tiles):

        @pl.when((starts[tile] < first + TILE) & (starts[tile + 1] > first))
        def _():
            mask = members_of(docs[...], tile)
            rows = pl.ds(tile * LANES, LANES)
            over = (((0,), (0,)), ((), ()))
            total[rows, :] += lax.dot_general(
                mask, high, over, preferred_element_type=jnp.float32
            ) + lax.dot_general(mask, low, over, preferred_element_type=jnp.float32)


def tiles_of(starts, parts):
    return jnp.maximum((starts[parts] + TILE - 1) >> TILE_BITS, 1)


def prepare(keys, counts, starts, table, positions, x_out, docs_out, total, rows32, table32, staged, listed, sems):
    width = table.shape[1]
    pieces = width // LANES
    chunk = staged.shape[1]
    chunks = table.shape[0] // chunk

    def load():
        def fetch(number, slot):
            return pltpu.make_async_copy(
                table.at[pl.ds(number * chunk, chunk), :], staged.at[slot], sems.at[slot]
            )

        fetch(0, 0).start()

        def gather_list(block, offset):
            base = block * SHARD_CAP

            def eight(group, carry):
                for one in range(8):
                    listed[offset + group * 8 + one] = keys[base + group * 8 + one]
                return carry

            lax.fori_loop(0, (counts[block] + 7) >> 3, eight, 0)
            return offset + counts[block]

        end = lax.fori_loop(0, 16, gather_list, 0)

        def tail(one, carry):
            listed[end + one] = NONE
            return carry

        lax.fori_loop(0, TILE, tail, 0)
        total[...] = jnp.zeros_like(total)
        for number in range(chunks):
            slot = number % 2
            if number + 1 < chunks:
                fetch(number + 1, 1 - slot).start()
            fetch(number, slot).wait()

            def widen(group, carry, number=number, slot=slot):
                values = staged[slot, pl.ds(pl.multiple_of(group * 16, 16), 16), :].astype(jnp.float32)
                base = number * chunk * pieces + group * 16 * pieces
                for eight in range(2):
                    for piece in range(pieces):
                        place = pl.multiple_of(base + eight * 8 * pieces + piece * 8, 8)
                        table32[pl.ds(place, 8), :] = values[
                            eight * 8 : eight * 8 + 8, piece * LANES : (piece + 1) * LANES
                        ]
                return carry

            lax.fori_loop(0, chunk // 16, widen, 0)

    load()
    parts = total.shape[0] // LANES

    def tile(x_ref, docs_ref):
        first = pl.program_id(0) * TILE

        def take(group, carry):
            for one in range(8):
                key = listed[first + group * 8 + one]
                place = key & 0x7FFF
                when = pl.multiple_of((key >> 12) & 0x78, 8)
                value = table32[pl.ds(place, pieces, stride=8), :] + positions[pl.ds(when, pieces), :]
                rows32[pl.ds(group * 8 * pieces + one, pieces, stride=8), :] = value
                docs_ref[pl.ds(group * 8 + one, 1), :] = jnp.full((1, LANES), key >> 19, jnp.int32)
            return carry

        lax.fori_loop(0, TILE // 8, take, 0)
        normed = []
        for sub in range(TILE // SUB):
            block = rows32[pl.ds(sub * SUB * pieces, SUB * pieces), :].reshape(SUB // 8, pieces, 8, LANES)
            values = jnp.concatenate([block[:, piece].reshape(SUB, LANES) for piece in range(pieces)], axis=1)
            mean = jnp.mean(values, axis=-1, keepdims=True)
            centred = values - mean
            var = jnp.mean(centred * centred, axis=-1, keepdims=True)
            normal = centred * lax.rsqrt(var + 1e-05)
            x_ref[pl.ds(sub * SUB, SUB), :] = (normal * 0.5).astype(jnp.bfloat16)
            normed.append(normal)
        pool(docs_ref, jnp.concatenate(normed, axis=0), starts, first, parts, total)

    pltpu.emit_pipeline(
        tile,
        grid=(tiles_of(starts, 2 * parts),),
        in_specs=[],
        out_specs=[
            pl.BlockSpec((TILE, width), lambda i: (i, 0)),
            pl.BlockSpec((TILE, LANES), lambda i: (i, 0)),
        ],
    )(x_out, docs_out)


def forward(starts, x_all, docs_all, *refs):
    weights, total = refs[:-1], refs[-1]
    width = x_all.shape[1]
    parts = total.shape[0] // LANES
    total[...] = jnp.zeros_like(total)

    def tile(x_ref, docs_ref):
        x = x_ref[...]
        branch = jnp.zeros(x.shape, jnp.float32)
        for ref in weights:
            rows = ref.shape[0]
            both = ref[...].reshape(rows // 32, 32, width)
            w_in = both[:, :16].reshape(rows // 2, width)
            w_out = both[:, 16:].reshape(rows // 2, width)
            pre = lax.dot_general(x, w_in, (((1,), (1,)), ((), ())), preferred_element_type=jnp.float32)
            hidden = half_gelu(pre).astype(jnp.bfloat16)
            branch = branch + jnp.dot(hidden, w_out, preferred_element_type=jnp.float32)
        pool(docs_ref, branch, starts, pl.program_id(0) * TILE, parts, total)

    pltpu.emit_pipeline(
        tile,
        grid=(tiles_of(starts, parts),),
        in_specs=[
            pl.BlockSpec((TILE, width), lambda i: (i, 0)),
            pl.BlockSpec((TILE, LANES), lambda i: (i, 0)),
        ],
        out_specs=[],
    )(x_all, docs_all)


def local(token_ids, doc_lengths, clusters, embed_table, positions, w_in, w_out):
    doc_dev = doc_lengths.shape[0]
    group, seq = token_ids.shape
    vocab_rows, width = embed_table.shape
    n_col = group // doc_dev
    most = 2 * n_col * SHARD_CAP
    smem, vmem, hbm = (pl.BlockSpec(memory_space=space) for space in (pltpu.SMEM, pltpu.VMEM, pl.ANY))

    units = w_in.shape[0]
    with jax.named_scope("weights"):
        mixed = jnp.concatenate([w_in[:16], w_out[:16], w_in[16:], w_out[16:]], axis=0)
        by_z = lax.all_gather(mixed, "z", axis=0, tiled=False)
        first_half, second_half = by_z[:, :units].reshape(-1, width), by_z[:, units:].reshape(-1, width)
        first_half = jnp.concatenate(ring(first_half, X), axis=0)
        second_half = jnp.concatenate(ring(second_half, "y"), axis=0)
        weights = ring(first_half, "y") + ring(second_half, X)

    with jax.named_scope("keys"):
        lengths = lax.all_gather(doc_lengths, COL, axis=0, tiled=True)
        row = token_ids - lax.axis_index(COL) * vocab_rows
        time = lax.broadcasted_iota(jnp.int32, (group, seq), 1)
        doc = lax.broadcasted_iota(jnp.int32, (group, seq), 0)
        keep = (row >= 0) & (row < vocab_rows) & (time < lengths[:, None])
        place = (row >> 3) * 64 + (row & 7)
        key = jnp.where(keep, (doc << 19) + (time << 15) + place, NONE)
        key = lax.sort(key.reshape(n_col, doc_dev * seq), dimension=1)[:, :SHARD_CAP]
        kept = jnp.sum(keep.astype(jnp.int32), axis=1)
        counts = jnp.sum(kept.reshape(n_col, doc_dev), axis=1)
        parts = jnp.sum(kept.reshape(group // LANES, LANES), axis=1)
        tally = jnp.concatenate([counts, parts, jnp.zeros((SHARD_CAP - n_col - group // LANES,), jnp.int32)])
        mine = jnp.concatenate([key, tally[None]], axis=0)
        other = step(mine, "core", 1)
        other_key = other[:n_col] + jnp.where(other[:n_col] < NONE, group << 19, 0)
        keys = jnp.concatenate([key, other_key], axis=0).reshape(-1)
        counts = jnp.concatenate([counts, other[n_col, :n_col]])
        parts = jnp.concatenate([parts, other[n_col, n_col : n_col + group // LANES]])
        starts = jnp.concatenate([jnp.zeros((1,), jnp.int32), jnp.cumsum(parts)])

    with jax.named_scope("prepare"):
        pieces = width // LANES
        x, docs, normed = pl.pallas_call(
            prepare,
            in_specs=[smem, smem, smem, hbm, vmem],
            out_specs=[hbm, hbm, vmem],
            out_shape=[
                jax.ShapeDtypeStruct((most, width), jnp.bfloat16),
                jax.ShapeDtypeStruct((most, LANES), jnp.int32),
                jax.ShapeDtypeStruct((group, width), jnp.float32),
            ],
            scratch_shapes=[
                pltpu.VMEM((TILE * pieces, LANES), jnp.float32),
                pltpu.VMEM((vocab_rows * pieces, LANES), jnp.float32),
                pltpu.VMEM((2, vocab_rows // 8, width), jnp.bfloat16),
                pltpu.SMEM((most + TILE + 8,), jnp.int32),
                pltpu.SemaphoreType.DMA((2,)),
            ],
            compiler_params=pltpu.CompilerParams(vmem_limit_bytes=44 << 20),
            cost_estimate=pl.CostEstimate(flops=4 << 30, bytes_accessed=32 << 20, transcendentals=0),
        )(keys, counts, starts, embed_table, positions.astype(jnp.float32).reshape(seq * pieces, LANES))

    with jax.named_scope("forward"):
        branch = pl.pallas_call(
            forward,
            in_specs=[smem, hbm, hbm] + [vmem] * len(weights),
            out_specs=vmem,
            out_shape=jax.ShapeDtypeStruct((2 * group, width), jnp.float32),
            compiler_params=pltpu.CompilerParams(vmem_limit_bytes=48 << 20),
            cost_estimate=pl.CostEstimate(flops=16 << 30, bytes_accessed=24 << 20, transcendentals=0),
        )(starts, x, docs, *weights)

    with jax.named_scope("pooled"):
        sums = branch[:group] + normed + step(branch[group:], "core", 1)
        sums = sums.astype(jnp.bfloat16).reshape(n_col, doc_dev, width)
        sums = lax.all_to_all(sums, COL, 0, 0, tiled=True)
        pooled = jnp.sum(sums.astype(jnp.float32), axis=0) / doc_lengths.astype(jnp.float32)[:, None]
        scale = lax.rsqrt(jnp.sum(pooled * pooled, axis=-1, keepdims=True) + 1e-06)
        embedding = (pooled * scale).astype(jnp.bfloat16)

    with jax.named_scope("match"):
        n_clusters = lax.axis_size(CHIPS)
        labels = clusters[:, 0]
        same = labels[:, None] == labels[None, :]
        order = jnp.arange(doc_dev, dtype=jnp.int32)
        rank = jnp.sum((same & (order[:, None] > order[None, :])).astype(jnp.int32), axis=1)
        slot = labels * 4 + rank
        chosen = slot[None, :] == jnp.arange(n_clusters * 4, dtype=jnp.int32)[:, None]
        sizes = jnp.sum((labels[None, :] == jnp.arange(n_clusters)[:, None]).astype(jnp.int32), axis=1)
        fourth = lax.broadcasted_iota(jnp.int32, (n_clusters, 4, width), 1) == 3
        flags = lax.broadcasted_iota(jnp.int32, (n_clusters, 4, width), 2) < sizes[:, None, None]
        outgoing = jnp.dot(chosen.astype(jnp.bfloat16), embedding, preferred_element_type=jnp.float32)
        outgoing = jnp.where(
            fourth, flags.astype(jnp.float32), outgoing.reshape(n_clusters, 4, width)
        ).astype(jnp.bfloat16)
        members = lax.all_to_all(outgoing, CHIPS, 0, 0, tiled=True)
        others = step(members, "core", 1)
        every = jnp.concatenate([members, others], axis=0)
        filled = jnp.pad(every[:, 3, :3], ((0, 0), (0, 1))).reshape(-1) > 0.5
        count = n_clusters * 4
        scores = jnp.dot(
            members.reshape(count, width), every.reshape(2 * count, width).T, preferred_element_type=jnp.float32
        )
        own = jnp.arange(count)[:, None] == jnp.arange(2 * count)[None, :]
        best = jnp.max(jnp.where(filled[None, :] & jnp.logical_not(own), scores, -1.0), axis=1)
        best = jnp.maximum(best, -1.0)
        returned = lax.all_to_all(best.reshape(n_clusters, 4), CHIPS, 0, 0, tiled=True).reshape(-1)
        return jnp.sum(jnp.where(chosen, returned[:, None], 0.0), axis=0)


def solution(mesh):
    fine = Mesh(mesh.devices.reshape(2, 4, 2, 2, 4), ("x_lo", "z", "core", "x_hi", "y"))
    everywhere = OWN + COL
    return jax.shard_map(
        local,
        mesh=fine,
        in_specs=(
            P(OWN, None),
            P(everywhere),
            P(everywhere, None),
            P(COL, None),
            P(),
            P(everywhere, None),
            P(everywhere, None),
        ),
        out_specs=P(everywhere),
        check_vma=False,
    )
```

```python
import functools

import jax
import jax.numpy as jnp
from jax import lax
from jax.experimental import pallas as pl
from jax.experimental.pallas import tpu as pltpu
from jax.sharding import Mesh
from jax.sharding import PartitionSpec as P

OWN = ("x_lo", "z", "core")
COL = ("x_hi", "y")
X = ("x_lo", "x_hi")
CHIPS = ("x_lo", "z", "x_hi", "y")
SHARD_CAP = 384
TILE_BITS = 8
TILE = 1 << TILE_BITS
LANES = 128
SUB = 64
SEQ_BITS = 4
NONE = 1 << 30
BOUNDS = 64
CHUNK = 512
WINDOW = 384
LIMIT = 5.4 * 5.4
ERF_Q = (
    0.7978853416207131,
    0.03633264203955081,
    -3.271896418592583e-05,
    -5.512179284196367e-05,
    3.917683168513537e-06,
    -1.2794852180568973e-07,
    1.6281616374933989e-09,
)


def step(value, axis, by):
    count = 2 if axis == "core" else 4
    place = (lambda x: (x % 2) * 2 + x // 2) if axis == X else (lambda x: x)
    return lax.ppermute(value, axis, [(place(i), place((i + by) % count)) for i in range(count)])


def ring(value, axis):
    return [value] + [step(value, axis, by) for by in (1, -1, 2)]


def copied(sources, shapes, moves):
    def kernel(*refs):
        inputs, (*outputs, sems) = refs[: len(sources)], refs[len(sources) :]
        copies = [
            pltpu.make_async_copy(
                inputs[source].at[pl.ds(from_row, rows), :], outputs[result].at[pl.ds(to_row, rows), :], sems.at[number]
            )
            for number, (source, from_row, result, to_row, rows) in enumerate(moves)
        ]
        for copy in copies:
            copy.start()
        for copy in copies:
            copy.wait()

    return pl.pallas_call(
        kernel,
        in_specs=[pl.BlockSpec(memory_space=pl.ANY)] * len(sources),
        out_specs=[pl.BlockSpec(memory_space=pltpu.VMEM)] * len(shapes),
        out_shape=[jax.ShapeDtypeStruct(shape, sources[0].dtype) for shape in shapes],
        scratch_shapes=[pltpu.SemaphoreType.DMA((len(moves),))],
        cost_estimate=pl.CostEstimate(flops=1 << 10, bytes_accessed=1 << 10, transcendentals=0),
    )(*sources)


def joined(rings, starts, rows):
    sources, shapes, moves = [], [], []
    for result, (pieces, start) in enumerate(zip(rings, starts)):
        half = rows // 2
        shapes.append((len(pieces) * rows, pieces[0].shape[1]))
        for number, piece in enumerate(pieces):
            for which in range(2):
                to_row = (which * len(pieces) + number) * half
                moves.append((len(sources) + number, start + which * half, result, to_row, half))
        sources += pieces
    return copied(sources, shapes, moves)


def half_gelu(half):
    square = jnp.minimum(half * half, LIMIT / 4)
    total = jnp.full_like(square, ERF_Q[-1] * 4.0 ** (len(ERF_Q) - 1) * 2)
    for power in range(len(ERF_Q) - 2, -1, -1):
        total = total * square + ERF_Q[power] * 4.0**power * 2
    return half * jnp.tanh(half * total) + half


def pool(docs, both, first, last, total):
    def window(start):
        start = pl.multiple_of(start, 8)
        lane = lax.broadcasted_iota(jnp.int32, docs.shape, 1)
        mask = jnp.concatenate(
            [(docs == lane + (start + part)).astype(jnp.bfloat16) for part in range(0, WINDOW, LANES)], axis=1
        )
        rows = pl.ds(start, WINDOW)
        total[rows, :] += lax.dot_general(
            jnp.concatenate([mask, mask], axis=0),
            both,
            (((0,), (0,)), ((), ())),
            preferred_element_type=jnp.float32,
        )

    window(first)

    @pl.when(last >= first + WINDOW)
    def _():
        lax.fori_loop(
            1, lax.div(last - first, WINDOW) + 1, lambda number, carry: (window(first + number * WINDOW), carry)[1], 0
        )


def split(values):
    high = values.astype(jnp.bfloat16)
    return jnp.concatenate([high, (values - high.astype(jnp.float32)).astype(jnp.bfloat16)], axis=0)


def prepare(keys, counts, table, positions, x_out, docs_out, bounds, total, rows32, table32, listed):
    width = table.shape[1]
    pieces = width // LANES

    def load():
        def gather_list(block, offset):
            base = block * SHARD_CAP

            def eight(group, carry):
                for one in range(8):
                    listed[offset + group * 8 + one] = keys[base + group * 8 + one]
                return carry

            lax.fori_loop(0, (counts[block] + 7) >> 3, eight, 0)
            return offset + counts[block]

        end = lax.fori_loop(0, 16, gather_list, 0)

        def tail(group, carry):
            for one in range(8):
                listed[end + group * 8 + one] = NONE
            return carry

        lax.fori_loop(0, TILE // 8, tail, 0)
        total[...] = jnp.zeros_like(total)

        def widen(group, carry):
            values = table[pl.ds(pl.multiple_of(group * 16, 16), 16), :].astype(jnp.float32)
            for eight in range(2):
                for piece in range(pieces):
                    place = pl.multiple_of((group * 2 + eight) * 8 * pieces + piece * 8, 8)
                    table32[pl.ds(place, 8), :] = values[
                        eight * 8 : eight * 8 + 8, piece * LANES : (piece + 1) * LANES
                    ]
            return carry

        lax.fori_loop(0, table.shape[0] // 16, widen, 0)
        return end

    end = load()
    tiles = jnp.maximum((end + TILE - 1) >> TILE_BITS, 1)
    own = total.shape[0] - WINDOW
    bounds[BOUNDS - 1] = tiles

    def tile(x_ref, docs_ref):
        first = pl.program_id(0) * TILE

        def take(group, carry):
            for one in range(8):
                key = listed[first + group * 8 + one]
                place = key & 0x7FFF
                when = pl.multiple_of((key >> 12) & 0x78, 8)
                value = table32[pl.ds(place, pieces, stride=8), :] + positions[pl.ds(when, pieces), :]
                rows32[pl.ds(group * 8 * pieces + one, pieces, stride=8), :] = value
                docs_ref[pl.ds(group * 8 + one, 1), :] = jnp.full((1, LANES), key >> 19, jnp.int32)
            return carry

        lax.fori_loop(0, TILE // 8, take, 0)
        normed = []
        for sub in range(TILE // SUB):
            block = rows32[pl.ds(sub * SUB * pieces, SUB * pieces), :].reshape(SUB // 8, pieces, 8, LANES)
            values = jnp.concatenate([block[:, piece].reshape(SUB, LANES) for piece in range(pieces)], axis=1)
            mean = jnp.mean(values, axis=-1, keepdims=True)
            centred = values - mean
            var = jnp.mean(centred * centred, axis=-1, keepdims=True)
            normal = centred * lax.rsqrt(var + 1e-05)
            x_ref[pl.ds(sub * SUB, SUB), :] = (normal * 0.5).astype(jnp.bfloat16)
            normed.append(normal)
        low = jnp.minimum((listed[first] >> 22) << 3, 2 * own - 8)
        high = jnp.minimum(listed[jnp.clip(end - 1, first, first + TILE - 1)] >> 19, 2 * own - 1)
        index = pl.program_id(0)
        bounds[2 * index] = low
        bounds[2 * index + 1] = high

        @pl.when(low < own)
        def _():
            pool(docs_ref[...], split(jnp.concatenate(normed, axis=0)), low, jnp.minimum(high, own - 1), total)

    pltpu.emit_pipeline(
        tile,
        grid=(tiles,),
        in_specs=[],
        out_specs=[
            pl.BlockSpec((TILE, width), lambda i: (i, 0)),
            pl.BlockSpec((TILE, LANES), lambda i: (i, 0)),
        ],
    )(x_out, docs_out)


def run_prepare(keys, counts, embed_table, positions, group):
    most = keys.shape[0]
    seq, width = positions.shape
    vocab_rows = embed_table.shape[0]
    pieces = width // LANES
    smem, vmem, hbm = (pl.BlockSpec(memory_space=space) for space in (pltpu.SMEM, pltpu.VMEM, pltpu.HBM))
    return pl.pallas_call(
        prepare,
        in_specs=[smem, smem, vmem, vmem],
        out_specs=[hbm, hbm, smem, vmem],
        out_shape=[
            jax.ShapeDtypeStruct((most, width), jnp.bfloat16),
            jax.ShapeDtypeStruct((most, LANES), jnp.int32),
            jax.ShapeDtypeStruct((BOUNDS,), jnp.int32),
            jax.ShapeDtypeStruct((group + WINDOW, width), jnp.float32),
        ],
        scratch_shapes=[
            pltpu.VMEM((TILE * pieces, LANES), jnp.float32),
            pltpu.VMEM((vocab_rows * pieces, LANES), jnp.float32),
            pltpu.SMEM((most + TILE + 8,), jnp.int32),
        ],
        compiler_params=pltpu.CompilerParams(vmem_limit_bytes=44 << 20),
        cost_estimate=pl.CostEstimate(flops=1 << 30, bytes_accessed=1 << 20, transcendentals=0),
    )(keys, counts, embed_table, positions.astype(jnp.float32).reshape(seq * pieces, LANES))


def over_tiles(tiles, several):
    def pair(number, carry):
        several(number * 2, 2)
        return carry

    lax.fori_loop(0, tiles >> 1, pair, 0)

    @pl.when((tiles & 1) == 1)
    def _():
        several(tiles - 1, 1)


def rows_of(tile, count):
    return pl.ds(pl.multiple_of(tile * TILE, TILE), count * TILE)


def load_pairs(tiles, loads):
    def copies(tile, slot):
        return [
            pltpu.make_async_copy(whole.at[rows_of(tile, 2), :], place.at[slot], sems.at[slot])
            for whole, place, sems in loads
        ]

    for copy in copies(0, 0):
        copy.start()

    def ready(tile):
        slot = (tile >> 1) & 1

        @pl.when(tile + 2 < tiles)
        def _():
            for copy in copies(tile + 2, 1 - slot):
                copy.start()

        for copy in copies(tile, slot):
            copy.wait()
        return slot

    return ready


def activate(inputs, w_in, hidden, first):
    rows = pl.ds(0, inputs.shape[0])
    for number in range(w_in.shape[0] // CHUNK):
        weights = w_in[pl.ds(number * CHUNK, CHUNK), :]
        pre = lax.dot_general(inputs, weights, (((1,), (1,)), ((), ())), preferred_element_type=jnp.float32)
        hidden[rows, pl.ds(first + number * CHUNK, CHUNK)] = half_gelu(pre).astype(jnp.bfloat16)


def first_units(near, bounds, x_all, *refs):
    pieces, (out, x, w_in, hidden, w_sems, x_sems, out_sems) = refs[:near], refs[near:]
    tiles = bounds[BOUNDS - 1]
    units = w_in.shape[0] // near
    copies = [
        pltpu.make_async_copy(piece.at[pl.ds(0, units), :], w_in.at[pl.ds(number * units, units), :], w_sems.at[number])
        for number, piece in enumerate(pieces)
    ]
    for copy in copies:
        copy.start()
    ready = load_pairs(tiles, [(x_all, x, x_sems)])
    for copy in copies:
        copy.wait()

    def store(tile, slot):
        return pltpu.make_async_copy(hidden.at[slot], out.at[rows_of(tile, 2), :], out_sems.at[slot])

    def several(tile, count):
        slot = ready(tile)

        @pl.when(tile >= 4)
        def _():
            store(tile - 4, slot).wait()

        activate(x[slot, pl.ds(0, count * TILE), :], w_in, hidden.at[slot], 0)
        store(tile, slot).start()

    over_tiles(tiles, several)
    last = ((tiles + 1) >> 1) * 2 - 2

    @pl.when(last >= 2)
    def _():
        store(last - 2, 1 - ((last >> 1) & 1)).wait()

    store(last, (last >> 1) & 1).wait()


def second_units(near, far, bounds, x_all, docs_all, normed, hidden_all, *refs):
    pieces, refs = refs[: near + far], refs[near + far :]
    own, other, total, x, docs, w_in, w_out, hidden, w_sems, x_sems, docs_sems, hidden_sems, ends = refs
    tiles = bounds[BOUNDS - 1]
    group = own.shape[0]
    units = pieces[0].shape[0] // 2
    parts = [(piece.at[pl.ds(units, units), :], w_out, number * units) for number, piece in enumerate(pieces)]
    parts += [(piece.at[pl.ds(0, units), :], w_in, number * units) for number, piece in enumerate(pieces[near:])]
    copies = [
        pltpu.make_async_copy(part, whole.at[pl.ds(row, units), :], w_sems.at[number])
        for number, (part, whole, row) in enumerate(parts)
    ]
    copies.append(pltpu.make_async_copy(normed.at[pl.ds(0, group), :], total.at[pl.ds(0, group), :], ends.at[0]))
    for copy in copies:
        copy.start()
    known = hidden.at[:, :, pl.ds(0, near * units)]
    ready = load_pairs(tiles, [(x_all, x, x_sems), (docs_all, docs, docs_sems), (hidden_all, known, hidden_sems)])
    rest = total.shape[0] - group
    total[pl.ds(group, rest), :] = jnp.zeros((rest, total.shape[1]), jnp.float32)
    for copy in copies:
        copy.wait()

    def several(tile, count):
        slot = ready(tile)
        rows = pl.ds(0, count * TILE)
        activate(x[slot, rows, :], w_in, hidden.at[slot], near * units)
        branch = jnp.dot(hidden[slot, rows, :], w_out[...], preferred_element_type=jnp.float32)
        for one in range(count):
            part = slice(one * TILE, (one + 1) * TILE)
            pool(docs[slot, part, :], split(branch[part]), bounds[2 * (tile + one)], bounds[2 * (tile + one) + 1], total)

    over_tiles(tiles, several)
    copies = [
        pltpu.make_async_copy(total.at[pl.ds(0, group), :], own, ends.at[0]),
        pltpu.make_async_copy(total.at[pl.ds(group, group), :], other, ends.at[1]),
    ]
    for copy in copies:
        copy.start()
    for copy in copies:
        copy.wait()


def run_first(near, bounds, x):
    most, width = x.shape
    units = len(near) * near[0].shape[0] // 2
    smem, hbm, anywhere = (pl.BlockSpec(memory_space=space) for space in (pltpu.SMEM, pltpu.HBM, pl.ANY))
    return pl.pallas_call(
        functools.partial(first_units, len(near)),
        in_specs=[smem, hbm] + [anywhere] * len(near),
        out_specs=hbm,
        out_shape=jax.ShapeDtypeStruct((most, units), jnp.bfloat16),
        scratch_shapes=[
            pltpu.VMEM((2, 2 * TILE, width), jnp.bfloat16),
            pltpu.VMEM((units, width), jnp.bfloat16),
            pltpu.VMEM((2, 2 * TILE, units), jnp.bfloat16),
            pltpu.SemaphoreType.DMA((len(near),)),
            pltpu.SemaphoreType.DMA((2,)),
            pltpu.SemaphoreType.DMA((2,)),
        ],
        compiler_params=pltpu.CompilerParams(vmem_limit_bytes=50 << 20),
        cost_estimate=pl.CostEstimate(flops=12 << 30, bytes_accessed=16 << 20, transcendentals=0),
    )(bounds, x, *near)


def run_second(near, far, bounds, x, docs, normed, hidden):
    most, width = x.shape
    group = normed.shape[0] - WINDOW
    units = near[0].shape[0] // 2
    count = len(near) + len(far)
    smem, hbm, anywhere = (pl.BlockSpec(memory_space=space) for space in (pltpu.SMEM, pltpu.HBM, pl.ANY))
    return pl.pallas_call(
        functools.partial(second_units, len(near), len(far)),
        in_specs=[smem, hbm, anywhere, anywhere, hbm] + [anywhere] * count,
        out_specs=[anywhere, anywhere],
        out_shape=[jax.ShapeDtypeStruct((group, width), jnp.float32)] * 2,
        scratch_shapes=[
            pltpu.VMEM((2 * group + WINDOW, width), jnp.float32),
            pltpu.VMEM((2, 2 * TILE, width), jnp.bfloat16),
            pltpu.VMEM((2, 2 * TILE, LANES), jnp.int32),
            pltpu.VMEM((len(far) * units, width), jnp.bfloat16),
            pltpu.VMEM((count * units, width), jnp.bfloat16),
            pltpu.VMEM((2, 2 * TILE, count * units), jnp.bfloat16),
            pltpu.SemaphoreType.DMA((count + len(far),)),
            pltpu.SemaphoreType.DMA((2,)),
            pltpu.SemaphoreType.DMA((2,)),
            pltpu.SemaphoreType.DMA((2,)),
            pltpu.SemaphoreType.DMA((2,)),
        ],
        compiler_params=pltpu.CompilerParams(vmem_limit_bytes=34 << 20),
        cost_estimate=pl.CostEstimate(flops=16 << 30, bytes_accessed=24 << 20, transcendentals=0),
    )(bounds, x, docs, normed, hidden, *near, *far)


def local(token_ids, doc_lengths, clusters, embed_table, positions, w_in, w_out):
    doc_dev = doc_lengths.shape[0]
    group, seq = token_ids.shape
    vocab_rows, width = embed_table.shape
    n_col = group // doc_dev

    with jax.named_scope("weights"):
        half = w_in.shape[0] // 2
        mixed = jnp.concatenate([w_in[:half], w_out[:half], w_in[half:], w_out[half:]], axis=0)
        by_z = ring(mixed, "z")
        ids = token_ids.reshape(n_col, doc_dev * seq)
        ids = jnp.concatenate([ids, step(ids, "core", 1)], axis=0)
        row = ids - lax.axis_index(COL) * vocab_rows
        block = lax.broadcasted_iota(jnp.int32, ids.shape, 0)
        token = lax.broadcasted_iota(jnp.int32, ids.shape, 1)
        keys = ((block * doc_dev + (token >> SEQ_BITS)) << 19) + ((token & (seq - 1)) << 15)
        keys = jnp.where((row >= 0) & (row < vocab_rows), keys + (row >> 3) * 64 + (row & 7), NONE)
        first, second = joined([by_z, by_z], [0, 2 * half], 2 * half)
        first, second, doc_lengths, keys = lax.optimization_barrier((first, second, doc_lengths, keys))
        lengths = lax.all_gather(doc_lengths, ("core",) + COL, axis=0, tiled=False)
        first, second = ring(first, X), ring(second, "y")
        first, second, lengths = lax.optimization_barrier((first, second, lengths))
        rows = first[0].shape[0]
        first, second = joined([first, second], [0, 0], rows)
        units = first.shape[0] // 2
        left, right = step(first, "y", 1), step(first, "y", -1)
        down, up = step(second, X, 1), step(second, X, -1)
        near = [first, left, right, second, down, up]

    with jax.named_scope("keys"):
        blocks, block = 2 * n_col, doc_dev * seq
        lengths = lengths.reshape(2, n_col, doc_dev)
        lengths = jnp.where(lax.axis_index("core") == 0, lengths, lengths[::-1]).reshape(blocks, doc_dev)
        token = jnp.arange(block, dtype=jnp.int32)[None, :]
        of_doc = (jnp.arange(doc_dev, dtype=jnp.int32)[:, None] == token >> SEQ_BITS).astype(jnp.bfloat16)
        used = jnp.dot(lengths.astype(jnp.bfloat16), of_doc, preferred_element_type=jnp.float32)
        keys = jnp.where((token & (seq - 1)).astype(jnp.float32) < used, keys, NONE)
        counts = jnp.sum((keys < NONE).astype(jnp.int32), axis=1)
        keys = lax.sort(keys, dimension=1)[:, :SHARD_CAP].reshape(-1)

    with jax.named_scope("prepare"):
        x, docs, bounds, normed = run_prepare(keys, counts, embed_table, positions, group)

    with jax.named_scope("forward"):
        far = [step(first, "y", 2), step(second, X, 2)]
        hidden = run_first(near, bounds, x)
        own, other = run_second(near, far, bounds, x, docs, normed, hidden)

    with jax.named_scope("pooled"):
        sums = own + step(other, "core", 1)
        sums = sums.astype(jnp.bfloat16).reshape(n_col, doc_dev, width)
        sums = lax.all_to_all(sums, COL, 0, 0, tiled=True)
        pooled = jnp.sum(sums.astype(jnp.float32), axis=0) / doc_lengths.astype(jnp.float32)[:, None]
        scale = lax.rsqrt(jnp.sum(pooled * pooled, axis=-1, keepdims=True) + 1e-06)
        embedding = (pooled * scale).astype(jnp.bfloat16)

    with jax.named_scope("match"):
        n_clusters = lax.axis_size(CHIPS)
        labels = clusters[:, 0]
        same = labels[:, None] == labels[None, :]
        order = jnp.arange(doc_dev, dtype=jnp.int32)
        rank = jnp.sum((same & (order[:, None] > order[None, :])).astype(jnp.int32), axis=1)
        slot = labels * 4 + rank
        chosen = slot[None, :] == jnp.arange(n_clusters * 4, dtype=jnp.int32)[:, None]
        sizes = jnp.sum((labels[None, :] == jnp.arange(n_clusters)[:, None]).astype(jnp.int32), axis=1)
        fourth = lax.broadcasted_iota(jnp.int32, (n_clusters, 4, width), 1) == 3
        flags = lax.broadcasted_iota(jnp.int32, (n_clusters, 4, width), 2) < sizes[:, None, None]
        outgoing = jnp.dot(chosen.astype(jnp.bfloat16), embedding, preferred_element_type=jnp.float32)
        outgoing = jnp.where(
            fourth, flags.astype(jnp.float32), outgoing.reshape(n_clusters, 4, width)
        ).astype(jnp.bfloat16)
        members = lax.all_to_all(outgoing, CHIPS, 0, 0, tiled=True)
        others = step(members, "core", 1)
        every = jnp.concatenate([members, others], axis=0)
        filled = jnp.pad(every[:, 3, :3], ((0, 0), (0, 1))).reshape(-1) > 0.5
        count = n_clusters * 4
        scores = jnp.dot(
            members.reshape(count, width), every.reshape(2 * count, width).T, preferred_element_type=jnp.float32
        )
        own = jnp.arange(count)[:, None] == jnp.arange(2 * count)[None, :]
        best = jnp.max(jnp.where(filled[None, :] & jnp.logical_not(own), scores, -1.0), axis=1)
        best = jnp.maximum(best, -1.0)
        returned = lax.all_to_all(best.reshape(n_clusters, 4), CHIPS, 0, 0, tiled=True).reshape(-1)
        return jnp.sum(jnp.where(chosen, returned[:, None], 0.0), axis=0)


def solution(mesh):
    fine = Mesh(mesh.devices.reshape(2, 4, 2, 2, 4), ("x_lo", "z", "core", "x_hi", "y"))
    everywhere = OWN + COL
    return jax.shard_map(
        local,
        mesh=fine,
        in_specs=(
            P(OWN, None),
            P(everywhere),
            P(everywhere, None),
            P(COL, None),
            P(),
            P(everywhere, None),
            P(everywhere, None),
        ),
        out_specs=P(everywhere),
        check_vma=False,
    )
```

```python
import functools

import jax
import jax.numpy as jnp
from jax import lax
from jax.experimental import pallas as pl
from jax.experimental.pallas import tpu as pltpu
from jax.sharding import Mesh
from jax.sharding import PartitionSpec as P

OWN = ("x_lo", "z", "core")
COL = ("x_hi", "y")
X = ("x_lo", "x_hi")
CHIPS = ("x_lo", "z", "x_hi", "y")
SHARD_CAP = 384
TILE_BITS = 8
TILE = 1 << TILE_BITS
LANES = 128
SUB = 64
SEQ_BITS = 4
NONE = 1 << 30
BOUNDS = 64
CHUNK = 256
WINDOW = 384
LIMIT = 5.4 * 5.4
ERF_Q = (
    0.7978853416207131,
    0.03633264203955081,
    -3.271896418592583e-05,
    -5.512179284196367e-05,
    3.917683168513537e-06,
    -1.2794852180568973e-07,
    1.6281616374933989e-09,
)


def step(value, axis, by):
    count = 2 if axis == "core" else 4
    place = (lambda x: (x % 2) * 2 + x // 2) if axis == X else (lambda x: x)
    return lax.ppermute(value, axis, [(place(i), place((i + by) % count)) for i in range(count)])


def ring(value, axis):
    return [value] + [step(value, axis, by) for by in (1, -1, 2)]


def copied(sources, shapes, moves):
    def kernel(*refs):
        inputs, (*outputs, sems) = refs[: len(sources)], refs[len(sources) :]
        copies = [
            pltpu.make_async_copy(
                inputs[source].at[pl.ds(from_row, rows), :], outputs[result].at[pl.ds(to_row, rows), :], sems.at[number]
            )
            for number, (source, from_row, result, to_row, rows) in enumerate(moves)
        ]
        for copy in copies:
            copy.start()
        for copy in copies:
            copy.wait()

    return pl.pallas_call(
        kernel,
        in_specs=[pl.BlockSpec(memory_space=pl.ANY)] * len(sources),
        out_specs=[pl.BlockSpec(memory_space=pltpu.VMEM)] * len(shapes),
        out_shape=[jax.ShapeDtypeStruct(shape, sources[0].dtype) for shape in shapes],
        scratch_shapes=[pltpu.SemaphoreType.DMA((len(moves),))],
        cost_estimate=pl.CostEstimate(flops=1 << 10, bytes_accessed=1 << 10, transcendentals=0),
    )(*sources)


def joined(rings, starts, rows, extra=None):
    sources, shapes, moves = [], [], []
    for result, (pieces, start) in enumerate(zip(rings, starts)):
        half = rows // 2
        shapes.append((len(pieces) * rows, pieces[0].shape[1]))
        for number, piece in enumerate(pieces):
            for which in range(2):
                to_row = (which * len(pieces) + number) * half
                moves.append((len(sources) + number, start + which * half, result, to_row, half))
        sources += pieces
    if extra is not None:
        height, width = shapes[-1]
        shapes[-1] = (height + extra.shape[0], width)
        moves.append((len(sources), 0, len(shapes) - 1, height, extra.shape[0]))
        sources.append(extra)
    return copied(sources, shapes, moves)


def half_gelu(half):
    square = jnp.minimum(half * half, LIMIT / 4)
    total = jnp.full_like(square, ERF_Q[-1] * 4.0 ** (len(ERF_Q) - 1) * 2)
    for power in range(len(ERF_Q) - 2, -1, -1):
        total = total * square + ERF_Q[power] * 4.0**power * 2
    return half * jnp.tanh(half * total) + half


def pool(docs, both, first, last, total):
    def window(start):
        start = pl.multiple_of(start, 8)
        lane = lax.broadcasted_iota(jnp.int32, docs.shape, 1)
        mask = jnp.concatenate(
            [(docs == lane + (start + part)).astype(jnp.bfloat16) for part in range(0, WINDOW, LANES)], axis=1
        )
        rows = pl.ds(start, WINDOW)
        total[rows, :] += lax.dot_general(
            jnp.concatenate([mask, mask], axis=0),
            both,
            (((0,), (0,)), ((), ())),
            preferred_element_type=jnp.float32,
        )

    window(first)

    @pl.when(last >= first + WINDOW)
    def _():
        lax.fori_loop(
            1, lax.div(last - first, WINDOW) + 1, lambda number, carry: (window(first + number * WINDOW), carry)[1], 0
        )


def split(values):
    high = values.astype(jnp.bfloat16)
    return jnp.concatenate([high, (values - high.astype(jnp.float32)).astype(jnp.bfloat16)], axis=0)


def prepare(keys, counts, table, positions, x_out, docs_out, bounds, normed_out, total, rows32, table32, listed, sem):
    width = table.shape[1]
    pieces = width // LANES

    def load():
        def gather_list(block, offset):
            base = block * SHARD_CAP

            def eight(group, carry):
                for one in range(8):
                    listed[offset + group * 8 + one] = keys[base + group * 8 + one]
                return carry

            lax.fori_loop(0, (counts[block] + 7) >> 3, eight, 0)
            return offset + counts[block]

        end = lax.fori_loop(0, 16, gather_list, 0)

        def tail(group, carry):
            for one in range(8):
                listed[end + group * 8 + one] = NONE
            return carry

        lax.fori_loop(0, TILE // 8, tail, 0)
        total[...] = jnp.zeros_like(total)

        def widen(group, carry):
            values = table[pl.ds(pl.multiple_of(group * 16, 16), 16), :].astype(jnp.float32)
            for eight in range(2):
                for piece in range(pieces):
                    place = pl.multiple_of((group * 2 + eight) * 8 * pieces + piece * 8, 8)
                    table32[pl.ds(place, 8), :] = values[
                        eight * 8 : eight * 8 + 8, piece * LANES : (piece + 1) * LANES
                    ]
            return carry

        lax.fori_loop(0, table.shape[0] // 16, widen, 0)
        return end

    end = load()
    tiles = jnp.maximum((end + TILE - 1) >> TILE_BITS, 1)
    own = total.shape[0] - WINDOW
    bounds[BOUNDS - 1] = tiles

    def tile(x_ref, docs_ref):
        first = pl.program_id(0) * TILE

        def take(group, carry):
            for one in range(8):
                key = listed[first + group * 8 + one]
                place = key & 0x7FFF
                when = pl.multiple_of((key >> 12) & 0x78, 8)
                value = table32[pl.ds(place, pieces, stride=8), :] + positions[pl.ds(when, pieces), :]
                rows32[pl.ds(group * 8 * pieces + one, pieces, stride=8), :] = value
                docs_ref[pl.ds(group * 8 + one, 1), :] = jnp.full((1, LANES), key >> 19, jnp.int32)
            return carry

        lax.fori_loop(0, TILE // 8, take, 0)
        normed = []
        for sub in range(TILE // SUB):
            block = rows32[pl.ds(sub * SUB * pieces, SUB * pieces), :].reshape(SUB // 8, pieces, 8, LANES)
            values = jnp.concatenate([block[:, piece].reshape(SUB, LANES) for piece in range(pieces)], axis=1)
            mean = jnp.mean(values, axis=-1, keepdims=True)
            centred = values - mean
            var = jnp.mean(centred * centred, axis=-1, keepdims=True)
            normal = centred * lax.rsqrt(var + 1e-05)
            x_ref[pl.ds(sub * SUB, SUB), :] = (normal * 0.5).astype(jnp.bfloat16)
            normed.append(normal)
        low = jnp.minimum((listed[first] >> 22) << 3, 2 * own - 8)
        high = jnp.minimum(listed[jnp.clip(end - 1, first, first + TILE - 1)] >> 19, 2 * own - 1)
        index = pl.program_id(0)
        bounds[2 * index] = low
        bounds[2 * index + 1] = high

        @pl.when(low < own)
        def _():
            pool(docs_ref[...], split(jnp.concatenate(normed, axis=0)), low, jnp.minimum(high, own - 1), total)

    pltpu.emit_pipeline(
        tile,
        grid=(tiles,),
        in_specs=[],
        out_specs=[
            pl.BlockSpec((TILE, width), lambda i: (i, 0)),
            pl.BlockSpec((TILE, LANES), lambda i: (i, 0)),
        ],
    )(x_out, docs_out)
    copy = pltpu.make_async_copy(total.at[pl.ds(0, own), :], normed_out, sem)
    copy.start()
    copy.wait()


def run_prepare(keys, counts, embed_table, positions, group):
    most = keys.shape[0]
    seq, width = positions.shape
    vocab_rows = embed_table.shape[0]
    pieces = width // LANES
    smem, vmem, hbm = (pl.BlockSpec(memory_space=space) for space in (pltpu.SMEM, pltpu.VMEM, pltpu.HBM))
    return pl.pallas_call(
        prepare,
        in_specs=[smem, smem, vmem, vmem],
        out_specs=[hbm, hbm, smem, hbm],
        out_shape=[
            jax.ShapeDtypeStruct((most, width), jnp.bfloat16),
            jax.ShapeDtypeStruct((most, LANES), jnp.int32),
            jax.ShapeDtypeStruct((BOUNDS,), jnp.int32),
            jax.ShapeDtypeStruct((group, width), jnp.float32),
        ],
        scratch_shapes=[
            pltpu.VMEM((group + WINDOW, width), jnp.float32),
            pltpu.VMEM((TILE * pieces, LANES), jnp.float32),
            pltpu.VMEM((vocab_rows * pieces, LANES), jnp.float32),
            pltpu.SMEM((most + TILE + 8,), jnp.int32),
            pltpu.SemaphoreType.DMA,
        ],
        compiler_params=pltpu.CompilerParams(vmem_limit_bytes=44 << 20),
        cost_estimate=pl.CostEstimate(flops=1 << 30, bytes_accessed=1 << 20, transcendentals=0),
    )(keys, counts, embed_table, positions.astype(jnp.float32).reshape(seq * pieces, LANES))


def over_tiles(tiles, several):
    def pair(number, carry):
        several(number * 2, 2)
        return carry

    lax.fori_loop(0, tiles >> 1, pair, 0)

    @pl.when((tiles & 1) == 1)
    def _():
        several(tiles - 1, 1)


def rows_of(tile, count):
    return pl.ds(pl.multiple_of(tile * TILE, TILE), count * TILE)


def load_pairs(tiles, loads):
    def copies(tile, slot):
        return [
            pltpu.make_async_copy(whole.at[rows_of(tile, 2), :], place.at[slot], sems.at[slot])
            for whole, place, sems in loads
        ]

    for copy in copies(0, 0):
        copy.start()

    def ready(tile):
        slot = (tile >> 1) & 1

        @pl.when(tile + 2 < tiles)
        def _():
            for copy in copies(tile + 2, 1 - slot):
                copy.start()

        for copy in copies(tile, slot):
            copy.wait()
        return slot

    return ready


def activate(inputs, w_in, hidden, first, staged):
    rows = pl.ds(0, inputs.shape[0])
    steps = w_in.shape[0] // CHUNK
    for number in range(steps + 1):
        if number < steps:
            weights = w_in[pl.ds(number * CHUNK, CHUNK), :]
            staged[number % 2, rows, :] = lax.dot_general(
                inputs[...], weights, (((1,), (1,)), ((), ())), preferred_element_type=jnp.float32
            )
        if number > 0:
            columns = pl.ds(first + (number - 1) * CHUNK, CHUNK)
            hidden[rows, columns] = half_gelu(staged[(number - 1) % 2, rows, :]).astype(jnp.bfloat16)


def first_units(near, bounds, x_all, *refs):
    pieces, (out, x, w_in, hidden, staged, w_sems, x_sems, out_sems) = refs[:near], refs[near:]
    tiles = bounds[BOUNDS - 1]
    units = w_in.shape[0] // near
    copies = [
        pltpu.make_async_copy(piece.at[pl.ds(0, units), :], w_in.at[pl.ds(number * units, units), :], w_sems.at[number])
        for number, piece in enumerate(pieces)
    ]
    for copy in copies:
        copy.start()
    ready = load_pairs(tiles, [(x_all, x, x_sems)])
    for copy in copies:
        copy.wait()

    def store(tile, slot):
        return pltpu.make_async_copy(hidden.at[slot], out.at[rows_of(tile, 2), :], out_sems.at[slot])

    def several(tile, count):
        slot = ready(tile)

        @pl.when(tile >= 4)
        def _():
            store(tile - 4, slot).wait()

        activate(x.at[slot, pl.ds(0, count * TILE), :], w_in, hidden.at[slot], 0, staged)
        store(tile, slot).start()

    over_tiles(tiles, several)
    last = ((tiles + 1) >> 1) * 2 - 2

    @pl.when(last >= 2)
    def _():
        store(last - 2, 1 - ((last >> 1) & 1)).wait()

    store(last, (last >> 1) & 1).wait()


def second_units(near, far, bounds, x_all, docs_all, normed, hidden_all, *refs):
    pieces, refs = refs[: near + far], refs[near + far :]
    own, other, total, x, docs, w_in, w_out, hidden, staged, w_sems, x_sems, docs_sems, hidden_sems, ends = refs
    tiles = bounds[BOUNDS - 1]
    group = own.shape[0]
    units = pieces[0].shape[0] // 2
    parts = [(piece.at[pl.ds(units, units), :], w_out, number * units) for number, piece in enumerate(pieces)]
    parts += [(piece.at[pl.ds(0, units), :], w_in, number * units) for number, piece in enumerate(pieces[near:])]
    copies = [
        pltpu.make_async_copy(part, whole.at[pl.ds(row, units), :], w_sems.at[number])
        for number, (part, whole, row) in enumerate(parts)
    ]
    copies.append(pltpu.make_async_copy(normed, total.at[pl.ds(0, group), :], ends.at[0]))
    for copy in copies:
        copy.start()
    known = hidden.at[:, :, pl.ds(0, near * units)]
    ready = load_pairs(tiles, [(x_all, x, x_sems), (docs_all, docs, docs_sems), (hidden_all, known, hidden_sems)])
    rest = total.shape[0] - group
    total[pl.ds(group, rest), :] = jnp.zeros((rest, total.shape[1]), jnp.float32)
    for copy in copies:
        copy.wait()

    def several(tile, count):
        slot = ready(tile)
        rows = pl.ds(0, count * TILE)
        activate(x.at[slot, rows, :], w_in, hidden.at[slot], near * units, staged)
        branch = jnp.dot(hidden[slot, rows, :], w_out[...], preferred_element_type=jnp.float32)
        for one in range(count):
            part = slice(one * TILE, (one + 1) * TILE)
            pool(docs[slot, part, :], split(branch[part]), bounds[2 * (tile + one)], bounds[2 * (tile + one) + 1], total)

    over_tiles(tiles, several)
    copies = [
        pltpu.make_async_copy(total.at[pl.ds(0, group), :], own, ends.at[0]),
        pltpu.make_async_copy(total.at[pl.ds(group, group), :], other, ends.at[1]),
    ]
    for copy in copies:
        copy.start()
    for copy in copies:
        copy.wait()


def run_first(near, bounds, x):
    most, width = x.shape
    units = len(near) * near[0].shape[0] // 2
    smem, hbm, anywhere = (pl.BlockSpec(memory_space=space) for space in (pltpu.SMEM, pltpu.HBM, pl.ANY))
    return pl.pallas_call(
        functools.partial(first_units, len(near)),
        in_specs=[smem, hbm] + [anywhere] * len(near),
        out_specs=hbm,
        out_shape=jax.ShapeDtypeStruct((most, units), jnp.bfloat16),
        scratch_shapes=[
            pltpu.VMEM((2, 2 * TILE, width), jnp.bfloat16),
            pltpu.VMEM((units, width), jnp.bfloat16),
            pltpu.VMEM((2, 2 * TILE, units), jnp.bfloat16),
            pltpu.VMEM((2, 2 * TILE, CHUNK), jnp.float32),
            pltpu.SemaphoreType.DMA((len(near),)),
            pltpu.SemaphoreType.DMA((2,)),
            pltpu.SemaphoreType.DMA((2,)),
        ],
        compiler_params=pltpu.CompilerParams(vmem_limit_bytes=44 << 20),
        cost_estimate=pl.CostEstimate(flops=12 << 30, bytes_accessed=16 << 20, transcendentals=0),
    )(bounds, x, *near)


def run_second(near, far, bounds, x, docs, normed, hidden):
    most, width = x.shape
    group = normed.shape[0]
    units = near[0].shape[0] // 2
    count = len(near) + len(far)
    smem, hbm, anywhere = (pl.BlockSpec(memory_space=space) for space in (pltpu.SMEM, pltpu.HBM, pl.ANY))
    return pl.pallas_call(
        functools.partial(second_units, len(near), len(far)),
        in_specs=[smem, hbm, hbm, anywhere, hbm] + [anywhere] * count,
        out_specs=[anywhere, anywhere],
        out_shape=[jax.ShapeDtypeStruct((group, width), jnp.float32)] * 2,
        scratch_shapes=[
            pltpu.VMEM((2 * group + WINDOW, width), jnp.float32),
            pltpu.VMEM((2, 2 * TILE, width), jnp.bfloat16),
            pltpu.VMEM((2, 2 * TILE, LANES), jnp.int32),
            pltpu.VMEM((len(far) * units, width), jnp.bfloat16),
            pltpu.VMEM((count * units, width), jnp.bfloat16),
            pltpu.VMEM((2, 2 * TILE, count * units), jnp.bfloat16),
            pltpu.VMEM((2, 2 * TILE, CHUNK), jnp.float32),
            pltpu.SemaphoreType.DMA((count + len(far),)),
            pltpu.SemaphoreType.DMA((2,)),
            pltpu.SemaphoreType.DMA((2,)),
            pltpu.SemaphoreType.DMA((2,)),
            pltpu.SemaphoreType.DMA((2,)),
        ],
        compiler_params=pltpu.CompilerParams(vmem_limit_bytes=34 << 20),
        cost_estimate=pl.CostEstimate(flops=16 << 30, bytes_accessed=24 << 20, transcendentals=0),
    )(bounds, x, docs, normed, hidden, *near, *far)


def local(token_ids, doc_lengths, clusters, embed_table, positions, w_in, w_out):
    doc_dev = doc_lengths.shape[0]
    group, seq = token_ids.shape
    vocab_rows, width = embed_table.shape
    n_col = group // doc_dev

    with jax.named_scope("weights"):
        half = w_in.shape[0] // 2
        mixed = jnp.concatenate([w_in[:half], w_out[:half], w_in[half:], w_out[half:]], axis=0)
        lengths = jnp.pad(doc_lengths, (0, width - doc_dev))[None].astype(jnp.bfloat16)
        over = lax.ppermute(lengths, "x_hi", [(0, 1), (1, 0)])
        cross = lax.ppermute(lengths, ("core", "x_hi"), [(0, 3), (1, 2), (2, 1), (3, 0)])
        upper = lax.axis_index("x_hi")
        places = lax.broadcasted_iota(jnp.int32, (16, width), 0)
        parts = [(0, 0, lengths), (0, 1, over), (1, 0, step(lengths, "core", 1)), (1, 1, cross)]
        lengths = functools.reduce(
            lambda known, part: jnp.where(places == 2 * part[0] + (upper ^ part[1]), part[2], known),
            parts,
            jnp.zeros((16, width), jnp.bfloat16),
        )
        by_z = ring(mixed, "z")
        first, second = joined([by_z, by_z], [0, 2 * half], 2 * half, lengths)
        rows = first.shape[0]
        mixed, token_ids = lax.optimization_barrier((mixed, token_ids))
        ids = token_ids.reshape(n_col, doc_dev * seq)
        ids = jnp.concatenate([ids, step(ids, "core", 1)], axis=0)
        row = ids - lax.axis_index(COL) * vocab_rows
        block = lax.broadcasted_iota(jnp.int32, ids.shape, 0)
        token = lax.broadcasted_iota(jnp.int32, ids.shape, 1)
        keys = ((block * doc_dev + (token >> SEQ_BITS)) << 19) + ((token & (seq - 1)) << 15)
        keys = jnp.where((row >= 0) & (row < vocab_rows), keys + (row >> 3) * 64 + (row & 7), NONE)
        first, second = ring(first, X), ring(second, "y")
        lengths = [piece[rows : rows + 4, :doc_dev].reshape(2, 2, 1, doc_dev) for piece in second]
        away = lax.broadcasted_iota(jnp.int32, (2, 2, 4, doc_dev), 2) - lax.axis_index("y") & 3
        lengths = functools.reduce(
            lambda known, by: jnp.where(away == by[0], by[1], known), zip((3, 1, 2), lengths[1:]), lengths[0]
        ).reshape(2 * n_col, doc_dev)
        first, second, lengths, keys = lax.optimization_barrier((first, second, lengths, keys))
        first, second = joined([first, second], [0, 0], rows)
        units = first.shape[0] // 2
        left, right = step(first, "y", 1), step(first, "y", -1)
        down, up = step(second, X, 1), step(second, X, -1)
        near = [first, left, right, second, down, up]

    with jax.named_scope("keys"):
        token = jnp.arange(doc_dev * seq, dtype=jnp.int32)[None, :]
        of_doc = (jnp.arange(doc_dev, dtype=jnp.int32)[:, None] == token >> SEQ_BITS).astype(jnp.bfloat16)
        used = jnp.dot(lengths, of_doc, preferred_element_type=jnp.float32)
        keys = jnp.where((token & (seq - 1)).astype(jnp.float32) < used, keys, NONE)
        counts = jnp.sum((keys < NONE).astype(jnp.int32), axis=1)
        keys = lax.sort(keys, dimension=1)[:, :SHARD_CAP].reshape(-1)

    with jax.named_scope("prepare"):
        x, docs, bounds, normed = run_prepare(keys, counts, embed_table, positions, group)

    with jax.named_scope("forward"):
        far = [step(first, "y", 2), step(second, X, 2)]
        hidden = run_first(near, bounds, x)
        own, other = run_second(near, far, bounds, x, docs, normed, hidden)

    with jax.named_scope("pooled"):
        sums = own + step(other, "core", 1)
        sums = sums.astype(jnp.bfloat16).reshape(n_col, doc_dev, width)
        sums = lax.all_to_all(sums, COL, 0, 0, tiled=True)
        pooled = jnp.sum(sums.astype(jnp.float32), axis=0) / doc_lengths.astype(jnp.float32)[:, None]
        scale = lax.rsqrt(jnp.sum(pooled * pooled, axis=-1, keepdims=True) + 1e-06)
        embedding = (pooled * scale).astype(jnp.bfloat16)

    with jax.named_scope("match"):
        n_clusters = lax.axis_size(CHIPS)
        labels = clusters[:, 0]
        same = labels[:, None] == labels[None, :]
        order = jnp.arange(doc_dev, dtype=jnp.int32)
        rank = jnp.sum((same & (order[:, None] > order[None, :])).astype(jnp.int32), axis=1)
        slot = labels * 4 + rank
        chosen = slot[None, :] == jnp.arange(n_clusters * 4, dtype=jnp.int32)[:, None]
        sizes = jnp.sum((labels[None, :] == jnp.arange(n_clusters)[:, None]).astype(jnp.int32), axis=1)
        fourth = lax.broadcasted_iota(jnp.int32, (n_clusters, 4, width), 1) == 3
        flags = lax.broadcasted_iota(jnp.int32, (n_clusters, 4, width), 2) < sizes[:, None, None]
        outgoing = jnp.dot(chosen.astype(jnp.bfloat16), embedding, preferred_element_type=jnp.float32)
        outgoing = jnp.where(
            fourth, flags.astype(jnp.float32), outgoing.reshape(n_clusters, 4, width)
        ).astype(jnp.bfloat16)
        members = lax.all_to_all(outgoing, CHIPS, 0, 0, tiled=True)
        others = step(members, "core", 1)
        every = jnp.concatenate([members, others], axis=0)
        filled = jnp.pad(every[:, 3, :3], ((0, 0), (0, 1))).reshape(-1) > 0.5
        count = n_clusters * 4
        scores = jnp.dot(
            members.reshape(count, width), every.reshape(2 * count, width).T, preferred_element_type=jnp.float32
        )
        own = jnp.arange(count)[:, None] == jnp.arange(2 * count)[None, :]
        best = jnp.max(jnp.where(filled[None, :] & jnp.logical_not(own), scores, -1.0), axis=1)
        best = jnp.maximum(best, -1.0)
        returned = lax.all_to_all(best.reshape(n_clusters, 4), CHIPS, 0, 0, tiled=True).reshape(-1)
        return jnp.sum(jnp.where(chosen, returned[:, None], 0.0), axis=0)


def solution(mesh):
    fine = Mesh(mesh.devices.reshape(2, 4, 2, 2, 4), ("x_lo", "z", "core", "x_hi", "y"))
    everywhere = OWN + COL
    return jax.shard_map(
        local,
        mesh=fine,
        in_specs=(
            P(OWN, None),
            P(everywhere),
            P(everywhere, None),
            P(COL, None),
            P(),
            P(everywhere, None),
            P(everywhere, None),
        ),
        out_specs=P(everywhere),
        check_vma=False,
    )
```

```python
import functools

import jax
import jax.numpy as jnp
from jax import lax
from jax.experimental import pallas as pl
from jax.experimental.pallas import tpu as pltpu
from jax.sharding import Mesh
from jax.sharding import PartitionSpec as P

OWN = ("x_lo", "z", "core")
COL = ("x_hi", "y")
X = ("x_lo", "x_hi")
CHIPS = ("x_lo", "z", "x_hi", "y")
SHARD_CAP = 384
TILE_BITS = 8
TILE = 1 << TILE_BITS
LANES = 128
SUB = 64
SEQ_BITS = 4
SEQ = 1 << SEQ_BITS
NONE = 1 << 30
BOUNDS = 64
CHUNK = 256
WINDOW = 384
LIMIT = 5.4 * 5.4
ERF_Q = (
    0.7978853416207131,
    0.03633264203955081,
    -3.271896418592583e-05,
    -5.512179284196367e-05,
    3.917683168513537e-06,
    -1.2794852180568973e-07,
    1.6281616374933989e-09,
)


def step(value, axis, by):
    count = 2 if axis == "core" else 4
    place = (lambda x: (x % 2) * 2 + x // 2) if axis == X else (lambda x: x)
    return lax.ppermute(value, axis, [(place(i), place((i + by) % count)) for i in range(count)])


def ring(value, axis):
    return [value] + [step(value, axis, by) for by in (1, -1, 2)]


def copied(sources, shapes, moves):
    def kernel(*refs):
        inputs, (*outputs, sems) = refs[: len(sources)], refs[len(sources) :]
        copies = [
            pltpu.make_async_copy(
                inputs[source].at[pl.ds(from_row, rows), :], outputs[result].at[pl.ds(to_row, rows), :], sems.at[number]
            )
            for number, (source, from_row, result, to_row, rows) in enumerate(moves)
        ]
        for copy in copies:
            copy.start()
        for copy in copies:
            copy.wait()

    return pl.pallas_call(
        kernel,
        in_specs=[pl.BlockSpec(memory_space=pl.ANY)] * len(sources),
        out_specs=[pl.BlockSpec(memory_space=pltpu.VMEM)] * len(shapes),
        out_shape=[jax.ShapeDtypeStruct(shape, sources[0].dtype) for shape in shapes],
        scratch_shapes=[pltpu.SemaphoreType.DMA((len(moves),))],
        compiler_params=pltpu.CompilerParams(vmem_limit_bytes=8 << 20),
        cost_estimate=pl.CostEstimate(flops=1 << 10, bytes_accessed=1 << 10, transcendentals=0),
    )(*sources)


def joined(rings, starts, rows, extra=None):
    sources, shapes, moves = [], [], []
    for result, (pieces, start) in enumerate(zip(rings, starts)):
        half = rows // 2
        shapes.append((len(pieces) * rows, pieces[0].shape[1]))
        for number, piece in enumerate(pieces):
            for which in range(2):
                to_row = (which * len(pieces) + number) * half
                moves.append((len(sources) + number, start + which * half, result, to_row, half))
        sources += pieces
    if extra is not None:
        height, width = shapes[-1]
        shapes[-1] = (height + extra.shape[0], width)
        moves.append((len(sources), 0, len(shapes) - 1, height, extra.shape[0]))
        sources.append(extra)
    return copied(sources, shapes, moves)


def half_gelu(half):
    square = jnp.minimum(half * half, LIMIT / 4)
    total = jnp.full_like(square, ERF_Q[-1] * 4.0 ** (len(ERF_Q) - 1) * 2)
    for power in range(len(ERF_Q) - 2, -1, -1):
        total = total * square + ERF_Q[power] * 4.0**power * 2
    return half * jnp.tanh(half * total) + half


def pool(docs, both, first, last, total):
    def window(start):
        start = pl.multiple_of(start, 8)
        lane = lax.broadcasted_iota(jnp.int32, docs.shape, 1)
        mask = jnp.concatenate(
            [(docs == lane + (start + part)).astype(jnp.bfloat16) for part in range(0, WINDOW, LANES)], axis=1
        )
        rows = pl.ds(start, WINDOW)
        total[rows, :] += lax.dot_general(
            jnp.concatenate([mask, mask], axis=0),
            both,
            (((0,), (0,)), ((), ())),
            preferred_element_type=jnp.float32,
        )

    window(first)

    @pl.when(last >= first + WINDOW)
    def _():
        lax.fori_loop(
            1, lax.div(last - first, WINDOW) + 1, lambda number, carry: (window(first + number * WINDOW), carry)[1], 0
        )


def split(values):
    high = values.astype(jnp.bfloat16)
    return jnp.concatenate([high, (values - high.astype(jnp.float32)).astype(jnp.bfloat16)], axis=0)


def compressed(keys, docs_of, used):
    rows = keys.shape[0]
    kept = (keys < NONE) & (docs_of < used)
    ones = kept.astype(jnp.bfloat16)
    row, lane = (lax.broadcasted_iota(jnp.int32, (LANES, LANES), axis) for axis in range(2))
    before = jnp.dot(ones, (row < lane).astype(jnp.bfloat16), preferred_element_type=jnp.float32)
    whole = jnp.dot(ones, jnp.ones((LANES, LANES), jnp.bfloat16), preferred_element_type=jnp.float32)
    row, lane = (lax.broadcasted_iota(jnp.int32, (rows, rows), axis) for axis in range(2))
    above = (lane < row).astype(jnp.bfloat16)
    before += jnp.dot(above, whole.astype(jnp.bfloat16), preferred_element_type=jnp.float32)
    row, lane = (lax.broadcasted_iota(jnp.int32, keys.shape, axis) for axis in range(2))
    moves = jnp.where(kept, row * LANES + lane - before.astype(jnp.int32), 0)
    keys = jnp.where(kept, keys, NONE)
    for bit in range((rows * LANES - 1).bit_length()):
        step_by = 1 << bit

        def after(values):
            if step_by >= LANES:
                return pltpu.roll(values, rows - step_by // LANES, 0)
            values = pltpu.roll(values, LANES - step_by, 1)
            return jnp.where(lane < LANES - step_by, values, pltpu.roll(values, rows - 1, 0))

        next_moves, next_keys = after(moves), after(keys)
        comes, goes = (next_moves & step_by) != 0, (moves & step_by) != 0
        keys = jnp.where(comes, next_keys, jnp.where(goes, NONE, keys))
        moves = jnp.where(comes, next_moves, jnp.where(goes, 0, moves))
    return keys, jnp.sum(ones.astype(jnp.float32), axis=0, keepdims=True)


def prepare(place, ids, l0, l1, l2, l3, table, positions, x_out, docs_out, bounds, normed_out, *scratch):
    total, rows32, table32, lengths, list_buffer, listed, sem, length_sems = scratch
    width = table.shape[1]
    pieces = width // LANES

    def load():
        copies = [
            pltpu.make_async_copy(piece.at[pl.ds(piece.shape[0] - 16, 16), :], lengths.at[number], length_sems.at[number])
            for number, piece in enumerate((l0, l1, l2, l3))
        ]
        for copy in copies:
            copy.start()
        total[...] = jnp.zeros_like(total)

        def widen(group, carry):
            values = table[pl.ds(pl.multiple_of(group * 16, 16), 16), :].astype(jnp.float32)
            for eight in range(2):
                for piece in range(pieces):
                    at = pl.multiple_of((group * 2 + eight) * 8 * pieces + piece * 8, 8)
                    table32[pl.ds(at, 8), :] = values[eight * 8 : eight * 8 + 8, piece * LANES : (piece + 1) * LANES]
            return carry

        lax.fori_loop(0, table.shape[0] // 16, widen, 0)
        for copy in copies:
            copy.wait()
        row, lane = (lax.broadcasted_iota(jnp.int32, (LANES, LANES), axis) for axis in range(2))
        of_doc = (row == lane >> SEQ_BITS).astype(jnp.bfloat16)
        used = []
        for part in range(4):
            columns = slice(part * LANES, (part + 1) * LANES)
            around = [
                jnp.dot(lengths[number, :, columns], of_doc, preferred_element_type=jnp.float32) for number in range(4)
            ]
            for y in range(4):
                away = (y - place[1]) & 3
                value = around[0]
                for by, number in ((3, 1), (1, 2), (2, 3)):
                    value = jnp.where(away == by, around[number], value)
                used.append(value)
        used = jnp.concatenate(used, axis=0).astype(jnp.int32)
        row, lane = (lax.broadcasted_iota(jnp.int32, ids.shape, axis) for axis in range(2))
        own_row = ids[...] - place[0]
        doc = (row >> 4) * (12 * 8) + (row & 15) * 8 + (lane >> SEQ_BITS)
        time = lane & (SEQ - 1)
        keys = (doc << 19) + (time << 15) + (own_row >> 3) * 64 + (own_row & 7)
        inside = (own_row >= 0) & (own_row < table.shape[0]) & ((row & 15) < 12)
        keys, sums = compressed(jnp.where(inside, keys, NONE), time, used)
        most = listed.shape[0] - 8
        list_buffer[pl.ds(0, most), :] = keys[:most]
        count = jnp.sum(sums, axis=1, keepdims=True).astype(jnp.int32)
        list_buffer[pl.ds(most, 8), :] = jnp.broadcast_to(count, (8, LANES))
        copy = pltpu.make_async_copy(list_buffer, listed, sem)
        copy.start()
        copy.wait()
        return listed[most, 0]

    end = load()
    tiles = jnp.maximum((end + TILE - 1) >> TILE_BITS, 1)
    own = total.shape[0] - WINDOW
    bounds[BOUNDS - 1] = tiles

    def tile(x_ref, docs_ref):
        index = pl.program_id(0)
        first = index * TILE

        def key_at(slot):
            return listed[slot >> 7, slot & (LANES - 1)]

        def take(group, carry):
            for one in range(8):
                key = listed[2 * index + (group >> 4), (group & 15) * 8 + one]
                at = key & 0x7FFF
                when = pl.multiple_of((key >> 12) & 0x78, 8)
                value = table32[pl.ds(at, pieces, stride=8), :] + positions[pl.ds(when, pieces), :]
                rows32[pl.ds(group * 8 * pieces + one, pieces, stride=8), :] = value
                docs_ref[pl.ds(group * 8 + one, 1), :] = jnp.full((1, LANES), key >> 19, jnp.int32)
            return carry

        lax.fori_loop(0, TILE // 8, take, 0)
        normed = []
        for sub in range(TILE // SUB):
            block = rows32[pl.ds(sub * SUB * pieces, SUB * pieces), :].reshape(SUB // 8, pieces, 8, LANES)
            values = jnp.concatenate([block[:, piece].reshape(SUB, LANES) for piece in range(pieces)], axis=1)
            mean = jnp.mean(values, axis=-1, keepdims=True)
            centred = values - mean
            var = jnp.mean(centred * centred, axis=-1, keepdims=True)
            normal = centred * lax.rsqrt(var + 1e-05)
            x_ref[pl.ds(sub * SUB, SUB), :] = (normal * 0.5).astype(jnp.bfloat16)
            normed.append(normal)
        low = jnp.minimum((key_at(first) >> 22) << 3, 2 * own - 8)
        high = jnp.minimum(key_at(jnp.clip(end - 1, first, first + TILE - 1)) >> 19, 2 * own - 1)
        bounds[2 * index] = low
        bounds[2 * index + 1] = high

        @pl.when(low < own)
        def _():
            pool(docs_ref[...], split(jnp.concatenate(normed, axis=0)), low, jnp.minimum(high, own - 1), total)

    pltpu.emit_pipeline(
        tile,
        grid=(tiles,),
        in_specs=[],
        out_specs=[
            pl.BlockSpec((TILE, width), lambda i: (i, 0)),
            pl.BlockSpec((TILE, LANES), lambda i: (i, 0)),
        ],
    )(x_out, docs_out)
    copy = pltpu.make_async_copy(total.at[pl.ds(0, own), :], normed_out, sem)
    copy.start()
    copy.wait()


def run_prepare(place, ids, lengths, embed_table, positions, group, most):
    seq, width = positions.shape
    vocab_rows = embed_table.shape[0]
    pieces = width // LANES
    smem, vmem, hbm = (pl.BlockSpec(memory_space=space) for space in (pltpu.SMEM, pltpu.VMEM, pltpu.HBM))
    return pl.pallas_call(
        prepare,
        in_specs=[smem, vmem] + [pl.BlockSpec(memory_space=pl.ANY)] * 4 + [vmem, vmem],
        out_specs=[hbm, hbm, smem, hbm],
        out_shape=[
            jax.ShapeDtypeStruct((most, width), jnp.bfloat16),
            jax.ShapeDtypeStruct((most, LANES), jnp.int32),
            jax.ShapeDtypeStruct((BOUNDS,), jnp.int32),
            jax.ShapeDtypeStruct((group, width), jnp.float32),
        ],
        scratch_shapes=[
            pltpu.VMEM((group + WINDOW, width), jnp.float32),
            pltpu.VMEM((TILE * pieces, LANES), jnp.float32),
            pltpu.VMEM((vocab_rows * pieces, LANES), jnp.float32),
            pltpu.VMEM((4, 16, width), jnp.bfloat16),
            pltpu.VMEM((most // LANES + 8, LANES), jnp.int32),
            pltpu.SMEM((most // LANES + 8, LANES), jnp.int32),
            pltpu.SemaphoreType.DMA,
            pltpu.SemaphoreType.DMA((4,)),
        ],
        compiler_params=pltpu.CompilerParams(vmem_limit_bytes=36 << 20),
        cost_estimate=pl.CostEstimate(flops=1 << 30, bytes_accessed=1 << 20, transcendentals=0),
    )(place, ids, *lengths, embed_table, positions.astype(jnp.float32).reshape(seq * pieces, LANES))


def over_tiles(tiles, several):
    def pair(number, carry):
        several(number * 2, 2)
        return carry

    lax.fori_loop(0, tiles >> 1, pair, 0)

    @pl.when((tiles & 1) == 1)
    def _():
        several(tiles - 1, 1)


def rows_of(tile, count):
    return pl.ds(pl.multiple_of(tile * TILE, TILE), count * TILE)


def load_pairs(tiles, loads):
    def copies(tile, slot):
        return [
            pltpu.make_async_copy(whole.at[rows_of(tile, 2), :], place.at[slot], sems.at[slot])
            for whole, place, sems in loads
        ]

    for copy in copies(0, 0):
        copy.start()

    def ready(tile):
        slot = (tile >> 1) & 1

        @pl.when(tile + 2 < tiles)
        def _():
            for copy in copies(tile + 2, 1 - slot):
                copy.start()

        for copy in copies(tile, slot):
            copy.wait()
        return slot

    return ready


def activate(inputs, w_in, hidden, first, staged):
    rows = pl.ds(0, inputs.shape[0])
    steps = w_in.shape[0] // CHUNK
    for number in range(steps + 1):
        if number < steps:
            weights = w_in[pl.ds(number * CHUNK, CHUNK), :]
            staged[number % 2, rows, :] = lax.dot_general(
                inputs[...], weights, (((1,), (1,)), ((), ())), preferred_element_type=jnp.float32
            )
        if number > 0:
            columns = pl.ds(first + (number - 1) * CHUNK, CHUNK)
            hidden[rows, columns] = half_gelu(staged[(number - 1) % 2, rows, :]).astype(jnp.bfloat16)


def first_units(near, bounds, x_all, *refs):
    pieces, (out, x, w_in, hidden, staged, w_sems, x_sems, out_sems) = refs[:near], refs[near:]
    tiles = bounds[BOUNDS - 1]
    units = w_in.shape[0] // near
    copies = [
        pltpu.make_async_copy(piece.at[pl.ds(0, units), :], w_in.at[pl.ds(number * units, units), :], w_sems.at[number])
        for number, piece in enumerate(pieces)
    ]
    for copy in copies:
        copy.start()
    ready = load_pairs(tiles, [(x_all, x, x_sems)])
    for copy in copies:
        copy.wait()

    def store(tile, slot):
        return pltpu.make_async_copy(hidden.at[slot], out.at[rows_of(tile, 2), :], out_sems.at[slot])

    def several(tile, count):
        slot = ready(tile)

        @pl.when(tile >= 4)
        def _():
            store(tile - 4, slot).wait()

        activate(x.at[slot, pl.ds(0, count * TILE), :], w_in, hidden.at[slot], 0, staged)
        store(tile, slot).start()

    over_tiles(tiles, several)
    last = ((tiles + 1) >> 1) * 2 - 2

    @pl.when(last >= 2)
    def _():
        store(last - 2, 1 - ((last >> 1) & 1)).wait()

    store(last, (last >> 1) & 1).wait()


def second_units(near, far, bounds, x_all, docs_all, normed, hidden_all, *refs):
    pieces, refs = refs[: near + far], refs[near + far :]
    own, other, total, x, docs, w_in, w_out, hidden, staged, w_sems, x_sems, docs_sems, hidden_sems, ends = refs
    tiles = bounds[BOUNDS - 1]
    group = own.shape[0]
    units = pieces[0].shape[0] // 2
    parts = [(piece.at[pl.ds(units, units), :], w_out, number * units) for number, piece in enumerate(pieces)]
    parts += [(piece.at[pl.ds(0, units), :], w_in, number * units) for number, piece in enumerate(pieces[near:])]
    copies = [
        pltpu.make_async_copy(part, whole.at[pl.ds(row, units), :], w_sems.at[number])
        for number, (part, whole, row) in enumerate(parts)
    ]
    copies.append(pltpu.make_async_copy(normed, total.at[pl.ds(0, group), :], ends.at[0]))
    for copy in copies:
        copy.start()
    known = hidden.at[:, :, pl.ds(0, near * units)]
    ready = load_pairs(tiles, [(x_all, x, x_sems), (docs_all, docs, docs_sems), (hidden_all, known, hidden_sems)])
    rest = total.shape[0] - group
    total[pl.ds(group, rest), :] = jnp.zeros((rest, total.shape[1]), jnp.float32)
    for copy in copies:
        copy.wait()

    def several(tile, count):
        slot = ready(tile)
        rows = pl.ds(0, count * TILE)
        activate(x.at[slot, rows, :], w_in, hidden.at[slot], near * units, staged)
        branch = jnp.dot(hidden[slot, rows, :], w_out[...], preferred_element_type=jnp.float32)
        for one in range(count):
            part = slice(one * TILE, (one + 1) * TILE)
            pool(docs[slot, part, :], split(branch[part]), bounds[2 * (tile + one)], bounds[2 * (tile + one) + 1], total)

    over_tiles(tiles, several)
    copies = [
        pltpu.make_async_copy(total.at[pl.ds(0, group), :], own, ends.at[0]),
        pltpu.make_async_copy(total.at[pl.ds(group, group), :], other, ends.at[1]),
    ]
    for copy in copies:
        copy.start()
    for copy in copies:
        copy.wait()


def run_first(near, bounds, x):
    most, width = x.shape
    units = len(near) * near[0].shape[0] // 2
    smem, hbm, anywhere = (pl.BlockSpec(memory_space=space) for space in (pltpu.SMEM, pltpu.HBM, pl.ANY))
    return pl.pallas_call(
        functools.partial(first_units, len(near)),
        in_specs=[smem, hbm] + [anywhere] * len(near),
        out_specs=hbm,
        out_shape=jax.ShapeDtypeStruct((most, units), jnp.bfloat16),
        scratch_shapes=[
            pltpu.VMEM((2, 2 * TILE, width), jnp.bfloat16),
            pltpu.VMEM((units, width), jnp.bfloat16),
            pltpu.VMEM((2, 2 * TILE, units), jnp.bfloat16),
            pltpu.VMEM((2, 2 * TILE, CHUNK), jnp.float32),
            pltpu.SemaphoreType.DMA((len(near),)),
            pltpu.SemaphoreType.DMA((2,)),
            pltpu.SemaphoreType.DMA((2,)),
        ],
        compiler_params=pltpu.CompilerParams(vmem_limit_bytes=44 << 20),
        cost_estimate=pl.CostEstimate(flops=12 << 30, bytes_accessed=16 << 20, transcendentals=0),
    )(bounds, x, *near)


def run_second(near, far, bounds, x, docs, normed, hidden):
    most, width = x.shape
    group = normed.shape[0]
    units = near[0].shape[0] // 2
    count = len(near) + len(far)
    smem, hbm, anywhere = (pl.BlockSpec(memory_space=space) for space in (pltpu.SMEM, pltpu.HBM, pl.ANY))
    return pl.pallas_call(
        functools.partial(second_units, len(near), len(far)),
        in_specs=[smem, hbm, hbm, anywhere, hbm] + [anywhere] * count,
        out_specs=[anywhere, anywhere],
        out_shape=[jax.ShapeDtypeStruct((group, width), jnp.float32)] * 2,
        scratch_shapes=[
            pltpu.VMEM((2 * group + WINDOW, width), jnp.float32),
            pltpu.VMEM((2, 2 * TILE, width), jnp.bfloat16),
            pltpu.VMEM((2, 2 * TILE, LANES), jnp.int32),
            pltpu.VMEM((len(far) * units, width), jnp.bfloat16),
            pltpu.VMEM((count * units, width), jnp.bfloat16),
            pltpu.VMEM((2, 2 * TILE, count * units), jnp.bfloat16),
            pltpu.VMEM((2, 2 * TILE, CHUNK), jnp.float32),
            pltpu.SemaphoreType.DMA((count + len(far),)),
            pltpu.SemaphoreType.DMA((2,)),
            pltpu.SemaphoreType.DMA((2,)),
            pltpu.SemaphoreType.DMA((2,)),
            pltpu.SemaphoreType.DMA((2,)),
        ],
        compiler_params=pltpu.CompilerParams(vmem_limit_bytes=34 << 20),
        cost_estimate=pl.CostEstimate(flops=16 << 30, bytes_accessed=24 << 20, transcendentals=0),
    )(bounds, x, docs, normed, hidden, *near, *far)


def local(token_ids, doc_lengths, clusters, embed_table, positions, w_in, w_out):
    doc_dev = doc_lengths.shape[0]
    group, seq = token_ids.shape
    vocab_rows, width = embed_table.shape
    n_col = group // doc_dev

    with jax.named_scope("weights"):
        half = w_in.shape[0] // 2
        mixed = jnp.concatenate([w_in[:half], w_out[:half], w_in[half:], w_out[half:]], axis=0)
        mixed, token_ids, doc_lengths = lax.optimization_barrier((mixed, token_ids, doc_lengths))
        lengths = jnp.pad(doc_lengths.reshape(doc_dev // 8, 8), ((0, 16 - doc_dev // 8), (0, LANES - 8))).astype(jnp.bfloat16)
        over = lax.ppermute(lengths, "x_hi", [(0, 1), (1, 0)])
        cross = lax.ppermute(lengths, ("core", "x_hi"), [(0, 3), (1, 2), (2, 1), (3, 0)])
        other = step(lengths, "core", 1)
        lower = lax.axis_index("x_hi") == 0
        parts = [jnp.where(lower, a, b) for a, b in ((lengths, over), (over, lengths), (other, cross), (cross, other))]
        lengths = jnp.pad(jnp.concatenate(parts, axis=1), ((0, 0), (0, width - 4 * LANES)))
        by_z = ring(mixed, "z")
        first, second = joined([by_z, by_z], [0, 2 * half], 2 * half, lengths)
        rows = first.shape[0]
        ids = token_ids.reshape(n_col, doc_dev * seq // LANES, LANES)
        ids = jnp.pad(ids, ((0, 0), (0, 16 - ids.shape[1]), (0, 0))).reshape(n_col * 16, LANES)
        ids = jnp.concatenate([ids, step(ids, "core", 1)], axis=0)
        place = jnp.stack([lax.axis_index(COL) * vocab_rows, lax.axis_index("y")]).astype(jnp.int32)
        first, second, ids = lax.optimization_barrier((first, second, ids))
        first, second = ring(first, X), ring(second, "y")
        lengths = second
        first, second = joined([first, second], [0, 0], rows)
        units = first.shape[0] // 2
        left, right = step(first, "y", 1), step(first, "y", -1)
        down, up = step(second, X, 1), step(second, X, -1)
        near = [first, left, right, second, down, up]

    with jax.named_scope("prepare"):
        most = 2 * n_col * SHARD_CAP
        x, docs, bounds, normed = run_prepare(place, ids, lengths, embed_table, positions, group, most)

    with jax.named_scope("forward"):
        near, x = lax.optimization_barrier((near, x))
        far = [step(near[0], "y", 2), step(near[3], X, 2)]
        hidden = run_first(near, bounds, x)
        own, other = run_second(near, far, bounds, x, docs, normed, hidden)

    with jax.named_scope("pooled"):
        sums = own + step(other, "core", 1)
        sums = sums.astype(jnp.bfloat16).reshape(n_col, doc_dev, width)
        sums = lax.all_to_all(sums, COL, 0, 0, tiled=True)
        pooled = jnp.sum(sums.astype(jnp.float32), axis=0) / doc_lengths.astype(jnp.float32)[:, None]
        scale = lax.rsqrt(jnp.sum(pooled * pooled, axis=-1, keepdims=True) + 1e-06)
        embedding = (pooled * scale).astype(jnp.bfloat16)

    with jax.named_scope("match"):
        n_clusters = lax.axis_size(CHIPS)
        labels = clusters[:, 0]
        same = labels[:, None] == labels[None, :]
        order = jnp.arange(doc_dev, dtype=jnp.int32)
        rank = jnp.sum((same & (order[:, None] > order[None, :])).astype(jnp.int32), axis=1)
        slot = labels * 4 + rank
        chosen = slot[None, :] == jnp.arange(n_clusters * 4, dtype=jnp.int32)[:, None]
        sizes = jnp.sum((labels[None, :] == jnp.arange(n_clusters)[:, None]).astype(jnp.int32), axis=1)
        fourth = lax.broadcasted_iota(jnp.int32, (n_clusters, 4, width), 1) == 3
        flags = lax.broadcasted_iota(jnp.int32, (n_clusters, 4, width), 2) < sizes[:, None, None]
        outgoing = jnp.dot(chosen.astype(jnp.bfloat16), embedding, preferred_element_type=jnp.float32)
        outgoing = jnp.where(
            fourth, flags.astype(jnp.float32), outgoing.reshape(n_clusters, 4, width)
        ).astype(jnp.bfloat16)
        members = lax.all_to_all(outgoing, CHIPS, 0, 0, tiled=True)
        others = step(members, "core", 1)
        every = jnp.concatenate([members, others], axis=0)
        filled = jnp.pad(every[:, 3, :3], ((0, 0), (0, 1))).reshape(-1) > 0.5
        count = n_clusters * 4
        scores = jnp.dot(
            members.reshape(count, width), every.reshape(2 * count, width).T, preferred_element_type=jnp.float32
        )
        own = jnp.arange(count)[:, None] == jnp.arange(2 * count)[None, :]
        best = jnp.max(jnp.where(filled[None, :] & jnp.logical_not(own), scores, -1.0), axis=1)
        best = jnp.maximum(best, -1.0)
        returned = lax.all_to_all(best.reshape(n_clusters, 4), CHIPS, 0, 0, tiled=True).reshape(-1)
        return jnp.sum(jnp.where(chosen, returned[:, None], 0.0), axis=0)


def solution(mesh):
    fine = Mesh(mesh.devices.reshape(2, 4, 2, 2, 4), ("x_lo", "z", "core", "x_hi", "y"))
    everywhere = OWN + COL
    return jax.shard_map(
        local,
        mesh=fine,
        in_specs=(
            P(OWN, None),
            P(everywhere),
            P(everywhere, None),
            P(COL, None),
            P(),
            P(everywhere, None),
            P(everywhere, None),
        ),
        out_specs=P(everywhere),
        check_vma=False,
    )
```

```python
import functools

import jax
import jax.numpy as jnp
from jax import lax
from jax.experimental import pallas as pl
from jax.experimental.pallas import tpu as pltpu
from jax.sharding import Mesh
from jax.sharding import PartitionSpec as P

OWN = ("x_lo", "z", "core")
COL = ("x_hi", "y")
X = ("x_lo", "x_hi")
CHIPS = ("x_lo", "z", "x_hi", "y")
SHARD_CAP = 384
TILE_BITS = 8
TILE = 1 << TILE_BITS
LANES = 128
SUB = 64
SEQ_BITS = 4
SEQ = 1 << SEQ_BITS
NONE = 1 << 30
BOUNDS = 64
CHUNK = 256
WINDOW = 384
LIMIT = 5.4 * 5.4
ERF_Q = (
    0.7978853416207131,
    0.03633264203955081,
    -3.271896418592583e-05,
    -5.512179284196367e-05,
    3.917683168513537e-06,
    -1.2794852180568973e-07,
    1.6281616374933989e-09,
)


def step(value, axis, by):
    count = 2 if axis == "core" else 4
    place = (lambda x: (x % 2) * 2 + x // 2) if axis == X else (lambda x: x)
    return lax.ppermute(value, axis, [(place(i), place((i + by) % count)) for i in range(count)])


def ring(value, axis):
    return [value] + [step(value, axis, by) for by in (1, -1, 2)]


def copied(sources, shapes, moves):
    def kernel(*refs):
        inputs, (*outputs, sems) = refs[: len(sources)], refs[len(sources) :]
        copies = [
            pltpu.make_async_copy(
                inputs[source].at[pl.ds(from_row, rows), :], outputs[result].at[pl.ds(to_row, rows), :], sems.at[number]
            )
            for number, (source, from_row, result, to_row, rows) in enumerate(moves)
        ]
        for copy in copies:
            copy.start()
        for copy in copies:
            copy.wait()

    return pl.pallas_call(
        kernel,
        in_specs=[pl.BlockSpec(memory_space=pl.ANY)] * len(sources),
        out_specs=[pl.BlockSpec(memory_space=pltpu.VMEM)] * len(shapes),
        out_shape=[jax.ShapeDtypeStruct(shape, sources[0].dtype) for shape in shapes],
        scratch_shapes=[pltpu.SemaphoreType.DMA((len(moves),))],
        compiler_params=pltpu.CompilerParams(vmem_limit_bytes=8 << 20),
        cost_estimate=pl.CostEstimate(flops=1 << 10, bytes_accessed=1 << 10, transcendentals=0),
    )(*sources)


def joined(rings, starts, rows, extra=None):
    sources, shapes, moves = [], [], []
    for result, (pieces, start) in enumerate(zip(rings, starts)):
        half = rows // 2
        shapes.append((len(pieces) * rows, pieces[0].shape[1]))
        for number, piece in enumerate(pieces):
            for which in range(2):
                to_row = (which * len(pieces) + number) * half
                moves.append((len(sources) + number, start + which * half, result, to_row, half))
        sources += pieces
    if extra is not None:
        height, width = shapes[-1]
        shapes[-1] = (height + extra.shape[0], width)
        moves.append((len(sources), 0, len(shapes) - 1, height, extra.shape[0]))
        sources.append(extra)
    return copied(sources, shapes, moves)


def half_gelu(half):
    square = half * half
    total = jnp.full_like(square, ERF_Q[-1] * 4.0 ** (len(ERF_Q) - 1) * 2)
    for power in range(len(ERF_Q) - 2, -1, -1):
        total = total * square + ERF_Q[power] * 4.0**power * 2
    return half * jnp.tanh(half * total) + half


def pool(docs, both, first, last, total):
    def window(start):
        start = pl.multiple_of(start, 8)
        lane = lax.broadcasted_iota(jnp.int32, docs.shape, 1)
        mask = jnp.concatenate(
            [(docs == lane + (start + part)).astype(jnp.bfloat16) for part in range(0, WINDOW, LANES)], axis=1
        )
        rows = pl.ds(start, WINDOW)
        total[rows, :] += lax.dot_general(
            jnp.concatenate([mask, mask], axis=0),
            both,
            (((0,), (0,)), ((), ())),
            preferred_element_type=jnp.float32,
        )

    window(first)

    @pl.when(last >= first + WINDOW)
    def _():
        lax.fori_loop(
            1, lax.div(last - first, WINDOW) + 1, lambda number, carry: (window(first + number * WINDOW), carry)[1], 0
        )


def split(values):
    high = values.astype(jnp.bfloat16)
    return jnp.concatenate([high, (values - high.astype(jnp.float32)).astype(jnp.bfloat16)], axis=0)


def compressed(keys, docs_of, used):
    rows = keys.shape[0]
    kept = (keys < NONE) & (docs_of < used)
    ones = kept.astype(jnp.bfloat16)
    row, lane = (lax.broadcasted_iota(jnp.int32, (LANES, LANES), axis) for axis in range(2))
    before = jnp.dot(ones, (row < lane).astype(jnp.bfloat16), preferred_element_type=jnp.float32)
    whole = jnp.dot(ones, jnp.ones((LANES, LANES), jnp.bfloat16), preferred_element_type=jnp.float32)
    row, lane = (lax.broadcasted_iota(jnp.int32, (rows, rows), axis) for axis in range(2))
    above = (lane < row).astype(jnp.bfloat16)
    before += jnp.dot(above, whole.astype(jnp.bfloat16), preferred_element_type=jnp.float32)
    row, lane = (lax.broadcasted_iota(jnp.int32, keys.shape, axis) for axis in range(2))
    moves = jnp.where(kept, row * LANES + lane - before.astype(jnp.int32), 0)
    keys = jnp.where(kept, keys, NONE)
    for bit in range((rows * LANES - 1).bit_length()):
        step_by = 1 << bit

        def after(values):
            if step_by >= LANES:
                return pltpu.roll(values, rows - step_by // LANES, 0)
            values = pltpu.roll(values, LANES - step_by, 1)
            return jnp.where(lane < LANES - step_by, values, pltpu.roll(values, rows - 1, 0))

        next_moves, next_keys = after(moves), after(keys)
        comes, goes = (next_moves & step_by) != 0, (moves & step_by) != 0
        keys = jnp.where(comes, next_keys, jnp.where(goes, NONE, keys))
        moves = jnp.where(comes, next_moves, jnp.where(goes, 0, moves))
    return keys, jnp.sum(ones.astype(jnp.float32), axis=0, keepdims=True)


def prepare(place, own_ids, other_ids, own_lengths, other_lengths, table_all, positions, x_out, docs_out, bounds, normed_out, *scratch):
    total, rows32, table32, table, list_buffer, listed, sem, table_sem = scratch
    width = table.shape[1]
    pieces = width // LANES
    table_copy = pltpu.make_async_copy(table_all, table, table_sem)
    table_copy.start()

    def load():
        total[...] = jnp.zeros_like(total)

        def widen(group, carry):
            values = table[pl.ds(pl.multiple_of(group * 16, 16), 16), :].astype(jnp.float32)
            for eight in range(2):
                for piece in range(pieces):
                    at = pl.multiple_of((group * 2 + eight) * 8 * pieces + piece * 8, 8)
                    table32[pl.ds(at, 8), :] = values[eight * 8 : eight * 8 + 8, piece * LANES : (piece + 1) * LANES]
            return carry

        row, lane = (lax.broadcasted_iota(jnp.int32, (LANES, LANES), axis) for axis in range(2))
        of_doc = (row == lane >> SEQ_BITS).astype(jnp.bfloat16)
        used = []
        for lengths in (own_lengths, other_lengths):
            for half in range(2):
                columns = slice(half * LANES, (half + 1) * LANES)
                around = [
                    jnp.dot(lengths[16 * number : 16 * number + 16, columns], of_doc, preferred_element_type=jnp.float32)
                    for number in range(4)
                ]
                for y in range(4):
                    away = (y - place[1]) & 3
                    value = around[0]
                    for by, number in ((3, 1), (1, 2), (2, 3)):
                        value = jnp.where(away == by, around[number], value)
                    used.append(value)
        used = jnp.concatenate(used, axis=0).astype(jnp.int32)
        ids = jnp.concatenate([own_ids[...], other_ids[...]], axis=0)
        row, lane = (lax.broadcasted_iota(jnp.int32, ids.shape, axis) for axis in range(2))
        own_row = ids - place[0]
        doc = (row >> 4) * (12 * 8) + (row & 15) * 8 + (lane >> SEQ_BITS)
        time = lane & (SEQ - 1)
        keys = (doc << 19) + (time << 15) + (own_row >> 3) * 64 + (own_row & 7)
        inside = (own_row >= 0) & (own_row < table.shape[0]) & ((row & 15) < 12)
        keys, sums = compressed(jnp.where(inside, keys, NONE), time, used)
        most = listed.shape[0] - 8
        list_buffer[pl.ds(0, most), :] = keys[:most]
        count = jnp.sum(sums, axis=1, keepdims=True).astype(jnp.int32)
        list_buffer[pl.ds(most, 8), :] = jnp.broadcast_to(count, (8, LANES))
        copy = pltpu.make_async_copy(list_buffer, listed, sem)
        copy.start()
        table_copy.wait()
        lax.fori_loop(0, table.shape[0] // 16, widen, 0)
        copy.wait()
        return listed[most, 0]

    end = load()
    tiles = jnp.maximum((end + TILE - 1) >> TILE_BITS, 1)
    own = total.shape[0] - WINDOW
    bounds[BOUNDS - 1] = tiles

    def tile(x_ref, docs_ref):
        index = pl.program_id(0)
        first = index * TILE

        def key_at(slot):
            return listed[slot >> 7, slot & (LANES - 1)]

        for half in range(TILE // LANES):

            def take(group, carry, half=half):
                for one in range(8):
                    key = listed[TILE // LANES * index + half, group * 8 + one]
                    at = key & 0x7FFF
                    when = pl.multiple_of((key >> 12) & 0x78, 8)
                    value = table32[pl.ds(at, pieces, stride=8), :] + positions[pl.ds(when, pieces), :]
                    rows32[pl.ds((half * 16 + group) * 8 * pieces + one, pieces, stride=8), :] = value
                    docs_ref[pl.ds((half * 16 + group) * 8 + one, 1), :] = jnp.full((1, LANES), key >> 19, jnp.int32)
                return carry

            lax.fori_loop(0, LANES // 8, take, 0, unroll=True)
        normed = []
        for sub in range(TILE // SUB):
            block = rows32[pl.ds(sub * SUB * pieces, SUB * pieces), :].reshape(SUB // 8, pieces, 8, LANES)
            values = jnp.concatenate([block[:, piece].reshape(SUB, LANES) for piece in range(pieces)], axis=1)
            mean = jnp.mean(values, axis=-1, keepdims=True)
            centred = values - mean
            var = jnp.mean(centred * centred, axis=-1, keepdims=True)
            normal = centred * lax.rsqrt(var + 1e-05)
            x_ref[pl.ds(sub * SUB, SUB), :] = (normal * 0.5).astype(jnp.bfloat16)
            normed.append(normal)
        low = jnp.minimum((key_at(first) >> 22) << 3, 2 * own - 8)
        high = jnp.minimum(key_at(jnp.clip(end - 1, first, first + TILE - 1)) >> 19, 2 * own - 1)
        bounds[2 * index] = low
        bounds[2 * index + 1] = high

        @pl.when(low < own)
        def _():
            pool(docs_ref[...], split(jnp.concatenate(normed, axis=0)), low, jnp.minimum(high, own - 1), total)

    pltpu.emit_pipeline(
        tile,
        grid=(tiles,),
        in_specs=[],
        out_specs=[
            pl.BlockSpec((TILE, width), lambda i: (i, 0)),
            pl.BlockSpec((TILE, LANES), lambda i: (i, 0)),
        ],
    )(x_out, docs_out)
    copy = pltpu.make_async_copy(total.at[pl.ds(0, own), :], normed_out, sem)
    copy.start()
    copy.wait()


def run_prepare(place, ids, other_ids, lengths, other_lengths, embed_table, positions, group, most):
    seq, width = positions.shape
    vocab_rows = embed_table.shape[0]
    pieces = width // LANES
    smem, vmem, hbm = (pl.BlockSpec(memory_space=space) for space in (pltpu.SMEM, pltpu.VMEM, pltpu.HBM))
    return pl.pallas_call(
        prepare,
        in_specs=[smem] + [vmem] * 4 + [hbm, vmem],
        out_specs=[hbm, hbm, smem, hbm],
        out_shape=[
            jax.ShapeDtypeStruct((most, width), jnp.bfloat16),
            jax.ShapeDtypeStruct((most, LANES), jnp.int32),
            jax.ShapeDtypeStruct((BOUNDS,), jnp.int32),
            jax.ShapeDtypeStruct((group, width), jnp.float32),
        ],
        scratch_shapes=[
            pltpu.VMEM((group + WINDOW, width), jnp.float32),
            pltpu.VMEM((TILE * pieces, LANES), jnp.float32),
            pltpu.VMEM((vocab_rows * pieces, LANES), jnp.float32),
            pltpu.VMEM((vocab_rows, width), jnp.bfloat16),
            pltpu.VMEM((most // LANES + 8, LANES), jnp.int32),
            pltpu.SMEM((most // LANES + 8, LANES), jnp.int32),
            pltpu.SemaphoreType.DMA,
            pltpu.SemaphoreType.DMA,
        ],
        compiler_params=pltpu.CompilerParams(vmem_limit_bytes=52 << 20),
        cost_estimate=pl.CostEstimate(flops=1 << 30, bytes_accessed=1 << 20, transcendentals=0),
    )(place, ids, other_ids, lengths, other_lengths, embed_table, positions.astype(jnp.float32).reshape(seq * pieces, LANES))


def over_tiles(tiles, several):
    def pair(number, carry):
        several(number * 2, 2)
        return carry

    lax.fori_loop(0, tiles >> 1, pair, 0)

    @pl.when((tiles & 1) == 1)
    def _():
        several(tiles - 1, 1)


def rows_of(tile, count):
    return pl.ds(pl.multiple_of(tile * TILE, TILE), count * TILE)


def load_pairs(tiles, loads):
    def copies(tile, slot):
        return [
            pltpu.make_async_copy(whole.at[rows_of(tile, 2), :], place.at[slot], sems.at[slot])
            for whole, place, sems in loads
        ]

    for copy in copies(0, 0):
        copy.start()

    def ready(tile):
        slot = (tile >> 1) & 1

        @pl.when(tile + 2 < tiles)
        def _():
            for copy in copies(tile + 2, 1 - slot):
                copy.start()

        for copy in copies(tile, slot):
            copy.wait()
        return slot

    return ready


def activate(inputs, w_in, hidden, first, staged):
    rows = pl.ds(0, inputs.shape[0])
    steps = w_in.shape[0] // CHUNK
    for number in range(steps + 1):
        if number < steps:
            weights = w_in[pl.ds(number * CHUNK, CHUNK), :]
            staged[number % 2, rows, :] = lax.dot_general(
                inputs[...], weights, (((1,), (1,)), ((), ())), preferred_element_type=jnp.float32
            )
        if number > 0:
            columns = pl.ds(first + (number - 1) * CHUNK, CHUNK)
            hidden[rows, columns] = half_gelu(staged[(number - 1) % 2, rows, :]).astype(jnp.bfloat16)


def load_units(pieces, w_in, w_out, sems):
    units = pieces[0].shape[0] // 2
    copies = []
    for number, piece in enumerate(pieces):
        for which, whole in enumerate((w_in, w_out)):
            part = piece.at[pl.ds(which * units, units), :]
            place = whole.at[pl.ds(number * units, units), :]
            copies.append(pltpu.make_async_copy(part, place, sems.at[2 * number + which]))
    for copy in copies:
        copy.start()
    return copies


def first_units(near, bounds, x_all, *refs):
    pieces, (out, x, w_in, w_out, hidden, staged, sums, w_sems, x_sems, out_sems) = refs[:near], refs[near:]
    tiles = bounds[BOUNDS - 1]
    copies = load_units(pieces, w_in, w_out, w_sems)
    ready = load_pairs(tiles, [(x_all, x, x_sems)])
    for copy in copies:
        copy.wait()

    def store(tile, slot):
        return pltpu.make_async_copy(sums.at[slot], out.at[rows_of(tile, 2), :], out_sems.at[slot])

    def several(tile, count):
        slot = ready(tile)

        @pl.when(tile >= 4)
        def _():
            store(tile - 4, slot).wait()

        rows = pl.ds(0, count * TILE)
        activate(x.at[slot, rows, :], w_in, hidden, 0, staged)
        sums[slot, rows, :] = jnp.dot(hidden[rows, :], w_out[...], preferred_element_type=jnp.float32)
        store(tile, slot).start()

    over_tiles(tiles, several)
    last = ((tiles + 1) >> 1) * 2 - 2

    @pl.when(last >= 2)
    def _():
        store(last - 2, 1 - ((last >> 1) & 1)).wait()

    store(last, (last >> 1) & 1).wait()


def second_units(far, bounds, x_all, docs_all, normed, sums_all, *refs):
    pieces, refs = refs[:far], refs[far:]
    own, other, total, x, docs, w_in, w_out, hidden, staged, sums, w_sems, x_sems, docs_sems, sums_sems, ends = refs
    tiles = bounds[BOUNDS - 1]
    group = own.shape[0]
    copies = load_units(pieces, w_in, w_out, w_sems)
    copies.append(pltpu.make_async_copy(normed, total.at[pl.ds(0, group), :], ends.at[0]))
    copies[-1].start()
    ready = load_pairs(tiles, [(x_all, x, x_sems), (docs_all, docs, docs_sems), (sums_all, sums, sums_sems)])
    rest = total.shape[0] - group
    total[pl.ds(group, rest), :] = jnp.zeros((rest, total.shape[1]), jnp.float32)
    for copy in copies:
        copy.wait()

    def several(tile, count):
        slot = ready(tile)
        rows = pl.ds(0, count * TILE)
        activate(x.at[slot, rows, :], w_in, hidden, 0, staged)
        branch = sums[slot, rows, :] + jnp.dot(hidden[rows, :], w_out[...], preferred_element_type=jnp.float32)
        for one in range(count):
            part = slice(one * TILE, (one + 1) * TILE)
            pool(docs[slot, part, :], split(branch[part]), bounds[2 * (tile + one)], bounds[2 * (tile + one) + 1], total)

    over_tiles(tiles, several)
    copies = [
        pltpu.make_async_copy(total.at[pl.ds(0, group), :], own, ends.at[0]),
        pltpu.make_async_copy(total.at[pl.ds(group, group), :], other, ends.at[1]),
    ]
    for copy in copies:
        copy.start()
    for copy in copies:
        copy.wait()


def run_first(near, bounds, x):
    most, width = x.shape
    units = len(near) * near[0].shape[0] // 2
    smem, hbm, anywhere = (pl.BlockSpec(memory_space=space) for space in (pltpu.SMEM, pltpu.HBM, pl.ANY))
    return pl.pallas_call(
        functools.partial(first_units, len(near)),
        in_specs=[smem, hbm] + [anywhere] * len(near),
        out_specs=hbm,
        out_shape=jax.ShapeDtypeStruct((most, width), jnp.float32),
        scratch_shapes=[
            pltpu.VMEM((2, 2 * TILE, width), jnp.bfloat16),
            pltpu.VMEM((units, width), jnp.bfloat16),
            pltpu.VMEM((units, width), jnp.bfloat16),
            pltpu.VMEM((2 * TILE, units), jnp.bfloat16),
            pltpu.VMEM((2, 2 * TILE, CHUNK), jnp.float32),
            pltpu.VMEM((2, 2 * TILE, width), jnp.float32),
            pltpu.SemaphoreType.DMA((2 * len(near),)),
            pltpu.SemaphoreType.DMA((2,)),
            pltpu.SemaphoreType.DMA((2,)),
        ],
        compiler_params=pltpu.CompilerParams(vmem_limit_bytes=44 << 20),
        cost_estimate=pl.CostEstimate(flops=20 << 30, bytes_accessed=16 << 20, transcendentals=0),
    )(bounds, x, *near)


def run_second(far, bounds, x, docs, normed, sums):
    most, width = x.shape
    group = normed.shape[0]
    units = len(far) * far[0].shape[0] // 2
    smem, hbm, anywhere = (pl.BlockSpec(memory_space=space) for space in (pltpu.SMEM, pltpu.HBM, pl.ANY))
    return pl.pallas_call(
        functools.partial(second_units, len(far)),
        in_specs=[smem, hbm, hbm, anywhere, hbm] + [anywhere] * len(far),
        out_specs=[anywhere, anywhere],
        out_shape=[jax.ShapeDtypeStruct((group, width), jnp.float32)] * 2,
        scratch_shapes=[
            pltpu.VMEM((2 * group + WINDOW, width), jnp.float32),
            pltpu.VMEM((2, 2 * TILE, width), jnp.bfloat16),
            pltpu.VMEM((2, 2 * TILE, LANES), jnp.int32),
            pltpu.VMEM((units, width), jnp.bfloat16),
            pltpu.VMEM((units, width), jnp.bfloat16),
            pltpu.VMEM((2 * TILE, units), jnp.bfloat16),
            pltpu.VMEM((2, 2 * TILE, CHUNK), jnp.float32),
            pltpu.VMEM((2, 2 * TILE, width), jnp.float32),
            pltpu.SemaphoreType.DMA((2 * len(far),)),
            pltpu.SemaphoreType.DMA((2,)),
            pltpu.SemaphoreType.DMA((2,)),
            pltpu.SemaphoreType.DMA((2,)),
            pltpu.SemaphoreType.DMA((2,)),
        ],
        compiler_params=pltpu.CompilerParams(vmem_limit_bytes=36 << 20),
        cost_estimate=pl.CostEstimate(flops=12 << 30, bytes_accessed=24 << 20, transcendentals=0),
    )(bounds, x, docs, normed, sums, *far)


def local(token_ids, doc_lengths, clusters, embed_table, positions, w_in, w_out):
    doc_dev = doc_lengths.shape[0]
    group, seq = token_ids.shape
    vocab_rows, width = embed_table.shape
    n_col = group // doc_dev

    with jax.named_scope("weights"):
        half = w_in.shape[0] // 2
        mixed = jnp.concatenate([w_in[:half], w_out[:half], w_in[half:], w_out[half:]], axis=0)
        mixed, doc_lengths = lax.optimization_barrier((mixed, doc_lengths))
        by_z = ring(mixed, "z")
        lengths = jnp.pad(doc_lengths.reshape(doc_dev // 8, 8), ((0, 16 - doc_dev // 8), (0, LANES - 8))).astype(jnp.bfloat16)
        over = lax.ppermute(lengths, "x_hi", [(0, 1), (1, 0)])
        lower = lax.axis_index("x_hi") == 0
        lengths = jnp.concatenate([jnp.where(lower, lengths, over), jnp.where(lower, over, lengths)], axis=1)
        lengths = jnp.pad(lengths, ((0, 0), (0, width - 2 * LANES)))
        first, second = joined([by_z, by_z], [0, 2 * half], 2 * half, lengths)
        rows = first.shape[0]
        place = jnp.stack([lax.axis_index(COL) * vocab_rows, lax.axis_index("y")]).astype(jnp.int32)
        first, second = ring(first, X), ring(second, "y")
        first, second, token_ids = lax.optimization_barrier((first, second, token_ids))
        lengths = jnp.concatenate([piece[rows:, : 2 * LANES] for piece in second], axis=0)
        lengths = (lengths, step(lengths, "core", 1))
        ids = token_ids.reshape(n_col, doc_dev * seq // LANES, LANES)
        ids = jnp.pad(ids, ((0, 0), (0, 16 - ids.shape[1]), (0, 0))).reshape(n_col * 16, LANES)
        ids = (ids, step(ids, "core", 1))
        first, second = joined([first, second], [0, 0], rows)
        units = first.shape[0] // 2
        left, right = step(first, "y", 1), step(first, "y", -1)
        down, up = step(second, X, 1), step(second, X, -1)
        near = [first, left, right, second, down, up]

    with jax.named_scope("prepare"):
        most = 2 * n_col * SHARD_CAP
        x, docs, bounds, normed = run_prepare(place, *ids, *lengths, embed_table, positions, group, most)

    with jax.named_scope("forward"):
        near, x = lax.optimization_barrier((near, x))
        far = [step(near[0], "y", 2), step(near[3], X, 2)]
        sums = run_first(near, bounds, x)
        own, other = run_second(far, bounds, x, docs, normed, sums)

    with jax.named_scope("pooled"):
        sums = own + step(other, "core", 1)
        sums = sums.astype(jnp.bfloat16).reshape(n_col, doc_dev, width)
        sums = lax.all_to_all(sums, COL, 0, 0, tiled=True)
        pooled = jnp.sum(sums.astype(jnp.float32), axis=0) / doc_lengths.astype(jnp.float32)[:, None]
        scale = lax.rsqrt(jnp.sum(pooled * pooled, axis=-1, keepdims=True) + 1e-06)
        embedding = (pooled * scale).astype(jnp.bfloat16)

    with jax.named_scope("match"):
        n_clusters = lax.axis_size(CHIPS)
        labels = clusters[:, 0]
        same = labels[:, None] == labels[None, :]
        order = jnp.arange(doc_dev, dtype=jnp.int32)
        rank = jnp.sum((same & (order[:, None] > order[None, :])).astype(jnp.int32), axis=1)
        slot = labels * 4 + rank
        chosen = slot[None, :] == jnp.arange(n_clusters * 4, dtype=jnp.int32)[:, None]
        sizes = jnp.sum((labels[None, :] == jnp.arange(n_clusters)[:, None]).astype(jnp.int32), axis=1)
        fourth = lax.broadcasted_iota(jnp.int32, (n_clusters, 4, width), 1) == 3
        flags = lax.broadcasted_iota(jnp.int32, (n_clusters, 4, width), 2) < sizes[:, None, None]
        outgoing = jnp.dot(chosen.astype(jnp.bfloat16), embedding, preferred_element_type=jnp.float32)
        outgoing = jnp.where(
            fourth, flags.astype(jnp.float32), outgoing.reshape(n_clusters, 4, width)
        ).astype(jnp.bfloat16)
        members = lax.all_to_all(outgoing, CHIPS, 0, 0, tiled=True)
        others = step(members, "core", 1)
        every = jnp.concatenate([members, others], axis=0)
        filled = jnp.pad(every[:, 3, :3], ((0, 0), (0, 1))).reshape(-1) > 0.5
        count = n_clusters * 4
        scores = jnp.dot(
            members.reshape(count, width), every.reshape(2 * count, width).T, preferred_element_type=jnp.float32
        )
        own = jnp.arange(count)[:, None] == jnp.arange(2 * count)[None, :]
        best = jnp.max(jnp.where(filled[None, :] & jnp.logical_not(own), scores, -1.0), axis=1)
        best = jnp.maximum(best, -1.0)
        returned = lax.all_to_all(best.reshape(n_clusters, 4), CHIPS, 0, 0, tiled=True).reshape(-1)
        return jnp.sum(jnp.where(chosen, returned[:, None], 0.0), axis=0)


def solution(mesh):
    fine = Mesh(mesh.devices.reshape(2, 4, 2, 2, 4), ("x_lo", "z", "core", "x_hi", "y"))
    everywhere = OWN + COL
    return jax.shard_map(
        local,
        mesh=fine,
        in_specs=(
            P(OWN, None),
            P(everywhere),
            P(everywhere, None),
            P(COL, None),
            P(),
            P(everywhere, None),
            P(everywhere, None),
        ),
        out_specs=P(everywhere),
        check_vma=False,
    )
```

```python
import functools

import jax
import jax.numpy as jnp
from jax import lax
from jax.experimental import pallas as pl
from jax.experimental.pallas import tpu as pltpu
from jax.sharding import Mesh
from jax.sharding import PartitionSpec as P

OWN = ("x_lo", "z", "core")
COL = ("x_hi", "y")
X = ("x_lo", "x_hi")
CHIPS = ("x_lo", "z", "x_hi", "y")
SHARD_CAP = 384
TILE_BITS = 8
TILE = 1 << TILE_BITS
LANES = 128
SUB = 64
SEQ_BITS = 4
SEQ = 1 << SEQ_BITS
NONE = 1 << 30
BOUNDS = 64
CHUNK = 256
WINDOW = 384
LIMIT = 5.4 * 5.4
ERF_Q = (
    0.7978853416207131,
    0.03633264203955081,
    -3.271896418592583e-05,
    -5.512179284196367e-05,
    3.917683168513537e-06,
    -1.2794852180568973e-07,
    1.6281616374933989e-09,
)


def step(value, axis, by):
    count = 2 if axis == "core" else 4
    place = (lambda x: (x % 2) * 2 + x // 2) if axis == X else (lambda x: x)
    return lax.ppermute(value, axis, [(place(i), place((i + by) % count)) for i in range(count)])


def ring(value, axis):
    return [value] + [step(value, axis, by) for by in (1, -1, 2)]


def copied(sources, shapes, moves):
    def kernel(*refs):
        inputs, outputs = refs[: len(sources)], refs[len(sources) :]
        for source, from_row, result, to_row, rows in moves:
            outputs[result][to_row : to_row + rows, :] = inputs[source][from_row : from_row + rows, :]

    vmem = pl.BlockSpec(memory_space=pltpu.VMEM)
    return pl.pallas_call(
        kernel,
        in_specs=[vmem] * len(sources),
        out_specs=[vmem] * len(shapes),
        out_shape=[jax.ShapeDtypeStruct(shape, sources[0].dtype) for shape in shapes],
        compiler_params=pltpu.CompilerParams(vmem_limit_bytes=8 << 20),
        cost_estimate=pl.CostEstimate(flops=1 << 10, bytes_accessed=1 << 10, transcendentals=0),
    )(*sources)


def joined(rings, starts, rows, extra=None):
    sources, shapes, moves = [], [], []
    for result, (pieces, start) in enumerate(zip(rings, starts)):
        half = rows // 2
        shapes.append((len(pieces) * rows, pieces[0].shape[1]))
        for number, piece in enumerate(pieces):
            for which in range(2):
                to_row = (which * len(pieces) + number) * half
                moves.append((len(sources) + number, start + which * half, result, to_row, half))
        sources += pieces
    if extra is not None:
        height, width = shapes[-1]
        shapes[-1] = (height + extra.shape[0], width)
        moves.append((len(sources), 0, len(shapes) - 1, height, extra.shape[0]))
        sources.append(extra)
    return copied(sources, shapes, moves)


def with_lengths(ids, pieces):
    def kernel(ids_ref, *refs):
        pieces, out = refs[:-1], refs[-1]
        out[: ids_ref.shape[0], :] = ids_ref[...]
        for half in range(2):
            for number, piece in enumerate(pieces):
                at = ids_ref.shape[0] + (half * len(pieces) + number) * 16
                part = piece[piece.shape[0] - 16 :, half * LANES : (half + 1) * LANES]
                out[at : at + 16, :] = part.astype(jnp.float32).astype(jnp.int32)

    vmem = pl.BlockSpec(memory_space=pltpu.VMEM)
    return pl.pallas_call(
        kernel,
        in_specs=[vmem] * (1 + len(pieces)),
        out_specs=vmem,
        out_shape=jax.ShapeDtypeStruct((ids.shape[0] + 32 * len(pieces), LANES), jnp.int32),
        compiler_params=pltpu.CompilerParams(vmem_limit_bytes=4 << 20),
        cost_estimate=pl.CostEstimate(flops=1 << 10, bytes_accessed=1 << 10, transcendentals=0),
    )(ids, *pieces)


def half_gelu(half):
    square = half * half
    total = jnp.full_like(square, ERF_Q[-1] * 4.0 ** (len(ERF_Q) - 1) * 2)
    for power in range(len(ERF_Q) - 2, -1, -1):
        total = total * square + ERF_Q[power] * 4.0**power * 2
    return half * jnp.tanh(half * total) + half


def pool(docs, both, first, last, total):
    def window(start):
        start = pl.multiple_of(start, 8)
        lane = lax.broadcasted_iota(jnp.int32, docs.shape, 1)
        mask = jnp.concatenate(
            [(docs == lane + (start + part)).astype(jnp.bfloat16) for part in range(0, WINDOW, LANES)], axis=1
        )
        rows = pl.ds(start, WINDOW)
        total[rows, :] += lax.dot_general(
            jnp.concatenate([mask, mask], axis=0),
            both,
            (((0,), (0,)), ((), ())),
            preferred_element_type=jnp.float32,
        )

    window(first)

    @pl.when(last >= first + WINDOW)
    def _():
        lax.fori_loop(
            1, lax.div(last - first, WINDOW) + 1, lambda number, carry: (window(first + number * WINDOW), carry)[1], 0
        )


def split(values):
    high = values.astype(jnp.bfloat16)
    return jnp.concatenate([high, (values - high.astype(jnp.float32)).astype(jnp.bfloat16)], axis=0)


def compressed(keys, docs_of, used):
    rows = keys.shape[0]
    kept = (keys < NONE) & (docs_of < used)
    ones = kept.astype(jnp.bfloat16)
    row, lane = (lax.broadcasted_iota(jnp.int32, (LANES, LANES), axis) for axis in range(2))
    before = jnp.dot(ones, (row < lane).astype(jnp.bfloat16), preferred_element_type=jnp.float32)
    whole = jnp.dot(ones, jnp.ones((LANES, LANES), jnp.bfloat16), preferred_element_type=jnp.float32)
    row, lane = (lax.broadcasted_iota(jnp.int32, (rows, rows), axis) for axis in range(2))
    above = (lane < row).astype(jnp.bfloat16)
    before += jnp.dot(above, whole.astype(jnp.bfloat16), preferred_element_type=jnp.float32)
    row, lane = (lax.broadcasted_iota(jnp.int32, keys.shape, axis) for axis in range(2))
    moves = jnp.where(kept, row * LANES + lane - before.astype(jnp.int32), 0)
    keys = jnp.where(kept, keys, NONE)
    for bit in range((rows * LANES - 1).bit_length()):
        step_by = 1 << bit

        def after(values):
            if step_by >= LANES:
                return pltpu.roll(values, rows - step_by // LANES, 0)
            values = pltpu.roll(values, LANES - step_by, 1)
            return jnp.where(lane < LANES - step_by, values, pltpu.roll(values, rows - 1, 0))

        next_moves, next_keys = after(moves), after(keys)
        comes, goes = (next_moves & step_by) != 0, (moves & step_by) != 0
        keys = jnp.where(comes, next_keys, jnp.where(goes, NONE, keys))
        moves = jnp.where(comes, next_moves, jnp.where(goes, 0, moves))
    return keys, jnp.sum(ones.astype(jnp.float32), axis=0, keepdims=True)


def prepare(place, own_ids, other_ids, table_all, positions, x_out, docs_out, bounds, normed_out, *scratch):
    total, rows32, table32, table, list_buffer, listed, sem, table_sem = scratch
    width = table.shape[1]
    pieces = width // LANES
    table_copy = pltpu.make_async_copy(table_all, table, table_sem)
    table_copy.start()

    def load():
        total[...] = jnp.zeros_like(total)

        def widen(group, carry):
            values = table[pl.ds(pl.multiple_of(group * 16, 16), 16), :].astype(jnp.float32)
            for eight in range(2):
                for piece in range(pieces):
                    at = pl.multiple_of((group * 2 + eight) * 8 * pieces + piece * 8, 8)
                    table32[pl.ds(at, 8), :] = values[eight * 8 : eight * 8 + 8, piece * LANES : (piece + 1) * LANES]
            return carry

        row, lane = (lax.broadcasted_iota(jnp.int32, (LANES, LANES), axis) for axis in range(2))
        of_doc = (row == lane >> SEQ_BITS).astype(jnp.bfloat16)
        used = []
        half_rows = own_ids.shape[0] // 2
        for tokens in (own_ids, other_ids):
            for half in range(2):
                around = []
                for number in range(4):
                    at = half_rows + (half * 4 + number) * 16
                    lengths = tokens[at : at + 16, :].astype(jnp.float32).astype(jnp.bfloat16)
                    around.append(jnp.dot(lengths, of_doc, preferred_element_type=jnp.float32))
                for y in range(4):
                    away = (y - place[1]) & 3
                    value = around[0]
                    for by, number in ((3, 1), (1, 2), (2, 3)):
                        value = jnp.where(away == by, around[number], value)
                    used.append(value)
        used = jnp.concatenate(used, axis=0).astype(jnp.int32)
        ids = jnp.concatenate([own_ids[:half_rows, :], other_ids[:half_rows, :]], axis=0)
        row, lane = (lax.broadcasted_iota(jnp.int32, ids.shape, axis) for axis in range(2))
        own_row = ids - place[0]
        doc = (row >> 4) * (12 * 8) + (row & 15) * 8 + (lane >> SEQ_BITS)
        time = lane & (SEQ - 1)
        keys = (doc << 19) + (time << 15) + (own_row >> 3) * 64 + (own_row & 7)
        inside = (own_row >= 0) & (own_row < table.shape[0]) & ((row & 15) < 12)
        keys, sums = compressed(jnp.where(inside, keys, NONE), time, used)
        most = listed.shape[0] - 8
        list_buffer[pl.ds(0, most), :] = keys[:most]
        count = jnp.sum(sums, axis=1, keepdims=True).astype(jnp.int32)
        list_buffer[pl.ds(most, 8), :] = jnp.broadcast_to(count, (8, LANES))
        copy = pltpu.make_async_copy(list_buffer, listed, sem)
        copy.start()
        table_copy.wait()
        lax.fori_loop(0, table.shape[0] // 16, widen, 0)
        copy.wait()
        return listed[most, 0]

    end = load()
    tiles = jnp.maximum((end + TILE - 1) >> TILE_BITS, 1)
    own = total.shape[0] - WINDOW
    bounds[BOUNDS - 1] = tiles

    def tile(x_ref, docs_ref):
        index = pl.program_id(0)
        first = index * TILE

        def key_at(slot):
            return listed[slot >> 7, slot & (LANES - 1)]

        for half in range(TILE // LANES):

            def take(group, carry, half=half):
                for one in range(8):
                    key = listed[TILE // LANES * index + half, group * 8 + one]
                    at = key & 0x7FFF
                    when = pl.multiple_of((key >> 12) & 0x78, 8)
                    value = table32[pl.ds(at, pieces, stride=8), :] + positions[pl.ds(when, pieces), :]
                    rows32[pl.ds((half * 16 + group) * 8 * pieces + one, pieces, stride=8), :] = value
                    docs_ref[pl.ds((half * 16 + group) * 8 + one, 1), :] = jnp.full((1, LANES), key >> 19, jnp.int32)
                return carry

            lax.fori_loop(0, LANES // 8, take, 0, unroll=True)
        normed = []
        for sub in range(TILE // SUB):
            block = rows32[pl.ds(sub * SUB * pieces, SUB * pieces), :].reshape(SUB // 8, pieces, 8, LANES)
            values = jnp.concatenate([block[:, piece].reshape(SUB, LANES) for piece in range(pieces)], axis=1)
            mean = jnp.mean(values, axis=-1, keepdims=True)
            centred = values - mean
            var = jnp.mean(centred * centred, axis=-1, keepdims=True)
            normal = centred * lax.rsqrt(var + 1e-05)
            x_ref[pl.ds(sub * SUB, SUB), :] = (normal * 0.5).astype(jnp.bfloat16)
            normed.append(normal)
        low = jnp.minimum((key_at(first) >> 22) << 3, 2 * own - 8)
        high = jnp.minimum(key_at(jnp.clip(end - 1, first, first + TILE - 1)) >> 19, 2 * own - 1)
        bounds[2 * index] = low
        bounds[2 * index + 1] = high

        @pl.when(low < own)
        def _():
            pool(docs_ref[...], split(jnp.concatenate(normed, axis=0)), low, jnp.minimum(high, own - 1), total)

    pltpu.emit_pipeline(
        tile,
        grid=(tiles,),
        in_specs=[],
        out_specs=[
            pl.BlockSpec((TILE, width), lambda i: (i, 0)),
            pl.BlockSpec((TILE, LANES), lambda i: (i, 0)),
        ],
    )(x_out, docs_out)
    copy = pltpu.make_async_copy(total.at[pl.ds(0, own), :], normed_out, sem)
    copy.start()
    copy.wait()


def run_prepare(place, own_ids, other_ids, embed_table, positions, group, most):
    seq, width = positions.shape
    vocab_rows = embed_table.shape[0]
    pieces = width // LANES
    smem, vmem, hbm = (pl.BlockSpec(memory_space=space) for space in (pltpu.SMEM, pltpu.VMEM, pltpu.HBM))
    return pl.pallas_call(
        prepare,
        in_specs=[smem, vmem, vmem, hbm, vmem],
        out_specs=[hbm, hbm, smem, hbm],
        out_shape=[
            jax.ShapeDtypeStruct((most, width), jnp.bfloat16),
            jax.ShapeDtypeStruct((most, LANES), jnp.int32),
            jax.ShapeDtypeStruct((BOUNDS,), jnp.int32),
            jax.ShapeDtypeStruct((group, width), jnp.float32),
        ],
        scratch_shapes=[
            pltpu.VMEM((group + WINDOW, width), jnp.float32),
            pltpu.VMEM((TILE * pieces, LANES), jnp.float32),
            pltpu.VMEM((vocab_rows * pieces, LANES), jnp.float32),
            pltpu.VMEM((vocab_rows, width), jnp.bfloat16),
            pltpu.VMEM((most // LANES + 8, LANES), jnp.int32),
            pltpu.SMEM((most // LANES + 8, LANES), jnp.int32),
            pltpu.SemaphoreType.DMA,
            pltpu.SemaphoreType.DMA,
        ],
        compiler_params=pltpu.CompilerParams(vmem_limit_bytes=52 << 20),
        cost_estimate=pl.CostEstimate(flops=1 << 30, bytes_accessed=1 << 20, transcendentals=0),
    )(place, own_ids, other_ids, embed_table, positions.astype(jnp.float32).reshape(seq * pieces, LANES))


def over_tiles(tiles, several):
    def pair(number, carry):
        several(number * 2, 2)
        return carry

    lax.fori_loop(0, tiles >> 1, pair, 0)

    @pl.when((tiles & 1) == 1)
    def _():
        several(tiles - 1, 1)


def rows_of(tile, count):
    return pl.ds(pl.multiple_of(tile * TILE, TILE), count * TILE)


def load_pairs(tiles, loads):
    def copies(tile, slot):
        return [
            pltpu.make_async_copy(whole.at[rows_of(tile, 2), :], place.at[slot], sems.at[slot])
            for whole, place, sems in loads
        ]

    for copy in copies(0, 0):
        copy.start()

    def ready(tile):
        slot = (tile >> 1) & 1

        @pl.when(tile + 2 < tiles)
        def _():
            for copy in copies(tile + 2, 1 - slot):
                copy.start()

        for copy in copies(tile, slot):
            copy.wait()
        return slot

    return ready


def activate(inputs, w_in, hidden, first, staged):
    rows = pl.ds(0, inputs.shape[0])
    steps = w_in.shape[0] // CHUNK
    for number in range(steps + 1):
        if number < steps:
            weights = w_in[pl.ds(number * CHUNK, CHUNK), :]
            staged[number % 2, rows, :] = lax.dot_general(
                inputs[...], weights, (((1,), (1,)), ((), ())), preferred_element_type=jnp.float32
            )
        if number > 0:
            columns = pl.ds(first + (number - 1) * CHUNK, CHUNK)
            hidden[rows, columns] = half_gelu(staged[(number - 1) % 2, rows, :]).astype(jnp.bfloat16)


def load_units(pieces, w_in, w_out, sems):
    units = pieces[0].shape[0] // 2
    copies = []
    for number, piece in enumerate(pieces):
        for which, whole in enumerate((w_in, w_out)):
            part = piece.at[pl.ds(which * units, units), :]
            place = whole.at[pl.ds(number * units, units), :]
            copies.append(pltpu.make_async_copy(part, place, sems.at[2 * number + which]))
    for copy in copies:
        copy.start()
    return copies


def first_units(near, bounds, x_all, *refs):
    pieces, (out, x, w_in, w_out, hidden, staged, sums, w_sems, x_sems, out_sems) = refs[:near], refs[near:]
    tiles = bounds[BOUNDS - 1]
    copies = load_units(pieces, w_in, w_out, w_sems)
    ready = load_pairs(tiles, [(x_all, x, x_sems)])
    for copy in copies:
        copy.wait()

    def store(tile, slot):
        return pltpu.make_async_copy(sums.at[slot], out.at[rows_of(tile, 2), :], out_sems.at[slot])

    def several(tile, count):
        slot = ready(tile)

        @pl.when(tile >= 4)
        def _():
            store(tile - 4, slot).wait()

        rows = pl.ds(0, count * TILE)
        activate(x.at[slot, rows, :], w_in, hidden, 0, staged)
        sums[slot, rows, :] = jnp.dot(hidden[rows, :], w_out[...], preferred_element_type=jnp.float32)
        store(tile, slot).start()

    over_tiles(tiles, several)
    last = ((tiles + 1) >> 1) * 2 - 2

    @pl.when(last >= 2)
    def _():
        store(last - 2, 1 - ((last >> 1) & 1)).wait()

    store(last, (last >> 1) & 1).wait()


def second_units(far, bounds, x_all, docs_all, normed, sums_all, *refs):
    pieces, refs = refs[:far], refs[far:]
    own, other, total, x, docs, w_in, w_out, hidden, staged, sums, w_sems, x_sems, docs_sems, sums_sems, ends = refs
    tiles = bounds[BOUNDS - 1]
    group = own.shape[0]
    copies = load_units(pieces, w_in, w_out, w_sems)
    copies.append(pltpu.make_async_copy(normed, total.at[pl.ds(0, group), :], ends.at[0]))
    copies[-1].start()
    ready = load_pairs(tiles, [(x_all, x, x_sems), (docs_all, docs, docs_sems), (sums_all, sums, sums_sems)])
    rest = total.shape[0] - group
    total[pl.ds(group, rest), :] = jnp.zeros((rest, total.shape[1]), jnp.float32)
    for copy in copies:
        copy.wait()

    def several(tile, count):
        slot = ready(tile)
        rows = pl.ds(0, count * TILE)
        activate(x.at[slot, rows, :], w_in, hidden, 0, staged)
        branch = sums[slot, rows, :] + jnp.dot(hidden[rows, :], w_out[...], preferred_element_type=jnp.float32)
        for one in range(count):
            part = slice(one * TILE, (one + 1) * TILE)
            pool(docs[slot, part, :], split(branch[part]), bounds[2 * (tile + one)], bounds[2 * (tile + one) + 1], total)

    over_tiles(tiles, several)
    copies = [
        pltpu.make_async_copy(total.at[pl.ds(0, group), :], own, ends.at[0]),
        pltpu.make_async_copy(total.at[pl.ds(group, group), :], other, ends.at[1]),
    ]
    for copy in copies:
        copy.start()
    for copy in copies:
        copy.wait()


def run_first(near, bounds, x):
    most, width = x.shape
    units = len(near) * near[0].shape[0] // 2
    smem, hbm, anywhere = (pl.BlockSpec(memory_space=space) for space in (pltpu.SMEM, pltpu.HBM, pl.ANY))
    return pl.pallas_call(
        functools.partial(first_units, len(near)),
        in_specs=[smem, hbm] + [anywhere] * len(near),
        out_specs=hbm,
        out_shape=jax.ShapeDtypeStruct((most, width), jnp.float32),
        scratch_shapes=[
            pltpu.VMEM((2, 2 * TILE, width), jnp.bfloat16),
            pltpu.VMEM((units, width), jnp.bfloat16),
            pltpu.VMEM((units, width), jnp.bfloat16),
            pltpu.VMEM((2 * TILE, units), jnp.bfloat16),
            pltpu.VMEM((2, 2 * TILE, CHUNK), jnp.float32),
            pltpu.VMEM((2, 2 * TILE, width), jnp.float32),
            pltpu.SemaphoreType.DMA((2 * len(near),)),
            pltpu.SemaphoreType.DMA((2,)),
            pltpu.SemaphoreType.DMA((2,)),
        ],
        compiler_params=pltpu.CompilerParams(vmem_limit_bytes=44 << 20),
        cost_estimate=pl.CostEstimate(flops=20 << 30, bytes_accessed=16 << 20, transcendentals=0),
    )(bounds, x, *near)


def run_second(far, bounds, x, docs, normed, sums):
    most, width = x.shape
    group = normed.shape[0]
    units = len(far) * far[0].shape[0] // 2
    smem, hbm, anywhere = (pl.BlockSpec(memory_space=space) for space in (pltpu.SMEM, pltpu.HBM, pl.ANY))
    return pl.pallas_call(
        functools.partial(second_units, len(far)),
        in_specs=[smem, hbm, hbm, anywhere, hbm] + [anywhere] * len(far),
        out_specs=[anywhere, anywhere],
        out_shape=[jax.ShapeDtypeStruct((group, width), jnp.float32)] * 2,
        scratch_shapes=[
            pltpu.VMEM((2 * group + WINDOW, width), jnp.float32),
            pltpu.VMEM((2, 2 * TILE, width), jnp.bfloat16),
            pltpu.VMEM((2, 2 * TILE, LANES), jnp.int32),
            pltpu.VMEM((units, width), jnp.bfloat16),
            pltpu.VMEM((units, width), jnp.bfloat16),
            pltpu.VMEM((2 * TILE, units), jnp.bfloat16),
            pltpu.VMEM((2, 2 * TILE, CHUNK), jnp.float32),
            pltpu.VMEM((2, 2 * TILE, width), jnp.float32),
            pltpu.SemaphoreType.DMA((2 * len(far),)),
            pltpu.SemaphoreType.DMA((2,)),
            pltpu.SemaphoreType.DMA((2,)),
            pltpu.SemaphoreType.DMA((2,)),
            pltpu.SemaphoreType.DMA((2,)),
        ],
        compiler_params=pltpu.CompilerParams(vmem_limit_bytes=36 << 20),
        cost_estimate=pl.CostEstimate(flops=12 << 30, bytes_accessed=24 << 20, transcendentals=0),
    )(bounds, x, docs, normed, sums, *far)


def local(token_ids, doc_lengths, clusters, embed_table, positions, w_in, w_out):
    doc_dev = doc_lengths.shape[0]
    group, seq = token_ids.shape
    vocab_rows, width = embed_table.shape
    n_col = group // doc_dev

    with jax.named_scope("weights"):
        half = w_in.shape[0] // 2
        mixed = jnp.concatenate([w_in[:half], w_out[:half], w_in[half:], w_out[half:]], axis=0)
        mixed, doc_lengths = lax.optimization_barrier((mixed, doc_lengths))
        by_z = ring(mixed, "z")
        lengths = jnp.pad(doc_lengths.reshape(doc_dev // 8, 8), ((0, 16 - doc_dev // 8), (0, LANES - 8))).astype(jnp.bfloat16)
        over = lax.ppermute(lengths, "x_hi", [(0, 1), (1, 0)])
        lower = lax.axis_index("x_hi") == 0
        lengths = jnp.concatenate([jnp.where(lower, lengths, over), jnp.where(lower, over, lengths)], axis=1)
        lengths = jnp.pad(lengths, ((0, 0), (0, width - 2 * LANES)))
        first, second = joined([by_z, by_z], [0, 2 * half], 2 * half, lengths)
        rows = first.shape[0]
        place = jnp.stack([lax.axis_index(COL) * vocab_rows, lax.axis_index("y")]).astype(jnp.int32)
        first, second = ring(first, X), ring(second, "y")
        first, second, token_ids = lax.optimization_barrier((first, second, token_ids))
        ids = token_ids.reshape(n_col, doc_dev * seq // LANES, LANES)
        ids = jnp.pad(ids, ((0, 0), (0, 16 - ids.shape[1]), (0, 0))).reshape(n_col * 16, LANES)
        own_ids = with_lengths(ids, second)
        other_ids = step(own_ids, "core", 1)
        first, second = joined([first, second], [0, 0], rows)
        units = first.shape[0] // 2
        left, right = step(first, "y", 1), step(first, "y", -1)
        down, up = step(second, X, 1), step(second, X, -1)
        near = [first, left, right, second, down, up]

    with jax.named_scope("prepare"):
        most = 2 * n_col * SHARD_CAP
        x, docs, bounds, normed = run_prepare(place, own_ids, other_ids, embed_table, positions, group, most)

    with jax.named_scope("forward"):
        near, x = lax.optimization_barrier((near, x))
        far = [step(near[0], "y", 2), step(near[3], X, 2)]
        sums = run_first(near, bounds, x)
        own, other = run_second(far, bounds, x, docs, normed, sums)

    with jax.named_scope("pooled"):
        sums = own + step(other, "core", 1)
        sums = sums.astype(jnp.bfloat16).reshape(n_col, doc_dev, width)
        sums = lax.all_to_all(sums, COL, 0, 0, tiled=True)
        pooled = jnp.sum(sums.astype(jnp.float32), axis=0) / doc_lengths.astype(jnp.float32)[:, None]
        scale = lax.rsqrt(jnp.sum(pooled * pooled, axis=-1, keepdims=True) + 1e-06)
        embedding = (pooled * scale).astype(jnp.bfloat16)

    with jax.named_scope("match"):
        n_clusters = lax.axis_size(CHIPS)
        labels = clusters[:, 0]
        same = labels[:, None] == labels[None, :]
        order = jnp.arange(doc_dev, dtype=jnp.int32)
        rank = jnp.sum((same & (order[:, None] > order[None, :])).astype(jnp.int32), axis=1)
        slot = labels * 4 + rank
        chosen = slot[None, :] == jnp.arange(n_clusters * 4, dtype=jnp.int32)[:, None]
        sizes = jnp.sum((labels[None, :] == jnp.arange(n_clusters)[:, None]).astype(jnp.int32), axis=1)
        fourth = lax.broadcasted_iota(jnp.int32, (n_clusters, 4, width), 1) == 3
        flags = lax.broadcasted_iota(jnp.int32, (n_clusters, 4, width), 2) < sizes[:, None, None]
        outgoing = jnp.dot(chosen.astype(jnp.bfloat16), embedding, preferred_element_type=jnp.float32)
        outgoing = jnp.where(
            fourth, flags.astype(jnp.float32), outgoing.reshape(n_clusters, 4, width)
        ).astype(jnp.bfloat16)
        members = lax.all_to_all(outgoing, CHIPS, 0, 0, tiled=True)
        others = step(members, "core", 1)
        every = jnp.concatenate([members, others], axis=0)
        filled = jnp.pad(every[:, 3, :3], ((0, 0), (0, 1))).reshape(-1) > 0.5
        count = n_clusters * 4
        scores = jnp.dot(
            members.reshape(count, width), every.reshape(2 * count, width).T, preferred_element_type=jnp.float32
        )
        own = jnp.arange(count)[:, None] == jnp.arange(2 * count)[None, :]
        best = jnp.max(jnp.where(filled[None, :] & jnp.logical_not(own), scores, -1.0), axis=1)
        best = jnp.maximum(best, -1.0)
        returned = lax.all_to_all(best.reshape(n_clusters, 4), CHIPS, 0, 0, tiled=True)
        of_cluster = (labels[:, None] == jnp.arange(n_clusters)[None, :]).astype(jnp.float32)
        rows = jnp.dot(of_cluster, returned, precision=lax.Precision.HIGHEST, preferred_element_type=jnp.float32)
        return jnp.sum(jnp.where(rank[:, None] == jnp.arange(4)[None, :], rows, 0.0), axis=1)


def solution(mesh):
    fine = Mesh(mesh.devices.reshape(2, 4, 2, 2, 4), ("x_lo", "z", "core", "x_hi", "y"))
    everywhere = OWN + COL
    return jax.shard_map(
        local,
        mesh=fine,
        in_specs=(
            P(OWN, None),
            P(everywhere),
            P(everywhere, None),
            P(COL, None),
            P(),
            P(everywhere, None),
            P(everywhere, None),
        ),
        out_specs=P(everywhere),
        check_vma=False,
    )
```

```python
import functools

import jax
import jax.numpy as jnp
from jax import lax
from jax.experimental import pallas as pl
from jax.experimental.pallas import tpu as pltpu
from jax.sharding import Mesh
from jax.sharding import PartitionSpec as P

OWN = ("x_lo", "z", "core")
COL = ("x_hi", "y")
X = ("x_lo", "x_hi")
CHIPS = ("x_lo", "z", "x_hi", "y")
SHARD_CAP = 384
TILE_BITS = 8
TILE = 1 << TILE_BITS
LANES = 128
SUB = 64
SEQ_BITS = 4
SEQ = 1 << SEQ_BITS
NONE = 1 << 30
BOUNDS = 64
CHUNK = 512
WINDOW = 384
ERF_Q = (
    0.7978853416207131,
    0.03633264203955081,
    -3.271896418592583e-05,
    -5.512179284196367e-05,
    3.917683168513537e-06,
    -1.2794852180568973e-07,
    1.6281616374933989e-09,
)


def step(value, axis, by):
    count = 2 if axis == "core" else 4
    place = (lambda x: (x % 2) * 2 + x // 2) if axis == X else (lambda x: x)
    return lax.ppermute(value, axis, [(place(i), place((i + by) % count)) for i in range(count)])


def ring(value, axis):
    return [value] + [step(value, axis, by) for by in (1, -1, 2)]


def copied(sources, shapes, moves):
    def kernel(*refs):
        inputs, outputs = refs[: len(sources)], refs[len(sources) :]
        for source, from_row, result, to_row, rows in moves:
            outputs[result][to_row : to_row + rows, :] = inputs[source][from_row : from_row + rows, :]

    vmem = pl.BlockSpec(memory_space=pltpu.VMEM)
    return pl.pallas_call(
        kernel,
        in_specs=[vmem] * len(sources),
        out_specs=[vmem] * len(shapes),
        out_shape=[jax.ShapeDtypeStruct(shape, sources[0].dtype) for shape in shapes],
        compiler_params=pltpu.CompilerParams(vmem_limit_bytes=8 << 20),
        cost_estimate=pl.CostEstimate(flops=1 << 10, bytes_accessed=1 << 10, transcendentals=0),
    )(*sources)


def joined(rings, starts, rows, extra=None):
    sources, shapes, moves = [], [], []
    for result, (pieces, start) in enumerate(zip(rings, starts)):
        half = rows // 2
        shapes.append((len(pieces) * rows, pieces[0].shape[1]))
        for number, piece in enumerate(pieces):
            for which in range(2):
                to_row = (which * len(pieces) + number) * half
                moves.append((len(sources) + number, start + which * half, result, to_row, half))
        sources += pieces
    if extra is not None:
        height, width = shapes[-1]
        shapes[-1] = (height + extra.shape[0], width)
        moves.append((len(sources), 0, len(shapes) - 1, height, extra.shape[0]))
        sources.append(extra)
    return copied(sources, shapes, moves)


def with_lengths(ids, pieces):
    def kernel(ids_ref, *refs):
        pieces, out = refs[:-1], refs[-1]
        out[: ids_ref.shape[0], :] = ids_ref[...]
        for half in range(2):
            for number, piece in enumerate(pieces):
                at = ids_ref.shape[0] + (half * len(pieces) + number) * 16
                part = piece[piece.shape[0] - 16 :, half * LANES : (half + 1) * LANES]
                out[at : at + 16, :] = part.astype(jnp.float32).astype(jnp.int32)

    vmem = pl.BlockSpec(memory_space=pltpu.VMEM)
    return pl.pallas_call(
        kernel,
        in_specs=[vmem] * (1 + len(pieces)),
        out_specs=vmem,
        out_shape=jax.ShapeDtypeStruct((ids.shape[0] + 32 * len(pieces), LANES), jnp.int32),
        compiler_params=pltpu.CompilerParams(vmem_limit_bytes=4 << 20),
        cost_estimate=pl.CostEstimate(flops=1 << 10, bytes_accessed=1 << 10, transcendentals=0),
    )(ids, *pieces)


def half_gelu(half):
    square = half * half
    total = jnp.full_like(square, ERF_Q[-1] * 4.0 ** (len(ERF_Q) - 1) * 2)
    for power in range(len(ERF_Q) - 2, -1, -1):
        total = total * square + ERF_Q[power] * 4.0**power * 2
    return half * jnp.tanh(half * total) + half


def pool(docs, both, first, last, total):
    def window(start):
        start = pl.multiple_of(start, 8)
        lane = lax.broadcasted_iota(jnp.int32, docs.shape, 1)
        mask = jnp.concatenate(
            [(docs == lane + (start + part)).astype(jnp.bfloat16) for part in range(0, WINDOW, LANES)], axis=1
        )
        rows = pl.ds(start, WINDOW)
        total[rows, :] += lax.dot_general(
            jnp.concatenate([mask, mask], axis=0),
            both,
            (((0,), (0,)), ((), ())),
            preferred_element_type=jnp.float32,
        )

    window(first)

    @pl.when(last >= first + WINDOW)
    def _():
        lax.fori_loop(
            1, lax.div(last - first, WINDOW) + 1, lambda number, carry: (window(first + number * WINDOW), carry)[1], 0
        )


def split(values):
    high = values.astype(jnp.bfloat16)
    return jnp.concatenate([high, (values - high.astype(jnp.float32)).astype(jnp.bfloat16)], axis=0)


def compressed(keys, docs_of, used):
    rows = keys.shape[0]
    kept = (keys < NONE) & (docs_of < used)
    ones = kept.astype(jnp.bfloat16)
    row, lane = (lax.broadcasted_iota(jnp.int32, (LANES, LANES), axis) for axis in range(2))
    before = jnp.dot(ones, (row < lane).astype(jnp.bfloat16), preferred_element_type=jnp.float32)
    whole = jnp.dot(ones, jnp.ones((LANES, LANES), jnp.bfloat16), preferred_element_type=jnp.float32)
    row, lane = (lax.broadcasted_iota(jnp.int32, (rows, rows), axis) for axis in range(2))
    above = (lane < row).astype(jnp.bfloat16)
    before += jnp.dot(above, whole.astype(jnp.bfloat16), preferred_element_type=jnp.float32)
    row, lane = (lax.broadcasted_iota(jnp.int32, keys.shape, axis) for axis in range(2))
    moves = jnp.where(kept, row * LANES + lane - before.astype(jnp.int32), 0)
    keys = jnp.where(kept, keys, NONE)
    for bit in range((rows * LANES - 1).bit_length()):
        step_by = 1 << bit

        def after(values):
            if step_by >= LANES:
                return pltpu.roll(values, rows - step_by // LANES, 0)
            values = pltpu.roll(values, LANES - step_by, 1)
            return jnp.where(lane < LANES - step_by, values, pltpu.roll(values, rows - 1, 0))

        next_moves, next_keys = after(moves), after(keys)
        comes, goes = (next_moves & step_by) != 0, (moves & step_by) != 0
        keys = jnp.where(comes, next_keys, jnp.where(goes, NONE, keys))
        moves = jnp.where(comes, next_moves, jnp.where(goes, 0, moves))
    return keys, jnp.sum(ones.astype(jnp.float32), axis=0, keepdims=True)


def prepare(place, own_ids, other_ids, table_all, positions, x_out, docs_out, bounds, normed_out, *scratch):
    total, rows32, table32, table, list_buffer, listed, sem, table_sem = scratch
    width = table.shape[1]
    pieces = width // LANES
    table_copy = pltpu.make_async_copy(table_all, table, table_sem)
    table_copy.start()

    def load():
        total[...] = jnp.zeros_like(total)

        def widen(group, carry):
            values = table[pl.ds(pl.multiple_of(group * 16, 16), 16), :].astype(jnp.float32)
            for eight in range(2):
                for piece in range(pieces):
                    at = pl.multiple_of((group * 2 + eight) * 8 * pieces + piece * 8, 8)
                    table32[pl.ds(at, 8), :] = values[eight * 8 : eight * 8 + 8, piece * LANES : (piece + 1) * LANES]
            return carry

        row, lane = (lax.broadcasted_iota(jnp.int32, (LANES, LANES), axis) for axis in range(2))
        of_doc = (row == lane >> SEQ_BITS).astype(jnp.bfloat16)
        used = []
        half_rows = own_ids.shape[0] // 2
        for tokens in (own_ids, other_ids):
            for half in range(2):
                around = []
                for number in range(4):
                    at = half_rows + (half * 4 + number) * 16
                    lengths = tokens[at : at + 16, :].astype(jnp.float32).astype(jnp.bfloat16)
                    around.append(jnp.dot(lengths, of_doc, preferred_element_type=jnp.float32))
                for y in range(4):
                    away = (y - place[1]) & 3
                    value = around[0]
                    for by, number in ((3, 1), (1, 2), (2, 3)):
                        value = jnp.where(away == by, around[number], value)
                    used.append(value)
        used = jnp.concatenate(used, axis=0).astype(jnp.int32)
        ids = jnp.concatenate([own_ids[:half_rows, :], other_ids[:half_rows, :]], axis=0)
        row, lane = (lax.broadcasted_iota(jnp.int32, ids.shape, axis) for axis in range(2))
        own_row = ids - place[0]
        doc = (row >> 4) * (12 * 8) + (row & 15) * 8 + (lane >> SEQ_BITS)
        time = lane & (SEQ - 1)
        keys = (doc << 19) + (time << 15) + (own_row >> 3) * 64 + (own_row & 7)
        inside = (own_row >= 0) & (own_row < table.shape[0]) & ((row & 15) < 12)
        keys, sums = compressed(jnp.where(inside, keys, NONE), time, used)
        most = listed.shape[0] - 8
        list_buffer[pl.ds(0, most), :] = keys[:most]
        count = jnp.sum(sums, axis=1, keepdims=True).astype(jnp.int32)
        list_buffer[pl.ds(most, 8), :] = jnp.broadcast_to(count, (8, LANES))
        copy = pltpu.make_async_copy(list_buffer, listed, sem)
        copy.start()
        table_copy.wait()
        lax.fori_loop(0, table.shape[0] // 16, widen, 0)
        copy.wait()
        return listed[most, 0]

    end = load()
    tiles = jnp.maximum((end + TILE - 1) >> TILE_BITS, 1)
    own = total.shape[0] - WINDOW
    bounds[BOUNDS - 1] = tiles

    def tile(x_ref, docs_ref):
        index = pl.program_id(0)
        first = index * TILE

        def key_at(slot):
            return listed[slot >> 7, slot & (LANES - 1)]

        for half in range(TILE // LANES):

            def take(group, carry, half=half):
                for one in range(8):
                    key = listed[TILE // LANES * index + half, group * 8 + one]
                    at = key & 0x7FFF
                    when = pl.multiple_of((key >> 12) & 0x78, 8)
                    value = table32[pl.ds(at, pieces, stride=8), :] + positions[pl.ds(when, pieces), :]
                    rows32[pl.ds((half * 16 + group) * 8 * pieces + one, pieces, stride=8), :] = value
                    docs_ref[pl.ds((half * 16 + group) * 8 + one, 1), :] = jnp.full((1, LANES), key >> 19, jnp.int32)
                return carry

            lax.fori_loop(0, LANES // 8, take, 0, unroll=True)
        normed = []
        for sub in range(TILE // SUB):
            block = rows32[pl.ds(sub * SUB * pieces, SUB * pieces), :].reshape(SUB // 8, pieces, 8, LANES)
            values = jnp.concatenate([block[:, piece].reshape(SUB, LANES) for piece in range(pieces)], axis=1)
            mean = jnp.mean(values, axis=-1, keepdims=True)
            centred = values - mean
            var = jnp.mean(centred * centred, axis=-1, keepdims=True)
            normal = centred * lax.rsqrt(var + 1e-05)
            x_ref[pl.ds(sub * SUB, SUB), :] = (normal * 0.5).astype(jnp.bfloat16)
            normed.append(normal)
        low = jnp.minimum((key_at(first) >> 22) << 3, 2 * own - 8)
        high = jnp.minimum(key_at(jnp.clip(end - 1, first, first + TILE - 1)) >> 19, 2 * own - 1)
        bounds[2 * index] = low
        bounds[2 * index + 1] = high

        @pl.when(low < own)
        def _():
            pool(docs_ref[...], split(jnp.concatenate(normed, axis=0)), low, jnp.minimum(high, own - 1), total)

    pltpu.emit_pipeline(
        tile,
        grid=(tiles,),
        in_specs=[],
        out_specs=[
            pl.BlockSpec((TILE, width), lambda i: (i, 0)),
            pl.BlockSpec((TILE, LANES), lambda i: (i, 0)),
        ],
    )(x_out, docs_out)
    copy = pltpu.make_async_copy(total.at[pl.ds(0, own), :], normed_out, sem)
    copy.start()
    copy.wait()


def run_prepare(place, own_ids, other_ids, embed_table, positions, group, most):
    seq, width = positions.shape
    vocab_rows = embed_table.shape[0]
    pieces = width // LANES
    smem, vmem, hbm = (pl.BlockSpec(memory_space=space) for space in (pltpu.SMEM, pltpu.VMEM, pltpu.HBM))
    return pl.pallas_call(
        prepare,
        in_specs=[smem, vmem, vmem, hbm, vmem],
        out_specs=[hbm, hbm, smem, hbm],
        out_shape=[
            jax.ShapeDtypeStruct((most, width), jnp.bfloat16),
            jax.ShapeDtypeStruct((most, LANES), jnp.int32),
            jax.ShapeDtypeStruct((BOUNDS,), jnp.int32),
            jax.ShapeDtypeStruct((group, width), jnp.float32),
        ],
        scratch_shapes=[
            pltpu.VMEM((group + WINDOW, width), jnp.float32),
            pltpu.VMEM(((TILE + 8) * pieces, LANES), jnp.float32),
            pltpu.VMEM(((vocab_rows + 8) * pieces, LANES), jnp.float32),
            pltpu.VMEM((vocab_rows, width), jnp.bfloat16),
            pltpu.VMEM((most // LANES + 8, LANES), jnp.int32),
            pltpu.SMEM((most // LANES + 8, LANES), jnp.int32),
            pltpu.SemaphoreType.DMA,
            pltpu.SemaphoreType.DMA,
        ],
        compiler_params=pltpu.CompilerParams(vmem_limit_bytes=52 << 20),
        cost_estimate=pl.CostEstimate(flops=1 << 30, bytes_accessed=1 << 20, transcendentals=0),
    )(place, own_ids, other_ids, embed_table, positions.astype(jnp.float32).reshape(seq * pieces, LANES))


def over_tiles(tiles, several):
    def pair(number, carry):
        several(number * 2, 2)
        return carry

    lax.fori_loop(0, tiles >> 1, pair, 0)

    @pl.when((tiles & 1) == 1)
    def _():
        several(tiles - 1, 1)


def rows_of(tile, count):
    return pl.ds(pl.multiple_of(tile * TILE, TILE), count * TILE)


def load_pairs(tiles, loads):
    def copies(tile, slot):
        return [
            pltpu.make_async_copy(whole.at[rows_of(tile, 2), :], place.at[slot], sems.at[slot])
            for whole, place, sems in loads
        ]

    for copy in copies(0, 0):
        copy.start()

    def ready(tile):
        slot = (tile >> 1) & 1

        @pl.when(tile + 2 < tiles)
        def _():
            for copy in copies(tile + 2, 1 - slot):
                copy.start()

        for copy in copies(tile, slot):
            copy.wait()
        return slot

    return ready


def activate(inputs, w_in, hidden, first, staged):
    rows = pl.ds(0, inputs.shape[0])
    steps = w_in.shape[0] // CHUNK
    for number in range(steps + 1):
        if number < steps:
            weights = w_in[pl.ds(number * CHUNK, CHUNK), :]
            staged[number % 2, rows, :] = lax.dot_general(
                inputs[...], weights, (((1,), (1,)), ((), ())), preferred_element_type=jnp.float32
            )
        if number > 0:
            columns = pl.ds(first + (number - 1) * CHUNK, CHUNK)
            hidden[rows, columns] = half_gelu(staged[(number - 1) % 2, rows, :]).astype(jnp.bfloat16)


def load_units(pieces, w_in, w_out, sems):
    units = pieces[0].shape[0] // 2
    copies = []
    for number, piece in enumerate(pieces):
        for which, whole in enumerate((w_in, w_out)):
            part = piece.at[pl.ds(which * units, units), :]
            place = whole.at[pl.ds(number * units, units), :]
            copies.append(pltpu.make_async_copy(part, place, sems.at[2 * number + which]))
    for copy in copies:
        copy.start()
    return copies


def first_units(near, bounds, x_all, *refs):
    pieces, (out, x, w_in, w_out, hidden, staged, sums, w_sems, x_sems, out_sems) = refs[:near], refs[near:]
    tiles = bounds[BOUNDS - 1]
    copies = load_units(pieces, w_in, w_out, w_sems)
    ready = load_pairs(tiles, [(x_all, x, x_sems)])
    for copy in copies:
        copy.wait()

    def store(tile, slot):
        return pltpu.make_async_copy(sums.at[slot], out.at[rows_of(tile, 2), :], out_sems.at[slot])

    def several(tile, count):
        slot = ready(tile)

        @pl.when(tile >= 4)
        def _():
            store(tile - 4, slot).wait()

        rows = pl.ds(0, count * TILE)
        activate(x.at[slot, rows, :], w_in, hidden, 0, staged)
        sums[slot, rows, :] = jnp.dot(hidden[rows, :], w_out[...], preferred_element_type=jnp.float32)
        store(tile, slot).start()

    over_tiles(tiles, several)
    last = ((tiles + 1) >> 1) * 2 - 2

    @pl.when(last >= 2)
    def _():
        store(last - 2, 1 - ((last >> 1) & 1)).wait()

    store(last, (last >> 1) & 1).wait()


def second_units(far, bounds, x_all, docs_all, normed, sums_all, *refs):
    pieces, refs = refs[:far], refs[far:]
    own, other, total, x, docs, w_in, w_out, hidden, staged, sums, w_sems, x_sems, docs_sems, sums_sems, ends = refs
    tiles = bounds[BOUNDS - 1]
    group = own.shape[0]
    copies = load_units(pieces, w_in, w_out, w_sems)
    copies.append(pltpu.make_async_copy(normed, total.at[pl.ds(0, group), :], ends.at[0]))
    copies[-1].start()
    ready = load_pairs(tiles, [(x_all, x, x_sems), (docs_all, docs, docs_sems), (sums_all, sums, sums_sems)])
    rest = total.shape[0] - group
    total[pl.ds(group, rest), :] = jnp.zeros((rest, total.shape[1]), jnp.float32)
    for copy in copies:
        copy.wait()

    def several(tile, count):
        slot = ready(tile)
        rows = pl.ds(0, count * TILE)
        activate(x.at[slot, rows, :], w_in, hidden, 0, staged)
        branch = sums[slot, rows, :] + jnp.dot(hidden[rows, :], w_out[...], preferred_element_type=jnp.float32)
        for one in range(count):
            part = slice(one * TILE, (one + 1) * TILE)
            pool(docs[slot, part, :], split(branch[part]), bounds[2 * (tile + one)], bounds[2 * (tile + one) + 1], total)

    over_tiles(tiles, several)
    copies = [
        pltpu.make_async_copy(total.at[pl.ds(0, group), :], own, ends.at[0]),
        pltpu.make_async_copy(total.at[pl.ds(group, group), :], other, ends.at[1]),
    ]
    for copy in copies:
        copy.start()
    for copy in copies:
        copy.wait()


def run_first(near, bounds, x):
    most, width = x.shape
    units = len(near) * near[0].shape[0] // 2
    smem, hbm, anywhere = (pl.BlockSpec(memory_space=space) for space in (pltpu.SMEM, pltpu.HBM, pl.ANY))
    return pl.pallas_call(
        functools.partial(first_units, len(near)),
        in_specs=[smem, hbm] + [anywhere] * len(near),
        out_specs=hbm,
        out_shape=jax.ShapeDtypeStruct((most, width), jnp.float32),
        scratch_shapes=[
            pltpu.VMEM((2, 2 * TILE, width), jnp.bfloat16),
            pltpu.VMEM((units, width), jnp.bfloat16),
            pltpu.VMEM((units, width), jnp.bfloat16),
            pltpu.VMEM((2 * TILE, units), jnp.bfloat16),
            pltpu.VMEM((2, 2 * TILE, CHUNK), jnp.float32),
            pltpu.VMEM((2, 2 * TILE, width), jnp.float32),
            pltpu.SemaphoreType.DMA((2 * len(near),)),
            pltpu.SemaphoreType.DMA((2,)),
            pltpu.SemaphoreType.DMA((2,)),
        ],
        compiler_params=pltpu.CompilerParams(vmem_limit_bytes=44 << 20),
        cost_estimate=pl.CostEstimate(flops=20 << 30, bytes_accessed=16 << 20, transcendentals=0),
    )(bounds, x, *near)


def run_second(far, bounds, x, docs, normed, sums):
    most, width = x.shape
    group = normed.shape[0]
    units = len(far) * far[0].shape[0] // 2
    smem, hbm, anywhere = (pl.BlockSpec(memory_space=space) for space in (pltpu.SMEM, pltpu.HBM, pl.ANY))
    return pl.pallas_call(
        functools.partial(second_units, len(far)),
        in_specs=[smem, hbm, hbm, anywhere, hbm] + [anywhere] * len(far),
        out_specs=[anywhere, anywhere],
        out_shape=[jax.ShapeDtypeStruct((group, width), jnp.float32)] * 2,
        scratch_shapes=[
            pltpu.VMEM((2 * group + WINDOW, width), jnp.float32),
            pltpu.VMEM((2, 2 * TILE, width), jnp.bfloat16),
            pltpu.VMEM((2, 2 * TILE, LANES), jnp.int32),
            pltpu.VMEM((units, width), jnp.bfloat16),
            pltpu.VMEM((units, width), jnp.bfloat16),
            pltpu.VMEM((2 * TILE, units), jnp.bfloat16),
            pltpu.VMEM((2, 2 * TILE, CHUNK), jnp.float32),
            pltpu.VMEM((2, 2 * TILE, width), jnp.float32),
            pltpu.SemaphoreType.DMA((2 * len(far),)),
            pltpu.SemaphoreType.DMA((2,)),
            pltpu.SemaphoreType.DMA((2,)),
            pltpu.SemaphoreType.DMA((2,)),
            pltpu.SemaphoreType.DMA((2,)),
        ],
        compiler_params=pltpu.CompilerParams(vmem_limit_bytes=36 << 20),
        cost_estimate=pl.CostEstimate(flops=12 << 30, bytes_accessed=24 << 20, transcendentals=0),
    )(bounds, x, docs, normed, sums, *far)


def local(token_ids, doc_lengths, clusters, embed_table, positions, w_in, w_out):
    doc_dev = doc_lengths.shape[0]
    group, seq = token_ids.shape
    vocab_rows, width = embed_table.shape
    n_col = group // doc_dev

    with jax.named_scope("weights"):
        half = w_in.shape[0] // 2
        mixed = jnp.concatenate([w_in[:half], w_out[:half], w_in[half:], w_out[half:]], axis=0)
        mixed, doc_lengths = lax.optimization_barrier((mixed, doc_lengths))
        by_z = ring(mixed, "z")
        lengths = jnp.pad(doc_lengths.reshape(doc_dev // 8, 8), ((0, 16 - doc_dev // 8), (0, LANES - 8))).astype(jnp.bfloat16)
        over = lax.ppermute(lengths, "x_hi", [(0, 1), (1, 0)])
        lower = lax.axis_index("x_hi") == 0
        lengths = jnp.concatenate([jnp.where(lower, lengths, over), jnp.where(lower, over, lengths)], axis=1)
        lengths = jnp.pad(lengths, ((0, 0), (0, width - 2 * LANES)))
        first, second = joined([by_z, by_z], [0, 2 * half], 2 * half, lengths)
        rows = first.shape[0]
        place = jnp.stack([lax.axis_index(COL) * vocab_rows, lax.axis_index("y")]).astype(jnp.int32)
        first, second = ring(first, X), ring(second, "y")
        first, second, token_ids = lax.optimization_barrier((first, second, token_ids))
        ids = token_ids.reshape(n_col, doc_dev * seq // LANES, LANES)
        ids = jnp.pad(ids, ((0, 0), (0, 16 - ids.shape[1]), (0, 0))).reshape(n_col * 16, LANES)
        own_ids = with_lengths(ids, second)
        other_ids = step(own_ids, "core", 1)
        first, second = joined([first, second], [0, 0], rows)
        units = first.shape[0] // 2
        left, right = step(first, "y", 1), step(first, "y", -1)
        down, up = step(second, X, 1), step(second, X, -1)
        near = [first, left, right, second, down, up]

    with jax.named_scope("prepare"):
        most = 2 * n_col * SHARD_CAP
        x, docs, bounds, normed = run_prepare(place, own_ids, other_ids, embed_table, positions, group, most)

    with jax.named_scope("forward"):
        near, x = lax.optimization_barrier((near, x))
        far = [step(near[0], "y", 2), step(near[3], X, 2)]
        sums = run_first(near, bounds, x)
        own, other = run_second(far, bounds, x, docs, normed, sums)

    with jax.named_scope("pooled"):
        sums = own + step(other, "core", 1)
        sums = sums.astype(jnp.bfloat16).reshape(n_col, doc_dev, width)
        sums = lax.all_to_all(sums, COL, 0, 0, tiled=True)
        pooled = jnp.sum(sums.astype(jnp.float32), axis=0) / doc_lengths.astype(jnp.float32)[:, None]
        scale = lax.rsqrt(jnp.sum(pooled * pooled, axis=-1, keepdims=True) + 1e-06)
        embedding = (pooled * scale).astype(jnp.bfloat16)

    with jax.named_scope("match"):
        n_clusters = lax.axis_size(CHIPS)
        labels = clusters[:, 0]
        same = labels[:, None] == labels[None, :]
        order = jnp.arange(doc_dev, dtype=jnp.int32)
        rank = jnp.sum((same & (order[:, None] > order[None, :])).astype(jnp.int32), axis=1)
        slot = labels * 4 + rank
        chosen = slot[None, :] == jnp.arange(n_clusters * 4, dtype=jnp.int32)[:, None]
        sizes = jnp.sum((labels[None, :] == jnp.arange(n_clusters)[:, None]).astype(jnp.int32), axis=1)
        fourth = lax.broadcasted_iota(jnp.int32, (n_clusters, 4, width), 1) == 3
        flags = lax.broadcasted_iota(jnp.int32, (n_clusters, 4, width), 2) < sizes[:, None, None]
        outgoing = jnp.dot(chosen.astype(jnp.bfloat16), embedding, preferred_element_type=jnp.float32)
        outgoing = jnp.where(
            fourth, flags.astype(jnp.float32), outgoing.reshape(n_clusters, 4, width)
        ).astype(jnp.bfloat16)
        members = lax.all_to_all(outgoing, CHIPS, 0, 0, tiled=True)
        others = step(members, "core", 1)
        every = jnp.concatenate([members, others], axis=0)
        filled = jnp.pad(every[:, 3, :3], ((0, 0), (0, 1))).reshape(-1) > 0.5
        count = n_clusters * 4
        scores = jnp.dot(
            members.reshape(count, width), every.reshape(2 * count, width).T, preferred_element_type=jnp.float32
        )
        own = jnp.arange(count)[:, None] == jnp.arange(2 * count)[None, :]
        best = jnp.max(jnp.where(filled[None, :] & jnp.logical_not(own), scores, -1.0), axis=1)
        best = jnp.maximum(best, -1.0)
        returned = lax.all_to_all(best.reshape(n_clusters, 4), CHIPS, 0, 0, tiled=True)
        of_cluster = (labels[:, None] == jnp.arange(n_clusters)[None, :]).astype(jnp.float32)
        rows = jnp.dot(of_cluster, returned, precision=lax.Precision.HIGHEST, preferred_element_type=jnp.float32)
        return jnp.sum(jnp.where(rank[:, None] == jnp.arange(4)[None, :], rows, 0.0), axis=1)


def solution(mesh):
    fine = Mesh(mesh.devices.reshape(2, 4, 2, 2, 4), ("x_lo", "z", "core", "x_hi", "y"))
    everywhere = OWN + COL
    return jax.shard_map(
        local,
        mesh=fine,
        in_specs=(
            P(OWN, None),
            P(everywhere),
            P(everywhere, None),
            P(COL, None),
            P(),
            P(everywhere, None),
            P(everywhere, None),
        ),
        out_specs=P(everywhere),
        check_vma=False,
    )
```

```python
import functools

import jax
import jax.numpy as jnp
from jax import lax
from jax.experimental import pallas as pl
from jax.experimental.pallas import tpu as pltpu
from jax.sharding import Mesh
from jax.sharding import PartitionSpec as P

OWN = ("x_lo", "z", "core")
COL = ("x_hi", "y")
X = ("x_lo", "x_hi")
CHIPS = ("x_lo", "z", "x_hi", "y")
SHARD_CAP = 384
TILE_BITS = 8
TILE = 1 << TILE_BITS
LANES = 128
SUB = 64
SEQ_BITS = 4
SEQ = 1 << SEQ_BITS
NONE = 1 << 30
BOUNDS = 64
CHUNK = 512
WINDOW = 256
ERF_Q = (
    0.7978853416207131,
    0.03633264203955081,
    -3.271896418592583e-05,
    -5.512179284196367e-05,
    3.917683168513537e-06,
    -1.2794852180568973e-07,
    1.6281616374933989e-09,
)


def step(value, axis, by):
    count = 2 if axis == "core" else 4
    place = (lambda x: (x % 2) * 2 + x // 2) if axis == X else (lambda x: x)
    return lax.ppermute(value, axis, [(place(i), place((i + by) % count)) for i in range(count)])


def ring(value, axis):
    return [value] + [step(value, axis, by) for by in (1, -1, 2)]


def copied(sources, shapes, moves):
    def kernel(*refs):
        inputs, outputs = refs[: len(sources)], refs[len(sources) :]
        for source, from_row, result, to_row, rows in moves:
            outputs[result][to_row : to_row + rows, :] = inputs[source][from_row : from_row + rows, :]

    vmem = pl.BlockSpec(memory_space=pltpu.VMEM)
    return pl.pallas_call(
        kernel,
        in_specs=[vmem] * len(sources),
        out_specs=[vmem] * len(shapes),
        out_shape=[jax.ShapeDtypeStruct(shape, sources[0].dtype) for shape in shapes],
        compiler_params=pltpu.CompilerParams(vmem_limit_bytes=8 << 20),
        cost_estimate=pl.CostEstimate(flops=1 << 10, bytes_accessed=1 << 10, transcendentals=0),
    )(*sources)


def joined(rings, starts, rows, extra=None):
    sources, shapes, moves = [], [], []
    for result, (pieces, start) in enumerate(zip(rings, starts)):
        half = rows // 2
        shapes.append((len(pieces) * rows, pieces[0].shape[1]))
        for number, piece in enumerate(pieces):
            for which in range(2):
                to_row = (which * len(pieces) + number) * half
                moves.append((len(sources) + number, start + which * half, result, to_row, half))
        sources += pieces
    if extra is not None:
        height, width = shapes[-1]
        shapes[-1] = (height + extra.shape[0], width)
        moves.append((len(sources), 0, len(shapes) - 1, height, extra.shape[0]))
        sources.append(extra)
    return copied(sources, shapes, moves)


def with_lengths(ids, pieces):
    def kernel(ids_ref, *refs):
        pieces, out = refs[:-1], refs[-1]
        out[: ids_ref.shape[0], :] = ids_ref[...]
        for half in range(2):
            for number, piece in enumerate(pieces):
                at = ids_ref.shape[0] + (half * len(pieces) + number) * 16
                part = piece[piece.shape[0] - 16 :, half * LANES : (half + 1) * LANES]
                out[at : at + 16, :] = part.astype(jnp.float32).astype(jnp.int32)

    vmem = pl.BlockSpec(memory_space=pltpu.VMEM)
    return pl.pallas_call(
        kernel,
        in_specs=[vmem] * (1 + len(pieces)),
        out_specs=vmem,
        out_shape=jax.ShapeDtypeStruct((ids.shape[0] + 32 * len(pieces), LANES), jnp.int32),
        compiler_params=pltpu.CompilerParams(vmem_limit_bytes=4 << 20),
        cost_estimate=pl.CostEstimate(flops=1 << 10, bytes_accessed=1 << 10, transcendentals=0),
    )(ids, *pieces)


def half_gelu(half):
    square = half * half
    total = jnp.full_like(square, ERF_Q[-1] * 4.0 ** (len(ERF_Q) - 1) * 2)
    for power in range(len(ERF_Q) - 2, -1, -1):
        total = total * square + ERF_Q[power] * 4.0**power * 2
    return half * jnp.tanh(half * total) + half


def pool(docs, both, first, last, total):
    def window(start):
        start = pl.multiple_of(start, 8)
        lane = lax.broadcasted_iota(jnp.int32, docs.shape, 1)
        mask = jnp.concatenate(
            [(docs == lane + (start + part)).astype(jnp.bfloat16) for part in range(0, WINDOW, LANES)], axis=1
        )
        rows = pl.ds(start, WINDOW)
        total[rows, :] += lax.dot_general(
            jnp.concatenate([mask, mask], axis=0),
            both,
            (((0,), (0,)), ((), ())),
            preferred_element_type=jnp.float32,
        )

    window(first)

    @pl.when(last >= first + WINDOW)
    def _():
        lax.fori_loop(
            1, lax.div(last - first, WINDOW) + 1, lambda number, carry: (window(first + number * WINDOW), carry)[1], 0
        )


def split(values):
    high = values.astype(jnp.bfloat16)
    return jnp.concatenate([high, (values - high.astype(jnp.float32)).astype(jnp.bfloat16)], axis=0)


def compressed(keys, docs_of, used):
    rows = keys.shape[0]
    kept = (keys < NONE) & (docs_of < used)
    ones = kept.astype(jnp.bfloat16)
    row, lane = (lax.broadcasted_iota(jnp.int32, (LANES, LANES), axis) for axis in range(2))
    before = jnp.dot(ones, (row < lane).astype(jnp.bfloat16), preferred_element_type=jnp.float32)
    whole = jnp.dot(ones, jnp.ones((LANES, LANES), jnp.bfloat16), preferred_element_type=jnp.float32)
    row, lane = (lax.broadcasted_iota(jnp.int32, (rows, rows), axis) for axis in range(2))
    above = (lane < row).astype(jnp.bfloat16)
    before += jnp.dot(above, whole.astype(jnp.bfloat16), preferred_element_type=jnp.float32)
    row, lane = (lax.broadcasted_iota(jnp.int32, keys.shape, axis) for axis in range(2))
    moves = jnp.where(kept, row * LANES + lane - before.astype(jnp.int32), 0)
    keys = jnp.where(kept, keys, NONE)
    for bit in range((rows * LANES - 1).bit_length()):
        step_by = 1 << bit

        def after(values):
            if step_by >= LANES:
                return pltpu.roll(values, rows - step_by // LANES, 0)
            values = pltpu.roll(values, LANES - step_by, 1)
            return jnp.where(lane < LANES - step_by, values, pltpu.roll(values, rows - 1, 0))

        next_moves, next_keys = after(moves), after(keys)
        comes, goes = (next_moves & step_by) != 0, (moves & step_by) != 0
        keys = jnp.where(comes, next_keys, jnp.where(goes, NONE, keys))
        moves = jnp.where(comes, next_moves, jnp.where(goes, 0, moves))
    return keys, jnp.sum(ones.astype(jnp.float32), axis=0, keepdims=True)


def prepare(place, own_ids, other_ids, table_all, positions, x_out, docs_out, bounds, normed_out, *scratch):
    total, rows32, table32, table, list_buffer, listed, sem, table_sem = scratch
    width = table.shape[1]
    pieces = width // LANES
    table_copy = pltpu.make_async_copy(table_all, table, table_sem)
    table_copy.start()

    def load():
        total[...] = jnp.zeros_like(total)

        def widen(group, carry):
            values = table[pl.ds(pl.multiple_of(group * 16, 16), 16), :].astype(jnp.float32)
            for eight in range(2):
                for piece in range(pieces):
                    at = pl.multiple_of((group * 2 + eight) * 8 * pieces + piece * 8, 8)
                    table32[pl.ds(at, 8), :] = values[eight * 8 : eight * 8 + 8, piece * LANES : (piece + 1) * LANES]
            return carry

        row, lane = (lax.broadcasted_iota(jnp.int32, (LANES, LANES), axis) for axis in range(2))
        of_doc = (row == lane >> SEQ_BITS).astype(jnp.bfloat16)
        used = []
        half_rows = own_ids.shape[0] // 2
        for tokens in (own_ids, other_ids):
            for half in range(2):
                around = []
                for number in range(4):
                    at = half_rows + (half * 4 + number) * 16
                    lengths = tokens[at : at + 16, :].astype(jnp.float32).astype(jnp.bfloat16)
                    around.append(jnp.dot(lengths, of_doc, preferred_element_type=jnp.float32))
                for y in range(4):
                    away = (y - place[1]) & 3
                    value = around[0]
                    for by, number in ((3, 1), (1, 2), (2, 3)):
                        value = jnp.where(away == by, around[number], value)
                    used.append(value)
        used = jnp.concatenate(used, axis=0).astype(jnp.int32)
        ids = jnp.concatenate([own_ids[:half_rows, :], other_ids[:half_rows, :]], axis=0)
        row, lane = (lax.broadcasted_iota(jnp.int32, ids.shape, axis) for axis in range(2))
        own_row = ids - place[0]
        doc = (row >> 4) * (12 * 8) + (row & 15) * 8 + (lane >> SEQ_BITS)
        time = lane & (SEQ - 1)
        keys = (doc << 19) + (time << 15) + (own_row >> 3) * 64 + (own_row & 7)
        inside = (own_row >= 0) & (own_row < table.shape[0]) & ((row & 15) < 12)
        keys, sums = compressed(jnp.where(inside, keys, NONE), time, used)
        most = listed.shape[0] - 8
        list_buffer[pl.ds(0, most), :] = keys[:most]
        count = jnp.sum(sums, axis=1, keepdims=True).astype(jnp.int32)
        list_buffer[pl.ds(most, 8), :] = jnp.broadcast_to(count, (8, LANES))
        copy = pltpu.make_async_copy(list_buffer, listed, sem)
        copy.start()
        table_copy.wait()
        lax.fori_loop(0, table.shape[0] // 16, widen, 0)
        copy.wait()
        return listed[most, 0]

    end = load()
    tiles = jnp.maximum((end + TILE - 1) >> TILE_BITS, 1)
    own = total.shape[0] - WINDOW
    bounds[BOUNDS - 1] = tiles

    def tile(x_ref, docs_ref):
        index = pl.program_id(0)
        first = index * TILE

        def key_at(slot):
            return listed[slot >> 7, slot & (LANES - 1)]

        for half in range(TILE // LANES):

            def take(group, carry, half=half):
                for one in range(8):
                    key = listed[TILE // LANES * index + half, group * 8 + one]
                    at = key & 0x7FFF
                    when = pl.multiple_of((key >> 12) & 0x78, 8)
                    value = table32[pl.ds(at, pieces, stride=8), :] + positions[pl.ds(when, pieces), :]
                    rows32[pl.ds((half * 16 + group) * 8 * pieces + one, pieces, stride=8), :] = value
                    docs_ref[pl.ds((half * 16 + group) * 8 + one, 1), :] = jnp.full((1, LANES), key >> 19, jnp.int32)
                return carry

            lax.fori_loop(0, LANES // 8, take, 0, unroll=True)
        normed = []
        for sub in range(TILE // SUB):
            block = rows32[pl.ds(sub * SUB * pieces, SUB * pieces), :].reshape(SUB // 8, pieces, 8, LANES)
            values = jnp.concatenate([block[:, piece].reshape(SUB, LANES) for piece in range(pieces)], axis=1)
            mean = jnp.mean(values, axis=-1, keepdims=True)
            centred = values - mean
            var = jnp.mean(centred * centred, axis=-1, keepdims=True)
            normal = centred * lax.rsqrt(var + 1e-05)
            x_ref[pl.ds(sub * SUB, SUB), :] = (normal * 0.5).astype(jnp.bfloat16)
            normed.append(normal)
        low = jnp.minimum((key_at(first) >> 22) << 3, 2 * own - 8)
        high = jnp.minimum(key_at(jnp.clip(end - 1, first, first + TILE - 1)) >> 19, 2 * own - 1)
        bounds[2 * index] = low
        bounds[2 * index + 1] = high

        @pl.when(low < own)
        def _():
            pool(docs_ref[...], split(jnp.concatenate(normed, axis=0)), low, jnp.minimum(high, own - 1), total)

    pltpu.emit_pipeline(
        tile,
        grid=(tiles,),
        in_specs=[],
        out_specs=[
            pl.BlockSpec((TILE, width), lambda i: (i, 0)),
            pl.BlockSpec((TILE, LANES), lambda i: (i, 0)),
        ],
    )(x_out, docs_out)
    copy = pltpu.make_async_copy(total.at[pl.ds(0, own), :], normed_out, sem)
    copy.start()
    copy.wait()


def run_prepare(place, own_ids, other_ids, embed_table, positions, group, most):
    seq, width = positions.shape
    vocab_rows = embed_table.shape[0]
    pieces = width // LANES
    smem, vmem, hbm = (pl.BlockSpec(memory_space=space) for space in (pltpu.SMEM, pltpu.VMEM, pltpu.HBM))
    return pl.pallas_call(
        prepare,
        in_specs=[smem, vmem, vmem, hbm, vmem],
        out_specs=[hbm, hbm, smem, hbm],
        out_shape=[
            jax.ShapeDtypeStruct((most, width), jnp.bfloat16),
            jax.ShapeDtypeStruct((most, LANES), jnp.int32),
            jax.ShapeDtypeStruct((BOUNDS,), jnp.int32),
            jax.ShapeDtypeStruct((group, width), jnp.float32),
        ],
        scratch_shapes=[
            pltpu.VMEM((group + WINDOW, width), jnp.float32),
            pltpu.VMEM(((TILE + 8) * pieces, LANES), jnp.float32),
            pltpu.VMEM(((vocab_rows + 8) * pieces, LANES), jnp.float32),
            pltpu.VMEM((vocab_rows, width), jnp.bfloat16),
            pltpu.VMEM((most // LANES + 8, LANES), jnp.int32),
            pltpu.SMEM((most // LANES + 8, LANES), jnp.int32),
            pltpu.SemaphoreType.DMA,
            pltpu.SemaphoreType.DMA,
        ],
        compiler_params=pltpu.CompilerParams(vmem_limit_bytes=52 << 20),
        cost_estimate=pl.CostEstimate(flops=1 << 30, bytes_accessed=1 << 20, transcendentals=0),
    )(place, own_ids, other_ids, embed_table, positions.astype(jnp.float32).reshape(seq * pieces, LANES))


def over_tiles(tiles, several):
    def pair(number, carry):
        several(number * 2, 2)
        return carry

    lax.fori_loop(0, tiles >> 1, pair, 0)

    @pl.when((tiles & 1) == 1)
    def _():
        several(tiles - 1, 1)


def rows_of(tile, count):
    return pl.ds(pl.multiple_of(tile * TILE, TILE), count * TILE)


def load_pairs(tiles, loads):
    def copies(tile, slot):
        return [
            pltpu.make_async_copy(whole.at[rows_of(tile, 2), :], place.at[slot], sems.at[slot])
            for whole, place, sems in loads
        ]

    for copy in copies(0, 0):
        copy.start()

    def ready(tile):
        slot = (tile >> 1) & 1

        @pl.when(tile + 2 < tiles)
        def _():
            for copy in copies(tile + 2, 1 - slot):
                copy.start()

        for copy in copies(tile, slot):
            copy.wait()
        return slot

    return ready


def activate(inputs, w_in, hidden, first, staged):
    rows = pl.ds(0, inputs.shape[0])
    steps = w_in.shape[0] // CHUNK
    for number in range(steps + 1):
        if number < steps:
            weights = w_in[pl.ds(number * CHUNK, CHUNK), :]
            staged[number % 2, rows, :] = lax.dot_general(
                inputs[...], weights, (((1,), (1,)), ((), ())), preferred_element_type=jnp.float32
            )
        if number > 0:
            columns = pl.ds(first + (number - 1) * CHUNK, CHUNK)
            hidden[rows, columns] = half_gelu(staged[(number - 1) % 2, rows, :]).astype(jnp.bfloat16)


def load_units(pieces, w_in, w_out, sems):
    units = pieces[0].shape[0] // 2
    copies = []
    for number, piece in enumerate(pieces):
        for which, whole in enumerate((w_in, w_out)):
            part = piece.at[pl.ds(which * units, units), :]
            place = whole.at[pl.ds(number * units, units), :]
            copies.append(pltpu.make_async_copy(part, place, sems.at[2 * number + which]))
    for copy in copies:
        copy.start()
    return copies


def first_units(near, bounds, x_all, *refs):
    pieces, (out, x, w_in, w_out, hidden, staged, sums, w_sems, x_sems, out_sems) = refs[:near], refs[near:]
    tiles = bounds[BOUNDS - 1]
    copies = load_units(pieces, w_in, w_out, w_sems)
    ready = load_pairs(tiles, [(x_all, x, x_sems)])
    for copy in copies:
        copy.wait()

    def store(tile, slot):
        return pltpu.make_async_copy(sums.at[slot], out.at[rows_of(tile, 2), :], out_sems.at[slot])

    def several(tile, count):
        slot = ready(tile)

        @pl.when(tile >= 4)
        def _():
            store(tile - 4, slot).wait()

        rows = pl.ds(0, count * TILE)
        activate(x.at[slot, rows, :], w_in, hidden, 0, staged)
        sums[slot, rows, :] = jnp.dot(hidden[rows, :], w_out[...], preferred_element_type=jnp.float32)
        store(tile, slot).start()

    over_tiles(tiles, several)
    last = ((tiles + 1) >> 1) * 2 - 2

    @pl.when(last >= 2)
    def _():
        store(last - 2, 1 - ((last >> 1) & 1)).wait()

    store(last, (last >> 1) & 1).wait()


def second_units(far, bounds, x_all, docs_all, normed, sums_all, *refs):
    pieces, refs = refs[:far], refs[far:]
    own, other, total, x, docs, w_in, w_out, hidden, staged, sums, w_sems, x_sems, docs_sems, sums_sems, ends = refs
    tiles = bounds[BOUNDS - 1]
    group = own.shape[0]
    copies = load_units(pieces, w_in, w_out, w_sems)
    copies.append(pltpu.make_async_copy(normed, total.at[pl.ds(0, group), :], ends.at[0]))
    copies[-1].start()
    ready = load_pairs(tiles, [(x_all, x, x_sems), (docs_all, docs, docs_sems), (sums_all, sums, sums_sems)])
    rest = total.shape[0] - group
    total[pl.ds(group, rest), :] = jnp.zeros((rest, total.shape[1]), jnp.float32)
    for copy in copies:
        copy.wait()

    def several(tile, count):
        slot = ready(tile)
        rows = pl.ds(0, count * TILE)
        activate(x.at[slot, rows, :], w_in, hidden, 0, staged)
        branch = sums[slot, rows, :] + jnp.dot(hidden[rows, :], w_out[...], preferred_element_type=jnp.float32)
        for one in range(count):
            part = slice(one * TILE, (one + 1) * TILE)
            pool(docs[slot, part, :], split(branch[part]), bounds[2 * (tile + one)], bounds[2 * (tile + one) + 1], total)

    over_tiles(tiles, several)
    copies = [
        pltpu.make_async_copy(total.at[pl.ds(0, group), :], own, ends.at[0]),
        pltpu.make_async_copy(total.at[pl.ds(group, group), :], other, ends.at[1]),
    ]
    for copy in copies:
        copy.start()
    for copy in copies:
        copy.wait()


def run_first(near, bounds, x):
    most, width = x.shape
    units = len(near) * near[0].shape[0] // 2
    smem, hbm, anywhere = (pl.BlockSpec(memory_space=space) for space in (pltpu.SMEM, pltpu.HBM, pl.ANY))
    return pl.pallas_call(
        functools.partial(first_units, len(near)),
        in_specs=[smem, hbm] + [anywhere] * len(near),
        out_specs=hbm,
        out_shape=jax.ShapeDtypeStruct((most, width), jnp.float32),
        scratch_shapes=[
            pltpu.VMEM((2, 2 * TILE, width), jnp.bfloat16),
            pltpu.VMEM((units, width), jnp.bfloat16),
            pltpu.VMEM((units, width), jnp.bfloat16),
            pltpu.VMEM((2 * TILE, units), jnp.bfloat16),
            pltpu.VMEM((2, 2 * TILE, CHUNK), jnp.float32),
            pltpu.VMEM((2, 2 * TILE, width), jnp.float32),
            pltpu.SemaphoreType.DMA((2 * len(near),)),
            pltpu.SemaphoreType.DMA((2,)),
            pltpu.SemaphoreType.DMA((2,)),
        ],
        compiler_params=pltpu.CompilerParams(vmem_limit_bytes=44 << 20),
        cost_estimate=pl.CostEstimate(flops=20 << 30, bytes_accessed=16 << 20, transcendentals=0),
    )(bounds, x, *near)


def run_second(far, bounds, x, docs, normed, sums):
    most, width = x.shape
    group = normed.shape[0]
    units = len(far) * far[0].shape[0] // 2
    smem, hbm, anywhere = (pl.BlockSpec(memory_space=space) for space in (pltpu.SMEM, pltpu.HBM, pl.ANY))
    return pl.pallas_call(
        functools.partial(second_units, len(far)),
        in_specs=[smem, hbm, hbm, anywhere, hbm] + [anywhere] * len(far),
        out_specs=[anywhere, anywhere],
        out_shape=[jax.ShapeDtypeStruct((group, width), jnp.float32)] * 2,
        scratch_shapes=[
            pltpu.VMEM((2 * group + WINDOW, width), jnp.float32),
            pltpu.VMEM((2, 2 * TILE, width), jnp.bfloat16),
            pltpu.VMEM((2, 2 * TILE, LANES), jnp.int32),
            pltpu.VMEM((units, width), jnp.bfloat16),
            pltpu.VMEM((units, width), jnp.bfloat16),
            pltpu.VMEM((2 * TILE, units), jnp.bfloat16),
            pltpu.VMEM((2, 2 * TILE, CHUNK), jnp.float32),
            pltpu.VMEM((2, 2 * TILE, width), jnp.float32),
            pltpu.SemaphoreType.DMA((2 * len(far),)),
            pltpu.SemaphoreType.DMA((2,)),
            pltpu.SemaphoreType.DMA((2,)),
            pltpu.SemaphoreType.DMA((2,)),
            pltpu.SemaphoreType.DMA((2,)),
        ],
        compiler_params=pltpu.CompilerParams(vmem_limit_bytes=36 << 20),
        cost_estimate=pl.CostEstimate(flops=12 << 30, bytes_accessed=24 << 20, transcendentals=0),
    )(bounds, x, docs, normed, sums, *far)


def local(token_ids, doc_lengths, clusters, embed_table, positions, w_in, w_out):
    doc_dev = doc_lengths.shape[0]
    group, seq = token_ids.shape
    vocab_rows, width = embed_table.shape
    n_col = group // doc_dev

    with jax.named_scope("weights"):
        half = w_in.shape[0] // 2
        mixed = jnp.concatenate([w_in[:half], w_out[:half], w_in[half:], w_out[half:]], axis=0)
        mixed, doc_lengths = lax.optimization_barrier((mixed, doc_lengths))
        by_z = ring(mixed, "z")
        lengths = jnp.pad(doc_lengths.reshape(doc_dev // 8, 8), ((0, 16 - doc_dev // 8), (0, LANES - 8))).astype(jnp.bfloat16)
        over = lax.ppermute(lengths, "x_hi", [(0, 1), (1, 0)])
        lower = lax.axis_index("x_hi") == 0
        lengths = jnp.concatenate([jnp.where(lower, lengths, over), jnp.where(lower, over, lengths)], axis=1)
        lengths = jnp.pad(lengths, ((0, 0), (0, width - 2 * LANES)))
        first, second = joined([by_z, by_z], [0, 2 * half], 2 * half, lengths)
        rows = first.shape[0]
        place = jnp.stack([lax.axis_index(COL) * vocab_rows, lax.axis_index("y")]).astype(jnp.int32)
        first, second = ring(first, X), ring(second, "y")
        first, second, token_ids = lax.optimization_barrier((first, second, token_ids))
        ids = token_ids.reshape(n_col, doc_dev * seq // LANES, LANES)
        ids = jnp.pad(ids, ((0, 0), (0, 16 - ids.shape[1]), (0, 0))).reshape(n_col * 16, LANES)
        own_ids = with_lengths(ids, second)
        other_ids = step(own_ids, "core", 1)
        first, second = joined([first, second], [0, 0], rows)
        units = first.shape[0] // 2
        left, right = step(first, "y", 1), step(first, "y", -1)
        down, up = step(second, X, 1), step(second, X, -1)
        near = [first, left, right, second, down, up]

    with jax.named_scope("prepare"):
        most = 2 * n_col * SHARD_CAP
        x, docs, bounds, normed = run_prepare(place, own_ids, other_ids, embed_table, positions, group, most)

    with jax.named_scope("forward"):
        near, x = lax.optimization_barrier((near, x))
        far = [step(near[0], "y", 2), step(near[3], X, 2)]
        sums = run_first(near, bounds, x)
        own, other = run_second(far, bounds, x, docs, normed, sums)

    with jax.named_scope("pooled"):
        sums = own + step(other, "core", 1)
        sums = sums.astype(jnp.bfloat16).reshape(n_col, doc_dev, width)
        sums = lax.all_to_all(sums, COL, 0, 0, tiled=True)
        pooled = jnp.sum(sums.astype(jnp.float32), axis=0) / doc_lengths.astype(jnp.float32)[:, None]
        scale = lax.rsqrt(jnp.sum(pooled * pooled, axis=-1, keepdims=True) + 1e-06)
        embedding = (pooled * scale).astype(jnp.bfloat16)

    with jax.named_scope("match"):
        n_clusters = lax.axis_size(CHIPS)
        labels = clusters[:, 0]
        same = labels[:, None] == labels[None, :]
        order = jnp.arange(doc_dev, dtype=jnp.int32)
        rank = jnp.sum((same & (order[:, None] > order[None, :])).astype(jnp.int32), axis=1)
        slot = labels * 4 + rank
        chosen = slot[None, :] == jnp.arange(n_clusters * 4, dtype=jnp.int32)[:, None]
        sizes = jnp.sum((labels[None, :] == jnp.arange(n_clusters)[:, None]).astype(jnp.int32), axis=1)
        fourth = lax.broadcasted_iota(jnp.int32, (n_clusters, 4, width), 1) == 3
        flags = lax.broadcasted_iota(jnp.int32, (n_clusters, 4, width), 2) < sizes[:, None, None]
        outgoing = jnp.dot(chosen.astype(jnp.bfloat16), embedding, preferred_element_type=jnp.float32)
        outgoing = jnp.where(
            fourth, flags.astype(jnp.float32), outgoing.reshape(n_clusters, 4, width)
        ).astype(jnp.bfloat16)
        members = lax.all_to_all(outgoing, CHIPS, 0, 0, tiled=True)
        others = step(members, "core", 1)
        every = jnp.concatenate([members, others], axis=0)
        filled = jnp.pad(every[:, 3, :3], ((0, 0), (0, 1))).reshape(-1) > 0.5
        count = n_clusters * 4
        scores = jnp.dot(
            members.reshape(count, width), every.reshape(2 * count, width).T, preferred_element_type=jnp.float32
        )
        own = jnp.arange(count)[:, None] == jnp.arange(2 * count)[None, :]
        best = jnp.max(jnp.where(filled[None, :] & jnp.logical_not(own), scores, -1.0), axis=1)
        best = jnp.maximum(best, -1.0)
        returned = lax.all_to_all(best.reshape(n_clusters, 4), CHIPS, 0, 0, tiled=True)
        of_cluster = (labels[:, None] == jnp.arange(n_clusters)[None, :]).astype(jnp.float32)
        rows = jnp.dot(of_cluster, returned, precision=lax.Precision.HIGHEST, preferred_element_type=jnp.float32)
        return jnp.sum(jnp.where(rank[:, None] == jnp.arange(4)[None, :], rows, 0.0), axis=1)


def solution(mesh):
    fine = Mesh(mesh.devices.reshape(2, 4, 2, 2, 4), ("x_lo", "z", "core", "x_hi", "y"))
    everywhere = OWN + COL
    return jax.shard_map(
        local,
        mesh=fine,
        in_specs=(
            P(OWN, None),
            P(everywhere),
            P(everywhere, None),
            P(COL, None),
            P(),
            P(everywhere, None),
            P(everywhere, None),
        ),
        out_specs=P(everywhere),
        check_vma=False,
    )
```
